32 devices in a mesh: dp: 8 (over z, x), tensor: 4 (over y, core).
Axes of the slice: x: 2, y: 2, z: 4, core: 2. Of those that a mesh axis runs over, the one named last changes fastest.
Arguments:
- residual: bfloat16 [8, 1024, 768], P('dp', 'tensor'), may hold values from -64 to 64
- cotangent: bfloat16 [8, 1024, 768], P('dp', 'tensor'), may hold values from -6 to 6
- memory: bfloat16 [8, 2, 2048, 768], P('dp'), may hold values from -6.4 to 6.4
- segment_ids: int32 [8, 1024], P('dp'), may hold values from 0 to 3, as said below
- plot_ids: int32 [8, 4], P('dp'), may hold values from 0 to 1
- attend_weight: float32 [4, 768, 768], P(None, 'dp', 'tensor'), may hold values from -0.2309401 to 0.2309401
- attend_first: float32 [4, 768, 768], P(None, 'dp', 'tensor'), may hold values from -0.00021362305 to 0.00021362305
- attend_second: float32 [4, 768, 768], P(None, 'dp', 'tensor'), may hold values from 1.05937946e-10 to 4.2375178e-10
- recall_weight: float32 [2, 768, 768], P(None, 'dp', 'tensor'), may hold values from -0.2309401 to 0.2309401
- recall_first: float32 [2, 768, 768], P(None, 'dp', 'tensor'), may hold values from -0.00021362305 to 0.00021362305
- recall_second: float32 [2, 768, 768], P(None, 'dp', 'tensor'), may hold values from 1.05937946e-10 to 4.2375178e-10
- outward_weight: float32 [2, 768, 768], P(None, 'tensor', 'dp'), may hold values from -2.6 to 2.6
- outward_first: float32 [2, 768, 768], P(None, 'tensor', 'dp'), may hold values from -0.00021362305 to 0.00021362305
- outward_second: float32 [2, 768, 768], P(None, 'tensor', 'dp'), may hold values from 2.118759e-11 to 8.475036e-11
- expand_weight: float32 [2, 768, 2048], P(None, 'dp', 'tensor'), may hold values from -0.2309401 to 0.2309401
- expand_first: float32 [2, 768, 2048], P(None, 'dp', 'tensor'), may hold values from -0.00021362305 to 0.00021362305
- expand_second: float32 [2, 768, 2048], P(None, 'dp', 'tensor'), may hold values from 2.118759e-11 to 8.475036e-11
- narrow_weight: float32 [2048, 768], P('tensor', 'dp'), may hold values from -0.14142136 to 0.14142136
- narrow_first: float32 [2048, 768], P('tensor', 'dp'), may hold values from -0.00021362305 to 0.00021362305
- narrow_second: float32 [2048, 768], P('tensor', 'dp'), may hold values from 1.05937946e-10 to 4.2375178e-10
- gain_weight: float32 [3, 768], replicated, may hold values from 0.4 to 2.3
- gain_first: float32 [3, 768], replicated, may hold values from -0.00021362305 to 0.00021362305
- gain_second: float32 [3, 768], replicated, may hold values from 1.05937946e-10 to 4.2375178e-10
Outputs:
- block_out: bfloat16 [8, 1024, 768], P('dp', 'tensor')
- residual_grad: bfloat16 [8, 1024, 768], P('dp', 'tensor')
- memory_grad: bfloat16 [8, 2, 2048, 768], P('dp', None, 'tensor')
- grad_norm: float32 [], replicated
- attend_master: float32 [4, 768, 768], P(None, 'dp', 'tensor')
- attend_moment: float32 [4, 768, 768], P(None, 'dp', 'tensor')
- attend_squares: float32 [4, 768, 768], P(None, 'dp', 'tensor')
- attend_copy: bfloat16 [4, 768, 768], P(None, 'dp', 'tensor')
- recall_master: float32 [2, 768, 768], P(None, 'dp', 'tensor')
- recall_moment: float32 [2, 768, 768], P(None, 'dp', 'tensor')
- recall_squares: float32 [2, 768, 768], P(None, 'dp', 'tensor')
- recall_copy: bfloat16 [2, 768, 768], P(None, 'dp', 'tensor')
- outward_master: float32 [2, 768, 768], P(None, 'tensor', 'dp')
- outward_moment: float32 [2, 768, 768], P(None, 'tensor', 'dp')
- outward_squares: float32 [2, 768, 768], P(None, 'tensor', 'dp')
- outward_copy: bfloat16 [2, 768, 768], P(None, 'tensor', 'dp')
- expand_master: float32 [2, 768, 2048], P(None, 'dp', 'tensor')
- expand_moment: float32 [2, 768, 2048], P(None, 'dp', 'tensor')
- expand_squares: float32 [2, 768, 2048], P(None, 'dp', 'tensor')
- expand_copy: bfloat16 [2, 768, 2048], P(None, 'dp', 'tensor')
- narrow_master: float32 [2048, 768], P('tensor', 'dp')
- narrow_moment: float32 [2048, 768], P('tensor', 'dp')
- narrow_squares: float32 [2048, 768], P('tensor', 'dp')
- narrow_copy: bfloat16 [2048, 768], P('tensor', 'dp')
- gain_master: float32 [3, 768], replicated
- gain_moment: float32 [3, 768], replicated
- gain_squares: float32 [3, 768], replicated
The draws below stay inside these ranges and needn't reach their ends.
Inputs may be any that keep to these rules, and one draw needn't show every extreme that they name: `segment_ids`: in every row the ids never fall, and every id holds one token or more.
All inputs are finite; a program needn't handle non-finite values.
Results may differ from the reference program's by a relative error of at most 0.03.
The reference program's roundings to bfloat16 on the way count: a program that leaves them out, or rounds other values in their place, can miss the bound.
Values may be sent and summed in bfloat16 or wider, within the bound.
A program may use at most 320 MiB of HBM per device.

```python
import math
import jax
import jax.numpy as jnp
from jax import lax

D = 768
HEADS = 12
HEAD = 64
FF = 2048
E = 768
LEN = 1024
PATCHES = 2048
PLOTS = 2
SEGS = 4
STEP = 10
ROWS = 8
PARAMS = 9439488


def linear_ramp(array_shape, axis_number, low_end, high_end):
    extent = array_shape[axis_number]
    fraction = jnp.arange(extent, dtype=jnp.float32) / max(extent - 1, 1)
    layout = [1] * len(array_shape)
    layout[axis_number] = extent
    return (low_end + (high_end - low_end) * fraction).reshape(layout)


def bounded_normal(key, array_shape):
    return jnp.clip(jax.random.normal(key, array_shape, jnp.float32), -4.0, 4.0)


def draw_residual(key, part):
    key = jax.random.fold_in(key, 1)
    noise_key, row_key, column_key = jax.random.split(key, 3)
    array_shape = (ROWS, LEN, D)
    row_scale = jnp.exp(jax.random.uniform(row_key, (ROWS, LEN, 1), jnp.float32, -0.6931472, 1.6094379))
    column_scale = jnp.exp(jax.random.uniform(column_key, (1, 1, D), jnp.float32, -1.1512925, 1.1512925))
    values = bounded_normal(noise_key, array_shape)
    return (values * row_scale * column_scale).astype(jnp.bfloat16)


def draw_memory(key, part):
    key = jax.random.fold_in(key, 2)
    array_shape = (ROWS, PLOTS, PATCHES, D)
    values = bounded_normal(key, array_shape) * linear_ramp(array_shape, 3, 0.8, 1.4)
    return values.astype(jnp.bfloat16)


def draw_segment_ids(key, part):
    key = jax.random.fold_in(key, 3)
    short_key, long_key = jax.random.split(key)
    shorts = jax.random.randint(short_key, (ROWS, SEGS), LEN // 32, LEN // 16 + 1)
    longest = jax.random.randint(long_key, (ROWS, 1), 0, SEGS)
    places = jnp.arange(SEGS)[None, :]
    others = jnp.where(places == longest, 0, shorts)
    lengths = jnp.where(places == longest, LEN - jnp.sum(others, axis=1, keepdims=True), others)
    bounds = jnp.cumsum(lengths, axis=1)
    positions = jnp.arange(LEN)
    return jnp.sum((positions[None, :, None] >= bounds[:, None, :]).astype(jnp.int32), axis=-1).astype(jnp.int32)


def draw_attend_weight(key, part):
    key = jax.random.fold_in(key, 4)
    array_shape = (4, D, E)
    values = bounded_normal(key, array_shape) * linear_ramp(array_shape, 2, 0.8, 1.4)
    return values * D ** (-0.5)


def draw_recall_weight(key, part):
    key = jax.random.fold_in(key, 5)
    array_shape = (2, D, E)
    values = bounded_normal(key, array_shape) * linear_ramp(array_shape, 2, 0.8, 1.4)
    return values * D ** (-0.5)


def draw_outward_weight(key, part):
    key = jax.random.fold_in(key, 6)
    array_shape = (2, E, D)
    slice_scale = jnp.array([0.15, 0.4], jnp.float32).reshape(2, 1, 1)
    values = bounded_normal(key, array_shape) * linear_ramp(array_shape, 1, 0.8, 1.4)
    return values * slice_scale


def draw_expand_weight(key, part):
    key = jax.random.fold_in(key, 7)
    array_shape = (2, D, FF)
    values = bounded_normal(key, array_shape) * linear_ramp(array_shape, 2, 0.8, 1.4)
    return values * D ** (-0.5)


def draw_narrow_weight(key, part):
    key = jax.random.fold_in(key, 8)
    array_shape = (FF, D)
    values = bounded_normal(key, array_shape) * linear_ramp(array_shape, 0, 0.8, 1.4)
    return values * FF ** (-0.5)


def draw_gain_weight(key, part):
    key = jax.random.fold_in(key, 9)
    array_shape = (3, D)
    values = bounded_normal(key, array_shape)
    growth = linear_ramp(array_shape, 1, 0.8, 1.4)
    return growth * (1.0 + 0.1 * values)


def with_ends(values, stream_key, smallest, largest):
    spot = [jax.random.randint(jax.random.fold_in(stream_key, axis), (), 0, length) for axis, length in enumerate(values.shape)]
    widest = values.shape.index(max(values.shape))
    next_to = spot[:widest] + [(spot[widest] + 1) % values.shape[widest]] + spot[widest + 1:]
    return values.at[tuple(spot)].set(smallest).at[tuple(next_to)].set(largest)


def steps_of(stream_key, shape, shards, low, top_value):
    level = 1.0
    for dim, parts in shards:
        steps = jax.random.uniform(jax.random.fold_in(jax.random.fold_in(stream_key, 6), dim), (parts,), jnp.float32, low / len(shards), top_value / len(shards))
        level = level * jnp.repeat(jnp.exp(steps), shape[dim] // parts).reshape((-1,) + (1,) * (len(shape) - 1 - dim))
    return level


def gaussian(stream_key, shape, scale, limit, cuts=(), kind=jnp.bfloat16):
    level = steps_of(stream_key, shape, cuts, -0.22, 0.18) if cuts else 1.0
    entries = jax.random.normal(stream_key, shape, jnp.float32) * scale * level
    return jnp.minimum(jnp.maximum(entries, -limit), limit).astype(kind)


def setup_inputs(seed: int = 0) -> dict:
    key_list = jax.random.split(jax.random.key(seed), 24)
    residual = draw_residual(jax.random.fold_in(key_list[23], 71), 0)
    cotangent = gaussian(key_list[1], (ROWS, LEN, D), 1.0, 6.0, ((0, 8), (1, 4)))
    memory = draw_memory(jax.random.fold_in(key_list[23], 71), 0)
    segment_ids = draw_segment_ids(jax.random.fold_in(key_list[23], 71), 0)
    plot_ids = with_ends(jax.random.randint(key_list[4], (ROWS, SEGS), 0, PLOTS), jax.random.fold_in(key_list[4], 1), 0, PLOTS - 1).astype(jnp.int32)
    attend_weight = draw_attend_weight(jax.random.fold_in(key_list[23], 71), 0)
    attend_first = gaussian(key_list[6], (4, D, E), (0.111 * PARAMS ** -0.5), 0.00021362305, ((1, 8), (2, 4)), jnp.float32)
    attend_second = jnp.clip(jnp.exp(math.log(4.23751783662496e-10) - 1.3862944 * jax.random.uniform(key_list[7], (4, D, E), jnp.float32) ** steps_of(key_list[7], (4, D, E), ((1, 8), (2, 4)), -0.2, 0.2)), 1.05937945915624e-10, 4.23751783662496e-10)
    recall_weight = draw_recall_weight(jax.random.fold_in(key_list[23], 71), 0)
    recall_first = gaussian(key_list[9], (2, D, E), (0.111 * PARAMS ** -0.5), 0.00021362305, ((1, 8), (2, 4)), jnp.float32)
    recall_second = jnp.clip(jnp.exp(math.log(4.23751783662496e-10) - 1.3862944 * jax.random.uniform(key_list[10], (2, D, E), jnp.float32) ** steps_of(key_list[10], (2, D, E), ((1, 8), (2, 4)), -0.2, 0.2)), 1.05937945915624e-10, 4.23751783662496e-10)
    outward_weight = draw_outward_weight(jax.random.fold_in(key_list[23], 71), 0)
    outward_first = gaussian(key_list[12], (2, E, D), (0.111 * PARAMS ** -0.5), 0.00021362305, ((1, 4), (2, 8)), jnp.float32)
    outward_second = jnp.clip(jnp.exp(math.log(8.475035950805676e-11) - 1.3862944 * jax.random.uniform(key_list[13], (2, E, D), jnp.float32) ** steps_of(key_list[13], (2, E, D), ((1, 4), (2, 8)), -0.2, 0.2)), 2.118758987701419e-11, 8.475035950805676e-11)
    expand_weight = draw_expand_weight(jax.random.fold_in(key_list[23], 71), 0)
    expand_first = gaussian(key_list[15], (2, D, FF), (0.111 * PARAMS ** -0.5), 0.00021362305, ((1, 8), (2, 4)), jnp.float32)
    expand_second = jnp.clip(jnp.exp(math.log(8.475035950805676e-11) - 1.3862944 * jax.random.uniform(key_list[16], (2, D, FF), jnp.float32) ** steps_of(key_list[16], (2, D, FF), ((1, 8), (2, 4)), -0.2, 0.2)), 2.118758987701419e-11, 8.475035950805676e-11)
    narrow_weight = draw_narrow_weight(jax.random.fold_in(key_list[23], 71), 0)
    narrow_first = gaussian(key_list[18], (FF, D), (0.111 * PARAMS ** -0.5), 0.00021362305, ((0, 4), (1, 8)), jnp.float32)
    narrow_second = jnp.clip(jnp.exp(math.log(4.23751783662496e-10) - 1.3862944 * jax.random.uniform(key_list[19], (FF, D), jnp.float32) ** steps_of(key_list[19], (FF, D), ((0, 4), (1, 8)), -0.2, 0.2)), 1.05937945915624e-10, 4.23751783662496e-10)
    gain_weight = draw_gain_weight(jax.random.fold_in(key_list[23], 71), 0)
    gain_first = gaussian(key_list[21], (3, D), (0.111 * PARAMS ** -0.5), 0.00021362305, (), jnp.float32)
    gain_second = jnp.clip(jnp.exp(jax.random.uniform(key_list[22], (3, D), jnp.float32, math.log(1.05937945915624e-10), math.log(4.23751783662496e-10))), 1.05937945915624e-10, 4.23751783662496e-10)
    return dict(residual=residual, cotangent=cotangent, memory=memory, segment_ids=segment_ids, plot_ids=plot_ids, attend_weight=attend_weight, attend_first=attend_first, attend_second=attend_second, recall_weight=recall_weight, recall_first=recall_first, recall_second=recall_second, outward_weight=outward_weight, outward_first=outward_first, outward_second=outward_second, expand_weight=expand_weight, expand_first=expand_first, expand_second=expand_second, narrow_weight=narrow_weight, narrow_first=narrow_first, narrow_second=narrow_second, gain_weight=gain_weight, gain_first=gain_first, gain_second=gain_second)


@jax.custom_vjp
def low(v):
    return lax.optimization_barrier(v.astype(jnp.bfloat16)).astype(jnp.float32)

@jax.custom_vjp
def low_back(v):
    return v

def low_keep(v):
    return (low(v), None)

def low_pass(kept, grad):
    return (grad,)

def back_keep(v):
    return (v, None)

def back_low(kept, grad):
    return (low(grad),)
low.defvjp(low_keep, low_pass)
low_back.defvjp(back_keep, back_low)
NORM_EPS = 1e-06
ADAM_EPS = 1e-08
BETA_ONE = 0.9
BETA_TWO = 0.999
DECAY = 0.1
RATE_INNER = 0.05
RATE_OUTER = 0.4
RATE_GAIN = 0.5
CLIP = 1.0
MASKED = -1e+30

def matmul(left, right):
    return jnp.dot(left, right, precision=lax.Precision.HIGHEST)

def normalize(stream, gain):
    scale_rows = lax.rsqrt(lax.optimization_barrier(jnp.mean(stream * stream, axis=-1, keepdims=True)) + NORM_EPS)
    return stream * scale_rows * gain

def split_heads(values):
    return values.reshape(values.shape[0], HEADS, HEAD)

def attend(queries, keys_all, values_all, query_tags, key_tags, causal):
    length = queries.shape[0]
    block_rows = min(512, length)
    block_total = length // block_rows
    score_scale = HEAD ** (-0.5)
    key_places = jnp.arange(keys_all.shape[0])

    def one_block(pieces):
        query_block, tag_block, place_block = pieces
        scores = jnp.einsum('qhd,khd->hqk', query_block, keys_all, precision=lax.Precision.HIGHEST) * score_scale
        scores = low_back(scores)
        allowed = tag_block[:, None] == key_tags[None, :]
        if causal:
            allowed = allowed & (key_places[None, :] <= place_block[:, None])
        scores = jnp.where(allowed[None], scores, MASKED)
        weights = low(jax.nn.softmax(scores, axis=-1))
        return jnp.einsum('hqk,khd->qhd', weights, values_all, precision=lax.Precision.HIGHEST)
    places = jnp.arange(length)
    mixture = lax.map(jax.checkpoint(one_block), (queries.reshape(block_total, block_rows, HEADS, HEAD), query_tags.reshape(block_total, block_rows), places.reshape(block_total, block_rows)))
    return mixture.reshape(length, HEADS * HEAD)

def row_forward(stream, memory_rows, gain_rows, attend_low, recall_low, outward_low, expand_low, narrow_low, segments, token_plots, key_plots):
    normed = low(normalize(stream, gain_rows[0]))
    queries = split_heads(low(low_back(matmul(normed, attend_low[0]))))
    keys_self = split_heads(low(low_back(matmul(normed, attend_low[1]))))
    values_self = split_heads(low(low_back(matmul(normed, attend_low[2]))))
    mixture = low(low_back(attend(queries, keys_self, values_self, segments, segments, True)))
    after_self = stream + low_back(matmul(mixture, outward_low[0]))
    normed = low(normalize(after_self, gain_rows[1]))
    queries = split_heads(low(low_back(matmul(normed, attend_low[3]))))
    keys_cross = split_heads(low(low_back(matmul(memory_rows, recall_low[0]))))
    values_cross = split_heads(low(low_back(matmul(memory_rows, recall_low[1]))))
    mixture = low(low_back(attend(queries, keys_cross, values_cross, token_plots, key_plots, False)))
    after_cross = after_self + low_back(matmul(mixture, outward_low[1]))
    normed = low(normalize(after_cross, gain_rows[2]))
    gate_value = low_back(matmul(normed, expand_low[0]))
    lifted = low_back(matmul(normed, expand_low[1]))
    activated = low(jax.nn.gelu(gate_value, approximate=True) * lifted)
    return after_cross + low_back(matmul(activated, narrow_low))

def adam_step(master, moment, second, gradient, step_rate, decay_rate):
    moment_new = BETA_ONE * moment + (1.0 - BETA_ONE) * gradient
    second_new = BETA_TWO * second + (1.0 - BETA_TWO) * gradient * gradient
    moment_hat = moment_new / (1.0 - BETA_ONE ** STEP)
    second_hat = second_new / (1.0 - BETA_TWO ** STEP)
    master_new = master - step_rate * (moment_hat / (jnp.sqrt(second_hat) + ADAM_EPS) + decay_rate * master)
    return (master_new, moment_new, second_new)

def reference(residual, cotangent, memory, segment_ids, plot_ids, attend_weight, attend_first, attend_second, recall_weight, recall_first, recall_second, outward_weight, outward_first, outward_second, expand_weight, expand_first, expand_second, narrow_weight, narrow_first, narrow_second, gain_weight, gain_first, gain_second):
    working = (low(attend_weight), low(recall_weight), low(outward_weight), low(expand_weight), low(narrow_weight))
    key_plots = jnp.arange(PLOTS * PATCHES) // PATCHES

    def one_row(running, pieces):
        row_stream, row_cotangent, row_memory, row_segments, row_plots = pieces
        token_plots = row_plots[row_segments]

        def forward(stream_in, memory_in, gain_rows, attend_low, recall_low, outward_low, expand_low, narrow_low):
            return row_forward(stream_in, memory_in, gain_rows, attend_low, recall_low, outward_low, expand_low, narrow_low, row_segments, token_plots, key_plots)
        row_out, pullback = jax.vjp(forward, row_stream.astype(jnp.float32), row_memory.reshape(PLOTS * PATCHES, D).astype(jnp.float32), gain_weight, *working)
        gradients = pullback(row_cotangent.astype(jnp.float32))
        running_new = tuple((total + gradient for total, gradient in zip(running, gradients[2:])))
        return (running_new, (row_out.astype(jnp.bfloat16), gradients[0].astype(jnp.bfloat16), gradients[1].reshape(PLOTS, PATCHES, D).astype(jnp.bfloat16)))
    initial = tuple((jnp.zeros(element.shape, jnp.float32) for element in (gain_weight,) + working))
    totals, outputs = lax.scan(one_row, initial, (residual, cotangent, memory, segment_ids, plot_ids))
    block_out, residual_grad, memory_grad = outputs
    squares = sum((jnp.sum(element * element) for element in totals))
    grad_norm = jnp.sqrt(squares)
    factor = jnp.minimum(1.0, CLIP / (grad_norm + 1e-06))
    masters = (attend_weight, recall_weight, outward_weight, expand_weight, narrow_weight)
    moments = (attend_first, recall_first, outward_first, expand_first, narrow_first)
    seconds = (attend_second, recall_second, outward_second, expand_second, narrow_second)
    step_rates = (RATE_INNER, RATE_INNER, RATE_OUTER, RATE_INNER, RATE_INNER)
    results = []
    for master, moment, second, gradient, step_rate in zip(masters, moments, seconds, totals[1:], step_rates):
        master_new, moment_new, second_new = adam_step(master, moment, second, gradient * factor, step_rate, DECAY)
        results.extend([master_new, moment_new, second_new, master_new.astype(jnp.bfloat16)])
    gain_new = adam_step(gain_weight, gain_first, gain_second, totals[0] * factor, RATE_GAIN, 0.0)
    return (block_out, residual_grad, memory_grad, grad_norm, results[0], results[1], results[2], results[3], results[4], results[5], results[6], results[7], results[8], results[9], results[10], results[11], results[12], results[13], results[14], results[15], results[16], results[17], results[18], results[19], gain_new[0], gain_new[1], gain_new[2])
```

```python
import functools

import jax
import jax.numpy as jnp
from jax import lax
from jax.experimental import pallas as pl
from jax.experimental.pallas import tpu as pltpu
from jax.sharding import PartitionSpec as P

HEAD = 64
SEGS = 4
STEP = 10
NORM_EPS = 1e-06
ADAM_EPS = 1e-08
BETA_ONE = 0.9
BETA_TWO = 0.999
DECAY = 0.1
RATE_INNER = 0.05
RATE_OUTER = 0.4
RATE_GAIN = 0.5
CLIP = 1.0
MASKED = -1e30
SCALE = HEAD ** (-0.5)

MESH = pl.DeviceIdType.MESH
BF = jnp.bfloat16
F32 = jnp.float32
VLIMIT = 58 * 2**20
VM = pl.BlockSpec(memory_space=pltpu.VMEM)
ANY = pl.BlockSpec(memory_space=pl.ANY)
SM = pl.BlockSpec(memory_space=pltpu.SMEM)
DMA = pltpu.SemaphoreType.DMA


def sds(shape, dtype):
    return jax.ShapeDtypeStruct(shape, dtype)


def nn(a, b):
    return lax.dot_general(a, b, (((1,), (0,)), ((), ())), preferred_element_type=F32)


def nt(a, b):
    return lax.dot_general(a, b, (((1,), (1,)), ((), ())), preferred_element_type=F32)


def rows(i, size):
    return pl.ds(pl.multiple_of(i * size, size), size)


def flat(ref):
    return ref[...].reshape(ref.shape[0] * ref.shape[1], ref.shape[2])


def norm(v, g):
    return v * lax.rsqrt(jnp.mean(v * v, axis=-1, keepdims=True) + NORM_EPS) * g


def norm_back(v, g, dy):
    r = lax.rsqrt(jnp.mean(v * v, axis=-1, keepdims=True) + NORM_EPS)
    n = v * r
    dn = dy * g
    dv = r * (dn - n * jnp.mean(dn * n, axis=-1, keepdims=True))
    return dv, jnp.sum(dy * n, axis=0, keepdims=True)


class Place:
    def __init__(self, n):
        self.n = n
        self.d = lax.axis_index("dp")
        self.t = lax.axis_index("tensor")
        self.tc = self.t + 1 - 2 * lax.rem(self.t, 2)
        self.ty = lax.rem(self.t + 2, 4)
        self.tcy = lax.rem(self.tc + 2, 4)
        self.core = (self.d, self.tc)
        self.y = (self.d, self.ty)
        self.dx = self.d + 1 - 2 * lax.rem(self.d, 2)
        self.x = (self.dx, self.t)

    def z(self, k):
        return (lax.rem(self.d + 2 * k, self.n), self.t)

    def from_z(self, k):
        return lax.rem(self.d - 2 * k + 2 * self.n, self.n)

    def x_from_z(self, k):
        return lax.rem(self.dx - 2 * k + 2 * self.n, self.n)


def greet(devices):
    bar = pltpu.get_barrier_semaphore()
    for dev in devices:
        pl.semaphore_signal(bar, inc=1, device_id=dev, device_id_type=MESH)
    pl.semaphore_wait(bar, len(devices))


def rcopy(src, dst, ss, rs, dev):
    return pltpu.make_async_remote_copy(
        src_ref=src, dst_ref=dst, send_sem=ss, recv_sem=rs, device_id=dev, device_id_type=MESH
    )


class TensorSum:
    def __init__(self, place, refs):
        self.p = place
        self.s0, self.s1, self.r0, self.r1, self.own, self.ys, self.yr, self.ss, self.rs = refs

    @staticmethod
    def scratch(tile, width, hop=F32):
        return [pltpu.VMEM((tile, width), hop)] * 4 + [
            pltpu.VMEM((tile, width), F32),
            pltpu.VMEM((tile, width), BF),
            pltpu.VMEM((tile, width), BF),
            DMA((3,)),
            DMA((3,)),
        ]

    def begin(self, tile_fn):
        p = self.p
        self.c0 = rcopy(self.s0, self.r0, self.ss.at[0], self.rs.at[0], p.core)
        self.c1 = rcopy(self.s1, self.r1, self.ss.at[1], self.rs.at[1], p.core)
        self.cy = rcopy(self.ys, self.yr, self.ss.at[2], self.rs.at[2], p.y)
        self.s0[...] = tile_fn(p.tcy).astype(self.s0.dtype)
        self.c0.start()
        part = tile_fn(p.ty)
        self.c0.wait_recv()
        self.ys[...] = (part + self.r0[...].astype(F32)).astype(BF)
        self.cy.start()
        self.s1[...] = tile_fn(p.tc).astype(self.s1.dtype)
        self.c1.start()
        self.own[...] = tile_fn(p.t)

    def end(self):
        self.c1.wait_recv()
        self.cy.wait_recv()
        total = self.own[...] + self.r1[...].astype(F32) + self.yr[...].astype(F32)
        self.c0.wait_send()
        self.c1.wait_send()
        self.cy.wait_send()
        return total


class TensorGather:
    def __init__(self, place, full, sems, tile):
        self.p = place
        self.full = full
        self.tile = tile
        ss, rs = sems
        p = place
        mine = full.at[rows(p.t, tile)]
        far = full.at[rows(p.ty, tile)]
        self.cc = rcopy(mine, mine, ss.at[0], rs.at[0], p.core)
        self.cy = rcopy(mine, mine, ss.at[1], rs.at[1], p.y)
        self.cf = rcopy(far, far, ss.at[2], rs.at[2], p.core)
        near = full.at[rows(p.tc, tile)]
        cross = full.at[rows(p.tcy, tile)]
        self.wc = rcopy(near, near, ss.at[0], rs.at[0], p.core)
        self.wy = rcopy(far, far, ss.at[1], rs.at[1], p.y)
        self.wf = rcopy(cross, cross, ss.at[2], rs.at[2], p.core)

    @staticmethod
    def scratch():
        return [DMA((3,)), DMA((3,))]

    def begin(self, own):
        self.full[rows(self.p.t, self.tile), :] = own
        self.cy.start()
        self.cc.start()

    def forward(self):
        self.wy.wait_recv()
        self.cf.start()

    def end(self):
        self.wc.wait_recv()
        self.wf.wait_recv()
        self.cy.wait_send()
        self.cc.wait_send()
        self.cf.wait_send()


class RowGather:
    def __init__(self, place, full, sems):
        self.p = place
        self.full = full
        self.zs, self.zr, self.xs, self.xr = sems
        self.steps = place.n // 2

    @staticmethod
    def scratch(n):
        return [DMA((n // 2,))] * 4

    def zcopy(self, k, slot):
        return rcopy(self.full.at[slot], self.full.at[slot], self.zs.at[k], self.zr.at[k], self.p.z(k))

    def xcopy(self, k, slot):
        return rcopy(self.full.at[slot], self.full.at[slot], self.xs.at[k], self.xr.at[k], self.p.x)

    def begin(self):
        for k in range(1, self.steps):
            self.zcopy(k, self.p.d).start()
        self.xcopy(0, self.p.d).start()

    def sent(self):
        for k in range(1, self.steps):
            self.zcopy(k, self.p.d).wait_send()

    def forward(self):
        for k in range(1, self.steps):
            slot = self.p.from_z(k)
            self.zcopy(k, slot).wait_recv()
            self.xcopy(k, slot).start()

    def end(self):
        for k in range(self.steps):
            self.xcopy(k, self.p.x_from_z(k)).wait_recv()
            self.xcopy(k, self.p.from_z(k)).wait_send()


def head_rows(qt, head):
    ids = lax.broadcasted_iota(jnp.int32, qt.shape, 0)
    return jnp.where((ids >= head * HEAD) & (ids < (head + 1) * HEAD), qt, 0.0).astype(BF)


def head_block(x, heads):
    ids = lax.broadcasted_iota(jnp.int32, x.shape, 1)
    return jnp.concatenate(
        [jnp.where((ids >= h * HEAD) & (ids < (h + 1) * HEAD), x, 0.0).astype(BF) for h in range(heads)], axis=0
    )


def segment_starts(seg):
    start = jnp.zeros(seg.shape, jnp.int32)
    for s in range(SEGS - 1):
        count = jnp.sum(jnp.where(seg == s, 1, 0), axis=1, keepdims=True)
        start = start + jnp.where(seg > s, count, 0)
    return start


def causal_mask(keys, tile, tau, start):
    key_place = lax.broadcasted_iota(jnp.int32, (keys, tile), 0)
    query_place = lax.broadcasted_iota(jnp.int32, (keys, tile), 1) + tau * tile
    return (key_place <= query_place) & (key_place >= start)


def first_kernel(n, gather, heads, x0_ref, cot_ref, gain_ref, seg_ref, sa_ref, sb_ref, sc_ref, m_hbm,
                 qkv_ref, qkvt_ref, a_ref, at_ref, lse_ref, x1_ref, qc_ref, qct_ref,
                 ga_out, gb_out, gc_out, h0_out, h1_out, e3_out, kv_out, kvt_out,
                 ga, gb, gc, h0, h1, e3, kv, kvt, m_ref, lsem, osem, *rest):
    rest = list(rest)

    def take(count):
        got = rest[:count]
        del rest[:count]
        return got

    p = Place(n)
    tile = x0_ref.shape[0]
    width = heads * HEAD
    tiles = h0.shape[0] // tile
    load_m = pltpu.make_async_copy(m_hbm, m_ref, lsem.at[0])
    load_m.start()
    sum_refs = take(9)
    gathers = [TensorGather(p, full, take(2), tile) for full in (h0, e3, h1)]
    if gather:
        parts = [RowGather(p, full, take(4)) for full in (ga, gb, gc)]
        for full, shard in ((ga, sa_ref), (gb, sb_ref), (gc, sc_ref)):
            full[p.d] = shard[...]
        greet([p.core, p.y, p.x] + [p.z(k) for k in range(1, n // 2)])
        parts[0].begin()
    else:
        copies = [pltpu.make_async_copy(s, f, lsem.at[1 + i]) for i, (s, f) in
                  enumerate(((sa_ref, ga), (sb_ref, gb), (sc_ref, gc)))]
        for c in copies:
            c.start()
        greet([p.core, p.y])

    x0 = x0_ref[...].astype(F32)
    gathers[0].begin(norm(x0, gain_ref[0:1, :]).astype(BF))
    start = segment_starts(seg_ref[...])
    if gather:
        parts[0].forward()
        parts[1].begin()
    gathers[0].forward()
    gathers[1].begin(cot_ref[...])
    gathers[0].end()
    if gather:
        parts[0].end()
    else:
        for c in copies:
            c.wait()

    wa = flat(ga)
    for i in range(tiles):
        at = slice(i * tile, (i + 1) * tile)
        x = nn(h0[at, :], wa[:, : 3 * width])
        qkv_ref[at, :] = x.astype(BF)
        qkvt_ref[:, at] = x.T.astype(BF)
    outs = []

    def put(src, dst):
        c = pltpu.make_async_copy(src, dst, osem.at[len(outs)])
        c.start()
        outs.append(c)

    put(ga, ga_out)
    put(h0, h0_out)
    if gather:
        parts[1].forward()
        parts[2].begin()
    gathers[1].forward()

    for i in range(tiles):
        at = slice(i * tile, (i + 1) * tile)
        keys = (i + 1) * tile
        kk = qkv_ref[0:keys, width : 2 * width]
        qt = qkvt_ref[0:width, at].astype(F32) * SCALE
        allowed = causal_mask(keys, tile, i, start[:, at])
        for h in range(heads):
            s = jnp.where(allowed, nn(kk, head_rows(qt, h)), MASKED)
            peak = jnp.max(s, axis=0, keepdims=True)
            e = jnp.exp(s - peak)
            total = jnp.sum(e, axis=0, keepdims=True)
            w = (e * (1.0 / total)).astype(BF)
            vt = qkvt_ref[2 * width + h * HEAD : 2 * width + (h + 1) * HEAD, 0:keys]
            at_ref[h * HEAD : (h + 1) * HEAD, at] = nn(vt, w)
            lse_ref[h : h + 1, at] = peak + jnp.log(total)
        a_ref[at, :] = at_ref[:, at].T.astype(BF)

    if gather:
        parts[1].end()
    gathers[1].end()
    put(gb, gb_out)
    put(e3, e3_out)
    wb = flat(gb)
    wo = wb[:, 2 * width : 3 * width]
    total = TensorSum(p, sum_refs)
    total.begin(lambda j: nt(a_ref[rows(j, tile), :], wo))
    load_m.wait()
    mtiles = m_ref.shape[0] // 256

    def project_memory(i, carry):
        x = nn(m_ref[rows(i, 256), :], flat(gb)[:, : 2 * width])
        kv[rows(i, 256), :] = x.astype(BF)
        kvt[:, rows(i, 256)] = x.T.astype(BF)
        return carry

    lax.fori_loop(0, mtiles // 2, project_memory, 0)
    if gather:
        parts[2].forward()
    x1 = x0 + total.end()
    x1_ref[...] = x1
    gathers[2].begin(norm(x1, gain_ref[1:2, :]).astype(BF))
    lax.fori_loop(mtiles // 2, mtiles, project_memory, 0)
    put(kv, kv_out)
    put(kvt, kvt_out)
    gathers[2].forward()
    gathers[2].end()
    put(h1, h1_out)
    wq = flat(ga)[:, 3 * width : 4 * width]
    for i in range(tiles):
        at = slice(i * tile, (i + 1) * tile)
        x = nn(h1[at, :], wq)
        qc_ref[at, :] = x.astype(BF)
        qct_ref[:, at] = x.T.astype(BF)
    if gather:
        for part in parts:
            part.sent()
        parts[2].end()
    put(gc, gc_out)
    for c in outs:
        c.wait()


def call_first(n, gather, x0, cot, gain, seg, sa, sb, sc, mem):
    tile, width_d = x0.shape
    length = seg.shape[1]
    states = mem.shape[0]
    cols = sa.shape[-1]
    width = cols // 4
    heads = width // HEAD
    chunk = (8, width_d // 8)
    shapes = [chunk + (s.shape[-1],) for s in (sa, sb, sc)]
    out_shape = [
        sds((length, 3 * width), BF),
        sds((3 * width, length), BF),
        sds((length, width), BF),
        sds((width, length), F32),
        sds((8, length), F32),
        sds((tile, width_d), F32),
        sds((length, width), BF),
        sds((width, length), BF),
        sds(shapes[0], BF),
        sds(shapes[1], BF),
        sds(shapes[2], BF),
        sds((length, width_d), BF),
        sds((length, width_d), BF),
        sds((length, width_d), BF),
        sds((states, 2 * width), BF),
        sds((2 * width, states), BF),
    ]
    scratch = [pltpu.VMEM(s, BF) for s in shapes]
    scratch += [pltpu.VMEM((length, width_d), BF)] * 3
    scratch += [
        pltpu.VMEM((states, 2 * width), BF),
        pltpu.VMEM((2 * width, states), BF),
        pltpu.VMEM((states, width_d), BF),
        DMA((4,)),
        DMA((8,)),
    ]
    scratch += TensorSum.scratch(tile, width_d)
    scratch += TensorGather.scratch() * 3
    if gather:
        scratch += RowGather.scratch(n) * 3
    shard = VM if gather else ANY
    return pl.pallas_call(
        functools.partial(first_kernel, n, gather, heads),
        out_shape=out_shape,
        in_specs=[VM, VM, VM, VM, shard, shard, shard, ANY],
        out_specs=[VM] * 8 + [ANY] * 8,
        scratch_shapes=scratch,
        compiler_params=pltpu.CompilerParams(collective_id=1, has_side_effects=True, vmem_limit_bytes=VLIMIT),
        name="self_forward",
    )(x0, cot, gain, seg, sa, sb, sc, mem)


def cross_forward_kernel(heads, plots, flags_ref, tp_ref, qct_ref, kv_ref, kvt_ref, ct_ref, c_ref, lse_ref, vte):
    width = heads * HEAD
    states = kv_ref.shape[0]
    patches = states // plots
    length = qct_ref.shape[1]
    tile = 256
    chunk = 512
    ext = HEAD + 16
    for h in range(heads):
        vte[h * ext : h * ext + HEAD, :] = kvt_ref[width + h * HEAD : width + (h + 1) * HEAD, :]
        vte[h * ext + HEAD : (h + 1) * ext, :] = jnp.ones((16, states), BF)
    ct_ref[...] = jnp.zeros(ct_ref.shape, F32)
    lse_ref[...] = jnp.zeros(lse_ref.shape, F32)

    def one_tile(i, carry):
        at = rows(i, tile)
        qt = qct_ref[:, at].astype(F32) * SCALE
        qh = [head_rows(qt, h) for h in range(heads)]
        tags = tp_ref[:, at]
        for plot in range(plots):

            @pl.when(flags_ref[i * plots + plot] != 0)
            def _():
                def one_chunk(j, state):
                    place = rows(plot * (patches // chunk) + j, chunk)
                    kk = kv_ref[place, 0:width]
                    new = []
                    for h in range(heads):
                        peak, acc = state[2 * h], state[2 * h + 1]
                        s = nn(kk, qh[h])
                        peak_new = jnp.maximum(peak, jnp.max(s, axis=0, keepdims=True))
                        e = jnp.exp(s - peak_new).astype(BF)
                        acc = acc * jnp.exp(peak - peak_new) + nn(vte[h * ext : (h + 1) * ext, place], e)
                        new += [peak_new, acc]
                    return tuple(new)

                init = (jnp.full((1, tile), MASKED, F32), jnp.zeros((ext, tile), F32)) * heads
                state = lax.fori_loop(0, patches // chunk, one_chunk, init)
                sel = tags == plot
                for h in range(heads):
                    peak, acc = state[2 * h], state[2 * h + 1]
                    total = acc[HEAD : HEAD + 1, :]
                    hs = slice(h * HEAD, (h + 1) * HEAD)
                    ct_ref[hs, at] = jnp.where(sel, acc[0:HEAD, :] * (1.0 / total), ct_ref[hs, at])
                    lse_ref[h : h + 1, at] = jnp.where(sel, peak + jnp.log(total), lse_ref[h : h + 1, at])

        c_ref[at, :] = ct_ref[:, at].T.astype(BF)
        return carry

    lax.fori_loop(0, length // tile, one_tile, 0)


def call_cross_forward(plots, flags, tp, qct, kv, kvt):
    width, length = qct.shape
    heads = width // HEAD
    return pl.pallas_call(
        functools.partial(cross_forward_kernel, heads, plots),
        out_shape=[sds((width, length), F32), sds((length, width), BF), sds((8, length), F32)],
        in_specs=[SM] + [VM] * 4,
        out_specs=[VM] * 3,
        scratch_shapes=[pltpu.VMEM((heads * (HEAD + 16), kv.shape[0]), BF)],
        compiler_params=pltpu.CompilerParams(vmem_limit_bytes=VLIMIT),
        name="cross_forward",
    )(flags, tp, qct, kv, kvt)


def ffn_kernel(n, heads, c_ref, x1_ref, gain_ref, gb_ref, gc_ref, e3_ref,
               x2_ref, out_ref, g2_ref, e2_ref, dgain_ref, du_ref,
               h2, f, dg, h2t, e3t, *rest):
    rest = list(rest)

    def take(count):
        got = rest[:count]
        del rest[:count]
        return got

    p = Place(n)
    tile, width_d = x1_ref.shape
    width = heads * HEAD
    hidden = f.shape[1]
    sums = [TensorSum(p, take(9)) for _ in range(3)]
    gathers = [TensorGather(p, full, take(2), tile) for full in (h2, e2_ref)]
    greet([p.core, p.y])
    wo = flat(gb_ref)[:, 3 * width : 4 * width]
    sums[0].begin(lambda j: nt(c_ref[rows(j, tile), :], wo))
    e3t[...] = e3_ref[...].T
    x2 = x1_ref[...] + sums[0].end()
    x2_ref[...] = x2
    gathers[0].begin(norm(x2, gain_ref[2:3, :]).astype(BF))

    def hidden_tile(j):
        at = rows(j, tile)
        gate = nn(h2[at, :], flat(gc_ref)[:, 0:hidden])
        up = nn(h2[at, :], flat(gc_ref)[:, hidden : 2 * hidden])
        df = nn(e3_ref[at, :], flat(gc_ref)[:, 2 * hidden : 3 * hidden])
        sq = gate * gate
        th = jnp.tanh(0.7978845608 * gate * (1.0 + 0.044715 * sq))
        half = 0.5 * (1.0 + th)
        act = gate * half
        slope = half + 0.5 * gate * (1.0 - th * th) * (0.7978845608 * (1.0 + 3.0 * 0.044715 * sq))
        f[at, :] = (act * up).astype(BF)
        dg[at, 0:hidden] = (df * up * slope).astype(BF)
        dg[at, hidden : 2 * hidden] = (df * act).astype(BF)

    hidden_tile(p.t)
    gathers[0].wc.wait_recv()
    hidden_tile(p.tc)
    gathers[0].forward()
    hidden_tile(p.ty)
    gathers[0].wf.wait_recv()
    hidden_tile(p.tcy)
    gathers[0].cy.wait_send()
    gathers[0].cc.wait_send()
    gathers[0].cf.wait_send()
    sums[1].begin(lambda j: nt(dg[rows(j, tile), :], flat(gc_ref)[:, 0 : 2 * hidden]))
    h2t[...] = h2[...].T
    for i in range(2 * hidden // 256):
        cs = slice(i * 256, (i + 1) * 256)
        du_ref[:, cs] = nn(h2t[...], dg[:, cs]).astype(BF)
    dh2 = sums[1].end()
    dv, dgain = norm_back(x2, gain_ref[2:3, :], dh2)
    dgain_ref[...] = dgain
    g2 = e3_ref[rows(p.t, tile), :].astype(F32) + dv
    g2_ref[...] = g2
    gathers[1].begin(g2.astype(BF))
    sums[2].begin(lambda j: nt(f[rows(j, tile), :], flat(gc_ref)[:, 2 * hidden : 3 * hidden]))
    gathers[1].forward()
    for i in range(hidden // 256):
        cs = slice(i * 256, (i + 1) * 256)
        du_ref[:, 2 * hidden + i * 256 : 2 * hidden + (i + 1) * 256] = nn(e3t[...], f[:, cs]).astype(BF)
    gathers[1].end()
    out_ref[...] = (x2 + sums[2].end()).astype(BF)


def call_ffn(n, c, x1, gain, gb, gc, e3):
    tile, width_d = x1.shape
    length, width = c.shape
    hidden = gc.shape[2] // 3
    scratch = [
        pltpu.VMEM((length, width_d), BF),
        pltpu.VMEM((length, hidden), BF),
        pltpu.VMEM((length, 2 * hidden), BF),
        pltpu.VMEM((width_d, length), BF),
        pltpu.VMEM((width_d, length), BF),
    ]
    scratch += TensorSum.scratch(tile, width_d) * 3 + TensorGather.scratch() * 2
    return pl.pallas_call(
        functools.partial(ffn_kernel, n, width // HEAD),
        out_shape=[
            sds((tile, width_d), F32),
            sds((tile, width_d), BF),
            sds((tile, width_d), F32),
            sds((length, width_d), BF),
            sds((1, width_d), F32),
            sds((width_d, 3 * hidden), BF),
        ],
        in_specs=[VM] * 6,
        out_specs=[VM] * 6,
        scratch_shapes=scratch,
        compiler_params=pltpu.CompilerParams(collective_id=2, has_side_effects=True, vmem_limit_bytes=VLIMIT),
        name="ffn",
    )(c, x1, gain, gb, gc, e3)


def cross_backward_kernel(heads, plots, flags_ref, tp_ref, e2_ref, gb_ref, qc_ref, qct_ref, kv_ref, kvt_ref,
                          ct_ref, lse_ref, dqc_ref, dk_ref, dv_ref, dka, dva, dqt, vrow):
    width = heads * HEAD
    states = kv_ref.shape[0]
    patches = states // plots
    length = qct_ref.shape[1]
    tile = 256
    chunk = 512
    dka[...] = jnp.zeros(dka.shape, F32)
    dva[...] = jnp.zeros(dva.shape, F32)
    vrow[...] = kv_ref[:, width : 2 * width]

    def one_tile(i, carry):
        at = rows(i, tile)
        dc = nn(e2_ref[at, :], flat(gb_ref)[:, 3 * width : 4 * width])
        dcr = dc.astype(BF)
        dct = dc.T.astype(BF).astype(F32)
        qt = qct_ref[:, at].astype(F32) * SCALE
        qh = [head_rows(qt, h) for h in range(heads)]
        dh = [head_rows(dct, h) for h in range(heads)]
        inner = [
            jnp.sum(dct[h * HEAD : (h + 1) * HEAD, :] * ct_ref[h * HEAD : (h + 1) * HEAD, at], axis=0, keepdims=True)
            for h in range(heads)
        ]
        qb = head_block(qc_ref[at, :].astype(F32) * SCALE, heads)
        db = head_block(dcr.astype(F32), heads)
        tags = tp_ref[:, at]
        dqt[...] = jnp.zeros(dqt.shape, F32)
        for plot in range(plots):

            @pl.when(flags_ref[i * plots + plot] != 0)
            def _():
                lse = [jnp.where(tags == plot, lse_ref[h : h + 1, at], -MASKED) for h in range(heads)]

                def one_chunk(j, carry):
                    place = rows(plot * (patches // chunk) + j, chunk)
                    kk = kv_ref[place, 0:width]
                    vv = vrow[place, :]
                    ps, ds = [], []
                    for h in range(heads):
                        prob = jnp.exp(nn(kk, qh[h]) - lse[h])
                        grad = (prob * (nn(vv, dh[h]) - inner[h])).astype(BF)
                        ps.append(prob.astype(BF))
                        ds.append(grad)
                        hs = slice(h * HEAD, (h + 1) * HEAD)
                        dqt[hs, :] += nn(kvt_ref[hs, place], grad)
                    dva[place, :] += nn(jnp.concatenate(ps, axis=1), db)
                    dka[place, :] += nn(jnp.concatenate(ds, axis=1), qb)
                    return carry

                lax.fori_loop(0, patches // chunk, one_chunk, 0)

        dqc_ref[at, :] = (dqt[...] * SCALE).T.astype(BF)
        return carry

    lax.fori_loop(0, length // tile, one_tile, 0)
    dk_ref[...] = dka[...].astype(BF)
    dv_ref[...] = dva[...].astype(BF)


def call_cross_backward(plots, flags, tp, e2, gb, qc, qct, kv, kvt, ct, lse):
    width, length = qct.shape
    states = kv.shape[0]
    return pl.pallas_call(
        functools.partial(cross_backward_kernel, width // HEAD, plots),
        out_shape=[sds((length, width), BF), sds((states, width), BF), sds((states, width), BF)],
        in_specs=[SM] + [VM] * 9,
        out_specs=[VM] * 3,
        scratch_shapes=[
            pltpu.VMEM((states, width), F32),
            pltpu.VMEM((states, width), F32),
            pltpu.VMEM((width, 256), F32),
            pltpu.VMEM((states, width), BF),
        ],
        compiler_params=pltpu.CompilerParams(vmem_limit_bytes=VLIMIT),
        name="cross_backward",
    )(flags, tp, e2, gb, qc, qct, kv, kvt, ct, lse)


def self_backward_kernel(n, heads, plots, x0_ref, x1_ref, g2_ref, gain_ref, seg_ref, dqc_ref, dk_ref, dv_ref,
                         e2_hbm, h1_hbm, h0_hbm, ga_hbm, gb_hbm, m_hbm, c_hbm, a_hbm, qkv_hbm, qkvt_hbm, at_hbm, lse_hbm,
                         res_ref, mem_ref, dgain_ref, ga_grad_ref, gb_grad_ref,
                         e2, h1, h0, ga, gb, mem, c, a, qkv, qkvt, att, lse, e1, dqkv, dka, dva, tr, lsem, *rest):
    rest = list(rest)

    def take(count):
        got = rest[:count]
        del rest[:count]
        return got

    p = Place(n)
    tile, width_d = x1_ref.shape
    width = heads * HEAD
    length = e1.shape[0]
    tiles = length // tile
    loads = [
        pltpu.make_async_copy(s, d, lsem.at[i])
        for i, (s, d) in enumerate(
            ((ga_hbm, ga), (gb_hbm, gb), (m_hbm, mem), (h1_hbm, h1), (e2_hbm, e2), (c_hbm, c), (a_hbm, a),
             (qkv_hbm, qkv), (qkvt_hbm, qkvt), (at_hbm, att), (lse_hbm, lse), (h0_hbm, h0))
        )
    ]
    for load in loads:
        load.start()
    sums = [TensorSum(p, take(9)) for _ in range(2)]
    gather = TensorGather(p, e1, take(2), tile)
    ms0, ms1, mr0, mr1, mys, myr, mss, mrs = take(8)
    greet([p.core, p.y])
    loads[0].wait()
    wq = flat(ga)[:, 3 * width : 4 * width]
    sums[0].begin(lambda j: nt(dqc_ref[rows(j, tile), :], wq))
    loads[1].wait()

    patches = dk_ref.shape[0] // plots
    blocks = patches // 4 // 256

    def mem_rows(owner, b):
        plot, part = b // blocks, b % blocks
        return pl.ds(pl.multiple_of(plot * patches + owner * (patches // 4) + part * 256, 256), 256)

    def mem_part(owner, b):
        at = mem_rows(owner, b)
        return nt(dk_ref[at, :], flat(gb)[:, 0:width]) + nt(dv_ref[at, :], flat(gb)[:, width : 2 * width])

    total_blocks = plots * blocks
    mc0 = [rcopy(ms0.at[b], mr0.at[b], mss.at[0, b], mrs.at[0, b], p.core) for b in range(total_blocks)]
    mc1 = [rcopy(ms1.at[b], mr1.at[b], mss.at[1, b], mrs.at[1, b], p.core) for b in range(total_blocks)]
    mcy = [rcopy(mys.at[b], myr.at[b], mss.at[2, b], mrs.at[2, b], p.y) for b in range(total_blocks)]
    for b in range(total_blocks):
        ms0[b] = mem_part(p.tcy, b).astype(BF)
        mc0[b].start()
    for b in range(total_blocks):
        ms1[b] = mem_part(p.tc, b).astype(BF)
        mc1[b].start()

    dh1 = sums[0].end()
    x1 = x1_ref[...]
    dv1, dgain1 = norm_back(x1, gain_ref[1:2, :], dh1)
    dgain_ref[1:2, :] = dgain1
    g1 = g2_ref[...] + dv1
    gather.begin(g1.astype(BF))
    for b in range(total_blocks):
        mc0[b].wait_recv()
        mys[b] = (mem_part(p.ty, b) + mr0[b].astype(F32)).astype(BF)
        mcy[b].start()

    loads[2].wait()
    states = dk_ref.shape[0]
    for i in range(states // length):
        part = slice(i * length, (i + 1) * length)
        tr[...] = mem[part, :].T
        if i == 0:
            dka[...] = nn(tr[...], dk_ref[part, :])
            dva[...] = nn(tr[...], dv_ref[part, :])
        else:
            dka[...] += nn(tr[...], dk_ref[part, :])
            dva[...] += nn(tr[...], dv_ref[part, :])
    gb_grad_ref[:, 0:width] = dka[...].astype(BF)
    gb_grad_ref[:, width : 2 * width] = dva[...].astype(BF)
    loads[3].wait()
    tr[...] = h1[...].T
    ga_grad_ref[:, 3 * width : 4 * width] = nn(tr[...], dqc_ref[...]).astype(BF)
    loads[4].wait()
    loads[5].wait()
    tr[...] = e2[...].T
    gb_grad_ref[:, 3 * width : 4 * width] = nn(tr[...], c[...]).astype(BF)
    gather.forward()
    gather.end()

    for load in loads[6:]:
        load.wait()
    start = segment_starts(seg_ref[...])
    tr[...] = e1[...].T
    gb_grad_ref[:, 2 * width : 3 * width] = nn(tr[...], a[...]).astype(BF)
    wo = flat(gb)[:, 2 * width : 3 * width]
    for i in range(tiles):
        at = slice(i * tile, (i + 1) * tile)
        keys = (i + 1) * tile
        da = nn(e1[at, :], wo)
        dar = da.astype(BF)
        dat = da.T.astype(BF).astype(F32)
        qt = qkvt[0:width, at].astype(F32) * SCALE
        allowed = causal_mask(keys, tile, i, start[:, at])
        kk = qkv[0:keys, width : 2 * width]
        vv = qkv[0:keys, 2 * width : 3 * width]
        ps, ds, dq = [], [], []
        for h in range(heads):
            hs = slice(h * HEAD, (h + 1) * HEAD)
            inner = jnp.sum(dat[hs, :] * att[hs, at], axis=0, keepdims=True)
            prob = jnp.where(allowed, jnp.exp(nn(kk, head_rows(qt, h)) - lse[h : h + 1, at]), 0.0)
            grad = (prob * (nn(vv, head_rows(dat, h)) - inner)).astype(BF)
            ps.append(prob.astype(BF))
            ds.append(grad)
            dq.append(nn(qkvt[width + h * HEAD : width + (h + 1) * HEAD, 0:keys], grad))
        dqkv[at, 0:width] = (jnp.concatenate(dq, axis=0) * SCALE).T
        dk = nn(jnp.concatenate(ds, axis=1), head_block(qkv[at, 0:width].astype(F32) * SCALE, heads))
        dv = nn(jnp.concatenate(ps, axis=1), head_block(dar.astype(F32), heads))
        if i:
            dqkv[0 : keys - tile, width : 2 * width] += dk[0 : keys - tile]
            dqkv[0 : keys - tile, 2 * width : 3 * width] += dv[0 : keys - tile]
        dqkv[at, width : 2 * width] = dk[keys - tile :]
        dqkv[at, 2 * width : 3 * width] = dv[keys - tile :]
    sums[1].begin(lambda j: nt(dqkv[rows(j, tile), :].astype(BF), flat(ga)[:, 0 : 3 * width]))
    tr[...] = h0[...].T
    ga_grad_ref[:, 0 : 3 * width] = nn(tr[...], dqkv[...].astype(BF)).astype(BF)
    for b in range(total_blocks):
        mc1[b].wait_recv()
        mcy[b].wait_recv()
        own = mem_part(p.t, b) + mr1[b].astype(F32) + myr[b].astype(F32)
        mem_ref[b // blocks, (b % blocks) * 256 : (b % blocks + 1) * 256, :] = own.astype(BF)
    dh0 = sums[1].end()
    dv0, dgain0 = norm_back(x0_ref[...].astype(F32), gain_ref[0:1, :], dh0)
    dgain_ref[0:1, :] = dgain0
    res_ref[...] = (g1 + dv0).astype(BF)
    for group in (mc0, mc1, mcy):
        for cpy in group:
            cpy.wait_send()


def call_self_backward(n, plots, x0, x1, g2, gain, seg, dqc, dk, dv, e2, h1, h0, ga, gb, mem, c, a, qkv, qkvt, att, lse):
    tile, width_d = x1.shape
    length, width = dqc.shape
    states = mem.shape[0]
    patches = states // plots
    total_blocks = plots * (patches // 4 // 256)
    hbm = (e2, h1, h0, ga, gb, mem, c, a, qkv, qkvt, att, lse)
    scratch = [pltpu.VMEM(v.shape, v.dtype) for v in hbm]
    scratch += [
        pltpu.VMEM((length, width_d), BF),
        pltpu.VMEM((length, 3 * width), F32),
        pltpu.VMEM((width_d, width), F32),
        pltpu.VMEM((width_d, width), F32),
        pltpu.VMEM((width_d, length), BF),
        DMA((12,)),
    ]
    scratch += TensorSum.scratch(tile, width_d) * 2 + TensorGather.scratch()
    scratch += [pltpu.VMEM((total_blocks, 256, width_d), BF)] * 6 + [DMA((3, total_blocks))] * 2
    return pl.pallas_call(
        functools.partial(self_backward_kernel, n, width // HEAD, plots),
        out_shape=[
            sds((tile, width_d), BF),
            sds((plots, patches // 4, width_d), BF),
            sds((8, width_d), F32),
            sds((width_d, 4 * width), BF),
            sds((width_d, 4 * width), BF),
        ],
        in_specs=[VM] * 8 + [ANY] * 12,
        out_specs=[VM] * 5,
        scratch_shapes=scratch,
        compiler_params=pltpu.CompilerParams(collective_id=3, has_side_effects=True, vmem_limit_bytes=VLIMIT),
        name="self_backward",
    )(x0, x1, g2, gain, seg, dqc, dk, dv, *hbm)


class RowSum:
    def __init__(self, place, mine, near, mid, far, sems):
        self.p = place
        self.mine, self.near, self.mid, self.far = mine, near, mid, far
        self.xs, self.xr, self.zs, self.zr = sems
        self.steps = place.n // 2

    @staticmethod
    def scratch(n, shard, width):
        half = (n // 2, shard, width)
        return [pltpu.VMEM(half, BF)] * 3 + [DMA((n // 2,))] * 4

    def slot(self, k):
        return lax.rem(self.p.d + 2 * k, self.p.n)

    def xcopy(self, k):
        return rcopy(self.mine.at[lax.rem(self.p.dx + 2 * k, self.p.n)], self.near.at[k], self.xs.at[k], self.xr.at[k], self.p.x)

    def zcopy(self, k):
        return rcopy(self.mid.at[k], self.far.at[k], self.zs.at[k], self.zr.at[k], self.p.z(k))

    def begin(self):
        for k in list(range(1, self.steps)) + [0]:
            self.xcopy(k).start()

    def middle(self):
        for k in range(1, self.steps):
            self.xcopy(k).wait_recv()
            self.mid[k] = (self.mine[self.slot(k)].astype(F32) + self.near[k].astype(F32)).astype(BF)
            self.zcopy(k).start()

    def end(self):
        self.xcopy(0).wait_recv()
        total = self.mine[self.p.d].astype(F32) + self.near[0].astype(F32)
        for k in range(1, self.steps):
            self.zcopy(k).wait_recv()
            total = total + self.far[k].astype(F32)
        return total

    def sent(self):
        for k in range(1, self.steps):
            self.zcopy(k).wait_send()
        for k in range(self.steps):
            self.xcopy(k).wait_send()


def grads_kernel(n, du_ref, gb_ref, ga_ref, dgain_ref, du_out, gb_out, ga_out, stat_ref,
                 stat_t, stat_d, tsem_s, tsem_r, dsem_s, dsem_r, *rest):
    rest = list(rest)

    def take(count):
        got = rest[:count]
        del rest[:count]
        return got

    p = Place(n)
    grads = (du_ref, gb_ref, ga_ref)
    outs = (du_out, gb_out, ga_out)
    sums = []
    for g in grads:
        near, mid, far, xs, xr, zs, zr = take(7)
        sums.append(RowSum(p, g, near, mid, far, (xs, xr, zs, zr)))
    tensor_peers = [(p.d, lax.rem(p.t + k, 4)) for k in range(1, 4)]
    dp_peers = [(lax.rem(p.d + k, n), p.t) for k in range(1, n)]
    greet(tensor_peers + dp_peers)
    for s in sums:
        s.begin()
    for s in sums:
        s.middle()
    squares = jnp.zeros((1, 1), F32)
    for s, o in zip(sums, outs):
        total = s.end()
        o[...] = total
        squares = squares + jnp.sum(jnp.sum(total * total, axis=1, keepdims=True), axis=0, keepdims=True)
    row = lax.broadcasted_iota(jnp.int32, dgain_ref.shape, 0)
    stat_t[0] = jnp.where(row < 3, dgain_ref[...], jnp.where(row == 3, squares, 0.0))
    copies = [rcopy(stat_t.at[0], stat_t.at[k], tsem_s.at[k], tsem_r.at[k], tensor_peers[k - 1]) for k in range(1, 4)]
    for c in copies:
        c.start()
    for c in copies:
        c.wait_recv()
    total = jnp.zeros(dgain_ref.shape, F32)
    for j in range(4):
        total = total + stat_t[lax.rem(p.t - j + 4, 4)]
    stat_d[0] = total
    copies2 = [rcopy(stat_d.at[0], stat_d.at[k], dsem_s.at[k], dsem_r.at[k], dp_peers[k - 1]) for k in range(1, n)]
    for c in copies2:
        c.start()
    for c in copies2:
        c.wait_recv()
    total = jnp.zeros(dgain_ref.shape, F32)
    for j in range(n):
        total = total + stat_d[lax.rem(p.d - j + n, n)]
    stat_ref[...] = total
    for c in copies + copies2:
        c.wait_send()
    for s in sums:
        s.sent()


def call_grads(n, du, gb, ga, dgain):
    width_d = dgain.shape[1]
    shard = width_d // n
    grads = [g.reshape(n, shard, g.shape[1]) for g in (du, gb, ga)]
    scratch = [
        pltpu.VMEM((4, 8, width_d), F32),
        pltpu.VMEM((n, 8, width_d), F32),
        DMA((4,)),
        DMA((4,)),
        DMA((n,)),
        DMA((n,)),
    ]
    for g in grads:
        scratch += RowSum.scratch(n, shard, g.shape[2])
    return pl.pallas_call(
        functools.partial(grads_kernel, n),
        out_shape=[sds((shard, g.shape[2]), F32) for g in grads] + [sds((8, width_d), F32)],
        in_specs=[VM] * 4,
        out_specs=[VM] * 4,
        scratch_shapes=scratch,
        compiler_params=pltpu.CompilerParams(collective_id=4, has_side_effects=True, vmem_limit_bytes=VLIMIT),
        name="grads",
    )(*grads, dgain)


def adam_step(master, moment, second, gradient, step_rate, decay_rate):
    moment_new = BETA_ONE * moment + (1.0 - BETA_ONE) * gradient
    second_new = BETA_TWO * second + (1.0 - BETA_TWO) * gradient * gradient
    moment_hat = moment_new / (1.0 - BETA_ONE**STEP)
    second_hat = second_new / (1.0 - BETA_TWO**STEP)
    master_new = master - step_rate * (
        moment_hat / (jnp.sqrt(second_hat) + ADAM_EPS) + decay_rate * master
    )
    return (master_new, moment_new, second_new)


def local(
    n,
    residual,
    cotangent,
    memory,
    segment_ids,
    plot_ids,
    attend_weight,
    attend_first,
    attend_second,
    recall_weight,
    recall_first,
    recall_second,
    outward_weight,
    outward_first,
    outward_second,
    expand_weight,
    expand_first,
    expand_second,
    narrow_weight,
    narrow_first,
    narrow_second,
    gain_weight,
    gain_first,
    gain_second,
):
    _, plots, patches, width_d = memory.shape
    shard = attend_weight.shape[1]
    aligned = shard % 16 == 0
    length = segment_ids.shape[1]

    def by_rows(w):
        return jnp.transpose(w, (1, 0, 2)).reshape(w.shape[1], -1)

    sa = by_rows(attend_weight).astype(BF)
    sb = jnp.concatenate(
        [by_rows(recall_weight), by_rows(jnp.transpose(outward_weight, (0, 2, 1)))], axis=1
    ).astype(BF)
    sc = jnp.concatenate([by_rows(expand_weight), narrow_weight.T], axis=1).astype(BF)
    if not aligned:
        sa, sb, sc = (
            lax.all_gather(s, "dp", axis=0, tiled=True).reshape(8, width_d // 8, s.shape[1]) for s in (sa, sb, sc)
        )
    mem = memory.reshape(plots * patches, width_d)
    token_plots = jnp.sum(
        jnp.where(segment_ids[:, :, None] == jnp.arange(SEGS)[None, None, :], plot_ids[:, None, :], 0), axis=-1
    )
    flags = (
        jnp.any(token_plots.reshape(length // 256, 1, 256) == jnp.arange(plots)[None, :, None], axis=-1)
        .astype(jnp.int32)
        .reshape(-1)
    )
    x0 = residual[0]
    qkv, qkvt, a, att, lse, x1, qc, qct, ga, gb, gc, h0, h1, e3, kv, kvt = call_first(
        n, aligned, x0, cotangent[0], gain_weight, segment_ids, sa, sb, sc, mem
    )
    ct, c, lse_c = call_cross_forward(plots, flags, token_plots, qct, kv, kvt)
    x2, block_out, g2, e2, dgain2, du = call_ffn(n, c, x1, gain_weight, gb, gc, e3)
    dqc, dk, dv = call_cross_backward(plots, flags, token_plots, e2, gb, qc, qct, kv, kvt, ct, lse_c)
    residual_grad, memory_grad, dgain, dga, dgb = call_self_backward(
        n, plots, x0, x1, g2, gain_weight, segment_ids, dqc, dk, dv, e2, h1, h0, ga, gb, mem, c, a, qkv, qkvt, att, lse
    )
    dgain = jnp.concatenate([dgain[0:2], dgain2, jnp.zeros((5, width_d), F32)], axis=0)
    if aligned:
        own_u, own_b, own_a, stat = call_grads(n, du, dgb, dga, dgain)
        square_total = stat[3, 0]
        gain_total = stat[0:3]
    else:
        own_u, own_b, own_a = (
            lax.psum_scatter(g.astype(F32), "dp", scatter_dimension=0, tiled=True) for g in (du, dgb, dga)
        )
        squares = sum(jnp.sum(g * g) for g in (own_u, own_b, own_a))
        gain_total, square_total = lax.psum((dgain[0:3], squares), ("dp", "tensor"))
    grad_norm = jnp.sqrt(square_total + jnp.sum(gain_total * gain_total))
    factor = jnp.minimum(1.0, CLIP / (grad_norm + 1e-06))

    width = attend_weight.shape[2]
    hidden = expand_weight.shape[2]
    grads = (
        jnp.stack([own_a[:, i * width : (i + 1) * width] for i in range(4)]),
        jnp.stack([own_b[:, i * width : (i + 1) * width] for i in range(2)]),
        jnp.stack([own_b[:, i * width : (i + 1) * width].T for i in (2, 3)]),
        jnp.stack([own_u[:, i * hidden : (i + 1) * hidden] for i in range(2)]),
        own_u[:, 2 * hidden :].T,
    )
    masters = (attend_weight, recall_weight, outward_weight, expand_weight, narrow_weight)
    moments = (attend_first, recall_first, outward_first, expand_first, narrow_first)
    seconds = (attend_second, recall_second, outward_second, expand_second, narrow_second)
    step_rates = (RATE_INNER, RATE_INNER, RATE_OUTER, RATE_INNER, RATE_INNER)
    results = []
    for master, moment, second, gradient, step_rate in zip(masters, moments, seconds, grads, step_rates):
        master_new, moment_new, second_new = adam_step(
            master, moment, second, gradient * factor, step_rate, DECAY
        )
        results.extend([master_new, moment_new, second_new, master_new.astype(BF)])
    gain_new = adam_step(gain_weight, gain_first, gain_second, gain_total * factor, RATE_GAIN, 0.0)
    return (
        (block_out[None], residual_grad[None], memory_grad[None], grad_norm) + tuple(results) + tuple(gain_new)
    )


def solution(mesh):
    rows_in = P("dp", "tensor", None)
    inner = P(None, "dp", "tensor")
    outer = P(None, "tensor", "dp")
    narrow = P("tensor", "dp")
    in_specs = (
        (rows_in, rows_in, P("dp", None, None, None), P("dp", None), P("dp", None))
        + (inner,) * 3
        + (inner,) * 3
        + (outer,) * 3
        + (inner,) * 3
        + (narrow,) * 3
        + (P(),) * 3
    )
    out_specs = (
        (rows_in, rows_in, P("dp", None, "tensor", None), P())
        + (inner,) * 4
        + (inner,) * 4
        + (outer,) * 4
        + (inner,) * 4
        + (narrow,) * 4
        + (P(),) * 3
    )
    return jax.shard_map(
        functools.partial(local, mesh.shape["dp"]),
        mesh=mesh,
        in_specs=in_specs,
        out_specs=out_specs,
        check_vma=False,
    )
```

```python
import functools

import jax
import jax.numpy as jnp
from jax import lax
from jax.experimental import pallas as pl
from jax.experimental.pallas import tpu as pltpu
from jax.sharding import PartitionSpec as P

HEAD = 64
SEGS = 4
STEP = 10
NORM_EPS = 1e-06
ADAM_EPS = 1e-08
BETA_ONE = 0.9
BETA_TWO = 0.999
DECAY = 0.1
RATE_INNER = 0.05
RATE_OUTER = 0.4
RATE_GAIN = 0.5
CLIP = 1.0
MASKED = -1e30
SCALE = HEAD ** (-0.5)

MESH = pl.DeviceIdType.MESH
BF = jnp.bfloat16
F32 = jnp.float32
VLIMIT = 62 * 2**20
VM = pl.BlockSpec(memory_space=pltpu.VMEM)
ANY = pl.BlockSpec(memory_space=pl.ANY)
SM = pl.BlockSpec(memory_space=pltpu.SMEM)
DMA = pltpu.SemaphoreType.DMA


def sds(shape, dtype):
    return jax.ShapeDtypeStruct(shape, dtype)


def nn(a, b):
    return lax.dot_general(a, b, (((1,), (0,)), ((), ())), preferred_element_type=F32)


def nt(a, b):
    return lax.dot_general(a, b, (((1,), (1,)), ((), ())), preferred_element_type=F32)


def rows(i, size):
    return pl.ds(pl.multiple_of(i * size, size), size)


def flat(ref):
    return ref[...].reshape(ref.shape[0] * ref.shape[1], ref.shape[2])


def norm(v, g):
    return v * lax.rsqrt(jnp.mean(v * v, axis=-1, keepdims=True) + NORM_EPS) * g


def norm_back(v, g, dy):
    r = lax.rsqrt(jnp.mean(v * v, axis=-1, keepdims=True) + NORM_EPS)
    n = v * r
    dn = dy * g
    dv = r * (dn - n * jnp.mean(dn * n, axis=-1, keepdims=True))
    return dv, jnp.sum(dy * n, axis=0, keepdims=True)


class Place:
    def __init__(self, n):
        self.n = n
        self.d = lax.axis_index("dp")
        self.t = lax.axis_index("tensor")
        self.tc = self.t + 1 - 2 * lax.rem(self.t, 2)
        self.ty = lax.rem(self.t + 2, 4)
        self.tcy = lax.rem(self.tc + 2, 4)
        self.core = (self.d, self.tc)
        self.y = (self.d, self.ty)
        self.dx = self.d + 1 - 2 * lax.rem(self.d, 2)
        self.x = (self.dx, self.t)

    def z(self, k):
        return (lax.rem(self.d + 2 * k, self.n), self.t)

    def from_z(self, k):
        return lax.rem(self.d - 2 * k + 2 * self.n, self.n)

    def x_from_z(self, k):
        return lax.rem(self.dx - 2 * k + 2 * self.n, self.n)


def greet(devices):
    bar = pltpu.get_barrier_semaphore()
    for dev in devices:
        pl.semaphore_signal(bar, inc=1, device_id=dev, device_id_type=MESH)
    pl.semaphore_wait(bar, len(devices))


class Puts:
    def __init__(self, sems):
        self.sems = sems
        self.all = []

    def __call__(self, src, dst):
        c = pltpu.make_async_copy(src, dst, self.sems.at[len(self.all)])
        c.start()
        self.all.append(c)

    def end(self):
        for c in self.all:
            c.wait()


def rcopy(src, dst, ss, rs, dev):
    return pltpu.make_async_remote_copy(
        src_ref=src, dst_ref=dst, send_sem=ss, recv_sem=rs, device_id=dev, device_id_type=MESH
    )


class TensorSum:
    def __init__(self, place, refs):
        self.p = place
        self.s0, self.s1, self.r0, self.r1, self.own, self.ys, self.yr, self.ss, self.rs = refs

    @staticmethod
    def scratch(tile, width, hop=F32):
        return [pltpu.VMEM((tile, width), hop)] * 4 + [
            pltpu.VMEM((tile, width), F32),
            pltpu.VMEM((tile, width), BF),
            pltpu.VMEM((tile, width), BF),
            DMA((3,)),
            DMA((3,)),
        ]

    def begin(self, tile_fn):
        self.send(tile_fn)
        self.pass_on(tile_fn)

    def send(self, tile_fn):
        p = self.p
        self.c0 = rcopy(self.s0, self.r0, self.ss.at[0], self.rs.at[0], p.core)
        self.c1 = rcopy(self.s1, self.r1, self.ss.at[1], self.rs.at[1], p.core)
        self.cy = rcopy(self.ys, self.yr, self.ss.at[2], self.rs.at[2], p.y)
        self.s0[...] = tile_fn(p.tcy).astype(self.s0.dtype)
        self.c0.start()
        self.s1[...] = tile_fn(p.tc).astype(self.s1.dtype)
        self.c1.start()

    def pass_on(self, tile_fn):
        p = self.p
        part = tile_fn(p.ty)
        self.c0.wait_recv()
        self.ys[...] = (part + self.r0[...].astype(F32)).astype(BF)
        self.cy.start()
        self.own[...] = tile_fn(p.t)

    def end(self):
        self.c1.wait_recv()
        self.cy.wait_recv()
        total = self.own[...] + self.r1[...].astype(F32) + self.yr[...].astype(F32)
        self.c0.wait_send()
        self.c1.wait_send()
        self.cy.wait_send()
        return total


class TensorGather:
    def __init__(self, place, full, sems):
        self.p = p = place
        self.full = full
        ss, rs = sems
        mine, far, near, cross = (full.at[i] for i in (p.t, p.ty, p.tc, p.tcy))
        self.cc = rcopy(mine, mine, ss.at[0], rs.at[0], p.core)
        self.cy = rcopy(mine, mine, ss.at[1], rs.at[1], p.y)
        self.cf = rcopy(far, far, ss.at[2], rs.at[2], p.core)
        self.wc = rcopy(near, near, ss.at[0], rs.at[0], p.core)
        self.wy = rcopy(far, far, ss.at[1], rs.at[1], p.y)
        self.wf = rcopy(cross, cross, ss.at[2], rs.at[2], p.core)

    @staticmethod
    def scratch():
        return [DMA((3,)), DMA((3,))]

    def begin(self, own):
        self.full[self.p.t] = own
        self.cy.start()
        self.cc.start()

    def forward(self):
        self.wy.wait_recv()
        self.cf.start()

    def end(self):
        self.wc.wait_recv()
        self.wf.wait_recv()
        self.cy.wait_send()
        self.cc.wait_send()
        self.cf.wait_send()


class TileSwap:
    def __init__(self, place, full, sems, tile):
        self.p = p = place
        ss, rs = sems
        mine = full.at[rows(p.t, tile)]
        far = full.at[rows(p.ty, tile)]
        self.out = rcopy(mine, mine, ss.at[0], rs.at[0], p.y)
        self.back = rcopy(far, far, ss.at[0], rs.at[0], p.y)

    @staticmethod
    def scratch():
        return [DMA((1,)), DMA((1,))]

    def begin(self):
        self.out.start()

    def end(self):
        self.back.wait_recv()
        self.out.wait_send()


class CoreShare:
    def __init__(self, place, full, sems, tile):
        self.p = p = place
        ss, rs = sems
        self.out = [rcopy(full.at[rows(i, tile)], full.at[rows(i, tile)], ss.at[k], rs.at[k], p.core)
                    for k, i in enumerate((p.t, p.ty))]
        self.back = [rcopy(full.at[rows(i, tile)], full.at[rows(i, tile)], ss.at[k], rs.at[k], p.core)
                     for k, i in enumerate((p.tc, p.tcy))]

    @staticmethod
    def scratch():
        return [DMA((2,)), DMA((2,))]

    def begin(self, k):
        self.out[k].start()

    def arrive(self, k):
        self.back[k].wait_recv()

    def sent(self):
        for c in self.out:
            c.wait_send()

    def end(self):
        self.arrive(0)
        self.arrive(1)
        self.sent()


class HeadExchange:
    def __init__(self, place, own, got, sems, tile):
        self.p = p = place
        self.own, self.got, self.tile = own, got, tile
        ss, rs = sems
        peers = ((p.core, (p.tc, p.tcy), p.tc), (p.y, (p.ty, p.t), p.ty), ((p.d, p.tcy), (p.tcy, p.tc), p.tcy))
        self.out = [[rcopy(own.at[rows(tiles[k], tile)], got.at[p.t, k], ss.at[i, k], rs.at[i, k], dev) for k in (0, 1)]
                    for i, (dev, tiles, _) in enumerate(peers)]
        self.back = [[rcopy(got.at[src, k], got.at[src, k], ss.at[i, k], rs.at[i, k], dev) for k in (0, 1)]
                     for i, (dev, _, src) in enumerate(peers)]

    @staticmethod
    def scratch(tile, width):
        return [pltpu.VMEM((4, 2, tile, width), BF), DMA((3, 2)), DMA((3, 2))]

    def begin(self):
        for k in (0, 1):
            for i in (1, 2, 0):
                self.out[i][k].start()
        self.got[self.p.t, 0] = self.own[rows(self.p.t, self.tile), :]
        self.got[self.p.t, 1] = self.own[rows(self.p.ty, self.tile), :]

    def arrive(self, k):
        for i in (0, 1, 2):
            self.back[i][k].wait_recv()

    def sent(self):
        for group in self.out:
            for c in group:
                c.wait_send()

    def project(self, k, weights):
        total = nt(self.got[0, k], weights[0])
        for s in range(1, 4):
            total = total + nt(self.got[s, k], weights[s])
        return total


class ChipSum:
    def __init__(self, place, refs):
        self.p = p = place
        self.s, self.r, self.ys, self.yr, self.ss, self.rs = refs
        self.core = [rcopy(self.s.at[k], self.r.at[k], self.ss.at[k], self.rs.at[k], p.core) for k in (0, 1)]
        self.y = [rcopy(self.ys.at[k], self.yr.at[1 - k], self.ss.at[2 + k], self.rs.at[3 - k], p.y) for k in (0, 1)]
        self.yback = [rcopy(self.ys.at[k], self.yr.at[k], self.ss.at[2 + k], self.rs.at[2 + k], p.y) for k in (0, 1)]

    @staticmethod
    def scratch(tile, width, hop=F32):
        return [pltpu.VMEM((2, tile, width), hop)] * 2 + [pltpu.VMEM((2, tile, width), BF)] * 2 + [DMA((4,)), DMA((4,))]

    def send(self, k, tile_fn):
        self.s[k] = tile_fn((self.p.tc, self.p.tcy)[k]).astype(self.s.dtype)
        self.core[k].start()

    def pass_on(self, k, tile_fn):
        part = tile_fn((self.p.t, self.p.ty)[k])
        self.core[k].wait_recv()
        self.ys[k] = (part + self.r[k].astype(F32)).astype(BF)
        self.y[k].start()

    def end(self, k):
        self.yback[k].wait_recv()
        return self.ys[k].astype(F32) + self.yr[k].astype(F32)

    def sent(self):
        for c in self.core + self.y:
            c.wait_send()


class RowGather:
    def __init__(self, place, full, sems):
        self.p = place
        self.full = full
        self.zs, self.zr, self.xs, self.xr = sems
        self.steps = place.n // 2

    @staticmethod
    def scratch(n):
        return [DMA((n // 2,))] * 4

    def zcopy(self, k, slot):
        return rcopy(self.full.at[slot], self.full.at[slot], self.zs.at[k], self.zr.at[k], self.p.z(k))

    def xcopy(self, k, slot):
        return rcopy(self.full.at[slot], self.full.at[slot], self.xs.at[k], self.xr.at[k], self.p.x)

    def begin(self):
        for k in range(1, self.steps):
            self.zcopy(k, self.p.d).start()
        self.xcopy(0, self.p.d).start()

    def sent(self):
        for k in range(1, self.steps):
            self.zcopy(k, self.p.d).wait_send()

    def forward(self, k):
        slot = self.p.from_z(k)
        self.zcopy(k, slot).wait_recv()
        self.xcopy(k, slot).start()

    def forward_all(self):
        for k in range(1, self.steps):
            self.forward(k)

    def end(self):
        for k in range(self.steps):
            self.xcopy(k, self.p.x_from_z(k)).wait_recv()
            self.xcopy(k, self.p.from_z(k)).wait_send()


def head_rows(qt, head):
    ids = lax.broadcasted_iota(jnp.int32, qt.shape, 0)
    return jnp.where((ids >= head * HEAD) & (ids < (head + 1) * HEAD), qt, 0.0).astype(BF)


def head_block(x, heads):
    ids = lax.broadcasted_iota(jnp.int32, x.shape, 1)
    return jnp.concatenate(
        [jnp.where((ids >= h * HEAD) & (ids < (h + 1) * HEAD), x, 0.0).astype(BF) for h in range(heads)], axis=0
    )


def segment_starts(seg):
    start = jnp.zeros(seg.shape, jnp.int32)
    for s in range(SEGS - 1):
        count = jnp.sum(jnp.where(seg == s, 1, 0), axis=1, keepdims=True)
        start = start + jnp.where(seg > s, count, 0)
    return start


def causal_mask(keys, tile, tau, start):
    key_place = lax.broadcasted_iota(jnp.int32, (keys, tile), 0)
    query_place = lax.broadcasted_iota(jnp.int32, (keys, tile), 1) + tau * tile
    return (key_place <= query_place) & (key_place >= start)


def plot_order(seg, plot_ref):
    counts = [jnp.sum(jnp.where(seg == s, 1, 0), axis=1, keepdims=True) for s in range(SEGS)]
    place = lax.broadcasted_iota(jnp.int32, seg.shape, 1)
    first = jnp.zeros((1, 1), jnp.int32)
    for s in range(SEGS):
        shift = jnp.zeros((1, 1), jnp.int32)
        for o in range(SEGS):
            if o != s:
                ahead = plot_ref[o] < plot_ref[s] if o > s else plot_ref[o] <= plot_ref[s]
                shift = shift + counts[o] * (ahead.astype(jnp.int32) - (1 if o < s else 0))
        place = place + jnp.where(seg == s, shift, 0)
        first = first + counts[s] * (plot_ref[s] == 0).astype(jnp.int32)
    return place, first


def order_tile(place, i, tile):
    spot = lax.broadcasted_iota(jnp.int32, (tile, place.shape[1]), 0) + i * tile
    return jnp.where(place == spot, 1.0, 0.0).astype(BF)


class Slots:
    tile = 256

    def __init__(self, place, first):
        self.place = place
        self.split = jnp.sum(first)
        self.zero_tiles = lax.div(self.split + (self.tile - 1), self.tile)
        self.shared = self.zero_tiles - lax.div(self.split, self.tile)
        self.count = place.shape[1] // self.tile + 1

    def at(self, s):
        plot = (s >= self.zero_tiles).astype(jnp.int32)
        i = s - plot * self.shared
        spot = lax.broadcasted_iota(jnp.int32, (1, self.tile), 1) + i * self.tile
        side = (spot >= self.split).astype(jnp.int32)
        counts = (side == plot) & (spot < self.place.shape[1])
        return plot, order_tile(self.place, i, self.tile), counts


def first_kernel(n, gather, heads, plot_ref, x0_ref, cot_ref, gain_ref, seg_ref, sa_ref, sb_ref, sc_ref, sd_ref, m_hbm,
                 lse_ref, qct_ref, c_ref, ct_ref, lsec_ref,
                 qkv_out, qkvt_out, a_out, at_out, x1_out, ga_out, gb_out, gc_out, gd_out, h0_out, h1_out, e3_out, kv_out, kvt_out, wo1_out, wa3_out,
                 qkv_ref, qkvt_ref, a_ref, at_ref, x1_ref,
                 ga, gb, gc, gd, h0, h1, e3, kv, kvt, wo0, wo1, wa3, xf, m_ref, vte, ctok, score, raised, lsem, osem, *rest):
    rest = list(rest)

    def take(count):
        got = rest[:count]
        del rest[:count]
        return got

    p = Place(n)
    tile = x0_ref.shape[0]
    width = heads * HEAD
    tiles = h0.shape[0] // tile
    load_m = pltpu.make_async_copy(m_hbm, m_ref, lsem.at[0])
    load_m.start()
    swaps = [TileSwap(p, full, take(2), tile) for full in (xf, e3)]
    shares = [CoreShare(p, full, take(2), tile) for full in (h0, e3, h1)]
    spreads = [TensorGather(p, full, take(2)) for full in (wo0, wo1, wa3)]
    heads_in, hs, hr = take(3)
    exchange = HeadExchange(p, a_ref, heads_in, (hs, hr), tile)
    xf[rows(p.t, tile), :] = x0_ref[...]
    e3[rows(p.t, tile), :] = cot_ref[...]
    if gather:
        parts = [RowGather(p, full, take(4)) for full in (ga, gb, gc, gd)]
        for full, shard in ((ga, sa_ref), (gb, sb_ref), (gc, sc_ref), (gd, sd_ref)):
            full[p.d] = shard[...]
        greet([p.core, p.y, (p.d, p.tcy), p.x] + [p.z(k) for k in range(1, n // 2)])
        swaps[0].begin()
        parts[0].begin()
    else:
        copies = [pltpu.make_async_copy(s, f, lsem.at[1 + i]) for i, (s, f) in
                  enumerate(((sa_ref, ga), (sb_ref, gb), (sc_ref, gc), (sd_ref, gd)))]
        for c in copies:
            c.start()
        greet([p.core, p.y, (p.d, p.tcy)])
        swaps[0].begin()

    def normed(v, i):
        return norm(v, gain_ref[i : i + 1, :]).astype(BF)

    def pair(k):
        return rows((p.t, p.ty)[k], tile)

    h0[pair(0), :] = normed(x0_ref[...].astype(F32), 0)
    shares[0].begin(0)
    start = segment_starts(seg_ref[...])
    swaps[0].end()
    swaps[1].begin()
    h0[pair(1), :] = normed(xf[pair(1), :].astype(F32), 0)
    shares[0].begin(1)
    if gather:
        parts[0].forward_all()
        parts[1].begin()
    shares[0].end()
    if gather:
        parts[0].end()
    else:
        for c in copies:
            c.wait()
    spreads[0].begin(flat(ga)[:, 3 * width : 4 * width])

    wa = flat(ga)
    for i in range(tiles):
        at = slice(i * tile, (i + 1) * tile)
        x = nn(h0[at, :], wa[:, : 3 * width])
        qkv_ref[at, :] = x.astype(BF)
        qkvt_ref[:, at] = x.T.astype(BF)
    put = Puts(osem)
    put(ga, ga_out)
    put(h0, h0_out)
    put(qkv_ref, qkv_out)
    put(qkvt_ref, qkvt_out)
    swaps[1].end()
    shares[1].begin(0)
    shares[1].begin(1)
    if gather:
        parts[2].begin()

    for i in range(tiles):
        at = slice(i * tile, (i + 1) * tile)
        keys = (i + 1) * tile
        kk = qkv_ref[0:keys, width : 2 * width]
        qt = qkvt_ref[0:width, at].astype(F32) * SCALE
        allowed = causal_mask(keys, tile, i, start[:, at])
        for h in range(heads):
            s = jnp.where(allowed, nn(kk, head_rows(qt, h)), MASKED)
            peak = jnp.max(s, axis=0, keepdims=True)
            e = jnp.exp(s - peak)
            total = jnp.sum(e, axis=0, keepdims=True)
            w = (e * (1.0 / total)).astype(BF)
            vt = qkvt_ref[2 * width + h * HEAD : 2 * width + (h + 1) * HEAD, 0:keys]
            at_ref[h * HEAD : (h + 1) * HEAD, at] = nn(vt, w)
            lse_ref[h : h + 1, at] = peak + jnp.log(total)
        a_ref[at, :] = at_ref[:, at].T.astype(BF)
        if i == 1:
            spreads[0].forward()
        if gather and i < 3:
            parts[1].forward(i + 1)
    exchange.begin()
    put(a_ref, a_out)
    put(at_ref, at_out)
    if gather:
        for k in range(4, n // 2):
            parts[1].forward(k)
    shares[1].end()
    put(e3, e3_out)
    spreads[0].end()
    if gather:
        parts[1].end()
        parts[3].begin()
    put(gb, gb_out)
    load_m.wait()
    mtiles = m_ref.shape[0] // 256

    def project_memory(i, carry):
        x = nn(m_ref[rows(i, 256), :], flat(gb)[:, : 2 * width])
        kv[rows(i, 256), :] = x.astype(BF)
        kvt[:, rows(i, 256)] = x.T.astype(BF)
        return carry

    lax.fori_loop(0, mtiles, project_memory, 0)
    put(kv, kv_out)
    put(kvt, kvt_out)
    for k in (0, 1):
        exchange.arrive(k)
        x1 = xf[pair(k), :].astype(F32) + exchange.project(k, wo0)
        x1_ref[k] = x1
        h1[pair(k), :] = normed(x1, 1)
        shares[2].begin(k)
    put(x1_ref, x1_out)
    if gather:
        parts[2].forward_all()
    spreads[1].begin(flat(gb)[:, 3 * width : 4 * width])
    spreads[2].begin(flat(gb)[:, 2 * width : 3 * width])
    shares[2].end()
    put(h1, h1_out)
    wq = flat(gb)[:, 2 * width : 3 * width]
    for i in range(tiles):
        at = slice(i * tile, (i + 1) * tile)
        qct_ref[:, at] = nn(h1[at, :], wq).T.astype(BF)

    states = kv.shape[0]
    patches = states // 2
    ext = HEAD + 16
    for h in range(heads):
        vte[h * ext : h * ext + HEAD, :] = kvt[width + h * HEAD : width + (h + 1) * HEAD, :]
        vte[h * ext + HEAD : (h + 1) * ext, :] = jnp.ones((16, states), BF)
    ctok[...] = jnp.zeros(ctok.shape, F32)
    lsec_ref[...] = jnp.zeros(lsec_ref.shape, F32)
    slots = Slots(*plot_order(seg_ref[...], plot_ref))

    def one_slot(s, carry):
        plot, order, counts = slots.at(s)
        qt = nt(qct_ref[...], order) * SCALE
        q = [head_rows(qt, h) for h in range(heads)]

        def scores(h, c, peak):
            near, far = slice(c * 256, (c + 1) * 256), slice(patches + c * 256, patches + (c + 1) * 256)
            x = nn(jnp.where(plot == 0, kv[near, 0:width], kv[far, 0:width]), q[h])
            score[h % 2, near] = x
            top = jnp.max(x, axis=0, keepdims=True)
            return top if peak is None else jnp.maximum(peak, top)

        chunks = patches // 256
        peak = None
        for c in range(chunks):
            peak = scores(0, c, peak)
        for h in range(heads):
            ahead = None
            for c in range(chunks):
                if h + 1 < heads:
                    ahead = scores(h + 1, c, ahead)
                near = slice(c * 256, (c + 1) * 256)
                raised[h % 2, near] = jnp.exp(score[h % 2, near] - peak).astype(BF)
            hs = slice(h * ext, (h + 1) * ext)
            acc = nn(jnp.where(plot == 0, vte[hs, 0:patches], vte[hs, patches:states]), raised[h % 2])
            total = acc[HEAD : HEAD + 1, :]
            ct_ref[s, h * HEAD : (h + 1) * HEAD, :] = jnp.where(counts, acc[0:HEAD, :] * (1.0 / total), 0.0)
            lsec_ref[s, h : h + 1, :] = jnp.where(counts, peak + jnp.log(total), -MASKED)
            peak = ahead
        ctok[...] += nn(ct_ref[s].astype(BF), order)
        if gather:
            for k in range(1, n // 2):
                pl.when(s == min(k - 1, slots.count - 1))(functools.partial(parts[3].forward, k))
        return carry

    lax.fori_loop(0, slots.count, one_slot, 0)
    c_ref[...] = ctok[...].T.astype(BF)
    spreads[1].forward()
    spreads[2].forward()
    spreads[1].end()
    put(wo1, wo1_out)
    spreads[2].end()
    put(wa3, wa3_out)
    exchange.sent()
    if gather:
        for part in parts:
            part.sent()
        parts[2].end()
        parts[3].end()
    put(gc, gc_out)
    put(gd, gd_out)
    put.end()


def call_first(n, gather, plot_ids, x0, cot, gain, seg, sa, sb, sc, sd, mem):
    tile, width_d = x0.shape
    length = seg.shape[1]
    states = mem.shape[0]
    cols = sa.shape[-1]
    width = cols // 4
    heads = width // HEAD
    chunk = (8, width_d // 8)
    shapes = [chunk + (s.shape[-1],) for s in (sa, sb, sc, sd)]
    spread = (4, width_d, width)
    early = [
        sds((length, 3 * width), BF),
        sds((3 * width, length), BF),
        sds((length, width), BF),
        sds((width, length), F32),
        sds((2, tile, width_d), F32),
    ]
    late = [
        sds(shapes[0], BF),
        sds(shapes[1], BF),
        sds(shapes[2], BF),
        sds(shapes[3], BF),
        sds((length, width_d), BF),
        sds((length, width_d), BF),
        sds((length, width_d), BF),
        sds((states, 2 * width), BF),
        sds((2 * width, states), BF),
        sds(spread, BF),
        sds(spread, BF),
    ]
    out_shape = [
        sds((8, length), F32),
        sds((width, length), BF),
        sds((length, width), BF),
        sds((length // 256 + 1, width, 256), F32),
        sds((length // 256 + 1, 8, 256), F32),
    ] + early + late
    scratch = [pltpu.VMEM(s.shape, s.dtype) for s in early] + [pltpu.VMEM(s, BF) for s in shapes]
    scratch += [pltpu.VMEM((length, width_d), BF)] * 3
    scratch += [
        pltpu.VMEM((states, 2 * width), BF),
        pltpu.VMEM((2 * width, states), BF),
        pltpu.VMEM(spread, BF),
        pltpu.VMEM(spread, BF),
        pltpu.VMEM(spread, BF),
        pltpu.VMEM((length, width_d), BF),
        pltpu.VMEM((states, width_d), BF),
        pltpu.VMEM((heads * (HEAD + 16), states), BF),
        pltpu.VMEM((width, length), F32),
        pltpu.VMEM((2, states // 2, 256), F32),
        pltpu.VMEM((2, states // 2, 256), BF),
        DMA((5,)),
        DMA((len(early + late),)),
    ]
    scratch += TileSwap.scratch() * 2 + CoreShare.scratch() * 3 + TensorGather.scratch() * 3
    scratch += HeadExchange.scratch(tile, width)
    if gather:
        scratch += RowGather.scratch(n) * 4
    shard = VM if gather else ANY
    return pl.pallas_call(
        functools.partial(first_kernel, n, gather, heads),
        out_shape=out_shape,
        in_specs=[SM, VM, VM, VM, VM, shard, shard, shard, shard, ANY],
        out_specs=[VM] * 5 + [ANY] * len(early + late),
        scratch_shapes=scratch,
        compiler_params=pltpu.CompilerParams(collective_id=1, has_side_effects=True, vmem_limit_bytes=VLIMIT),
        name="attention_forward",
    )(plot_ids, x0, cot, gain, seg, sa, sb, sc, sd, mem)


def ffn_kernel(n, c_ref, gain_ref, x1_hbm, wo_hbm, gc_hbm, wn_hbm, e3_hbm,
               dgain_ref, f_out, g2_out, e2_out, du_out, x2_out,
               x1, wo, gc, wn, e3, f, g2, e2, du, x2, h2, dg, h2t, e3t, lsem, osem, *rest):
    rest = list(rest)

    def take(count):
        got = rest[:count]
        del rest[:count]
        return got

    p = Place(n)
    _, tile, width_d = x1.shape
    hidden = f.shape[1]
    heads_in, hs, hr = take(3)
    exchange = HeadExchange(p, c_ref, heads_in, (hs, hr), tile)
    shares = [CoreShare(p, full, take(2), tile) for full in (h2, e2)]
    total = ChipSum(p, take(6))
    put = Puts(osem)
    loads = [pltpu.make_async_copy(s, d, lsem.at[i]) for i, (s, d) in
             enumerate(((e3_hbm, e3), (wo_hbm, wo), (x1_hbm, x1), (gc_hbm, gc), (wn_hbm, wn)))]
    for load in loads:
        load.start()
    greet([p.core, p.y, (p.d, p.tcy)])
    exchange.begin()
    loads[0].wait()
    e3t[...] = e3[...].T

    def pair(k):
        return rows((p.t, p.ty)[k], tile)

    def hidden_tile(j):
        at = rows(j, tile)
        gate = nn(h2[at, :], flat(gc)[:, 0:hidden])
        up = nn(h2[at, :], flat(gc)[:, hidden : 2 * hidden])
        df = nn(e3[at, :], flat(wn))
        sq = gate * gate
        th = jnp.tanh(0.7978845608 * gate * (1.0 + 0.044715 * sq))
        half = 0.5 * (1.0 + th)
        act = gate * half
        slope = half + 0.5 * gate * (1.0 - th * th) * (0.7978845608 * (1.0 + 3.0 * 0.044715 * sq))
        f[at, :] = (act * up).astype(BF)
        dg[at, 0:hidden] = (df * up * slope).astype(BF)
        dg[at, hidden : 2 * hidden] = (df * act).astype(BF)

    def back_tile(j):
        return nt(dg[rows(j, tile), :], flat(gc)[:, 0 : 2 * hidden])

    for load in loads[1:]:
        load.wait()
    for k in (0, 1):
        exchange.arrive(k)
        x2[k] = x1[k] + exchange.project(k, wo)
        h2[pair(k), :] = norm(x2[k], gain_ref[2:3, :]).astype(BF)
        shares[0].begin(k)
    put(x2, x2_out)
    for k in (0, 1):
        hidden_tile((p.t, p.ty)[k])
        shares[0].arrive(k)
        hidden_tile((p.tc, p.tcy)[k])
        total.send(k, back_tile)
        if k == 1:
            total.pass_on(0, back_tile)
    total.pass_on(1, back_tile)
    put(f, f_out)
    h2t[...] = h2[...].T
    for i in range(2 * hidden // 256):
        cs = slice(i * 256, (i + 1) * 256)
        du[:, cs] = nn(h2t[...], dg[:, cs]).astype(BF)
    for i in range(hidden // 256):
        cs = slice(i * 256, (i + 1) * 256)
        du[:, 2 * hidden + i * 256 : 2 * hidden + (i + 1) * 256] = nn(e3t[...], f[:, cs]).astype(BF)
    put(du, du_out)
    for k in (0, 1):
        dv, dgain = norm_back(x2[k], gain_ref[2:3, :], total.end(k))
        if k == 0:
            dgain_ref[...] = dgain
        g2[k] = e3[pair(k), :].astype(F32) + dv
        e2[pair(k), :] = g2[k].astype(BF)
        shares[1].begin(k)
    put(g2, g2_out)
    shares[0].sent()
    exchange.sent()
    total.sent()
    shares[1].end()
    put(e2, e2_out)
    put.end()


def call_ffn(n, c, x1, gain, wo, gc, wn, e3):
    _, tile, width_d = x1.shape
    length, width = c.shape
    hidden = gc.shape[2] // 2
    late = [
        sds((length, hidden), BF),
        sds((2, tile, width_d), F32),
        sds((length, width_d), BF),
        sds((width_d, 3 * hidden), BF),
        sds((2, tile, width_d), F32),
    ]
    scratch = [pltpu.VMEM(v.shape, v.dtype) for v in [x1, wo, gc, wn, e3] + late]
    scratch += [
        pltpu.VMEM((length, width_d), BF),
        pltpu.VMEM((length, 2 * hidden), BF),
        pltpu.VMEM((width_d, length), BF),
        pltpu.VMEM((width_d, length), BF),
        DMA((5,)),
        DMA((len(late),)),
    ]
    scratch += HeadExchange.scratch(tile, width) + CoreShare.scratch() * 2 + ChipSum.scratch(tile, width_d)
    return pl.pallas_call(
        functools.partial(ffn_kernel, n),
        out_shape=[sds((1, width_d), F32)] + late,
        in_specs=[VM] * 2 + [ANY] * 5,
        out_specs=[VM] + [ANY] * len(late),
        scratch_shapes=scratch,
        compiler_params=pltpu.CompilerParams(collective_id=2, has_side_effects=True, vmem_limit_bytes=VLIMIT),
        name="ffn",
    )(c, gain, x1, wo, gc, wn, e3)


def cross_backward_kernel(n, reduce, heads, plot_ref, seg_ref, qct_ref, ct_ref, lse_ref, e2_hbm, gb_hbm, kv_hbm, kvt_hbm,
                          f_hbm, x2_hbm, wn_hbm, du_hbm, dqc_ref, dk_ref, dv_ref, blk_ref, *rest):
    rest = list(rest)

    def take(count):
        got = rest[:count]
        del rest[:count]
        return got

    p = Place(n)
    width = heads * HEAD
    states = kv_hbm.shape[0]
    patches = states // 2
    length = qct_ref.shape[1]
    hidden = f_hbm.shape[1]
    if reduce:
        du_out, mine_u = take(2)
        rest_u = RowSum(p, mine_u, take(6))
    dka, dva, dct_all, dqtok, vrow, e2, gb, kv, kvt, f, x2, wn, lsem = take(13)
    tile = x2.shape[0]
    block = TensorSum(p, take(9))
    pairs = [(f_hbm, f), (wn_hbm, wn), (e2_hbm, e2), (gb_hbm, gb), (kv_hbm, kv),
             (kvt_hbm.at[0:width], kvt), (x2_hbm.at[0], x2)]
    if reduce:
        pairs.insert(0, (du_hbm, mine_u))
    loads = [pltpu.make_async_copy(s, d, lsem.at[i]) for i, (s, d) in enumerate(pairs)]
    for load in loads:
        load.start()
    greet([p.core, p.y] + ([p.x] + [p.z(k) for k in range(1, n // 2)] if reduce else []))
    if reduce:
        loads.pop(0).wait()
        rest_u.begin()
    loads[0].wait()
    loads[1].wait()

    def out_tile(j):
        return nt(f[rows(j, tile), :], flat(wn))

    block.send(out_tile)
    for load in loads[2:]:
        load.wait()
    dka[...] = jnp.zeros(dka.shape, F32)
    dva[...] = jnp.zeros(dva.shape, F32)
    dqtok[...] = jnp.zeros(dqtok.shape, F32)
    vrow[...] = kv[:, width : 2 * width]
    wo = flat(gb)[:, 3 * width : 4 * width]
    for i in range(length // 256):
        at = slice(i * 256, (i + 1) * 256)
        dct_all[:, at] = nn(e2[at, :], wo).T.astype(BF)
    block.pass_on(out_tile)
    slots = Slots(*plot_order(seg_ref[...], plot_ref))

    def one_slot(s, carry):
        plot, order, _ = slots.at(s)
        dct = nt(dct_all[...], order)
        qt = nt(qct_ref[...], order) * SCALE
        kk = jnp.where(plot == 0, kv[0:patches, 0:width], kv[patches:states, 0:width])
        vv = jnp.where(plot == 0, vrow[0:patches, :], vrow[patches:states, :])
        ps, ds, dq = [], [], []
        for h in range(heads):
            hs = slice(h * HEAD, (h + 1) * HEAD)
            inner = jnp.sum(dct[hs, :] * ct_ref[s, hs, :], axis=0, keepdims=True)
            prob = jnp.exp(nn(kk, head_rows(qt, h)) - lse_ref[s, h : h + 1, :])
            grad = (prob * (nn(vv, head_rows(dct, h)) - inner)).astype(BF)
            ps.append(prob.astype(BF))
            ds.append(grad)
            kt = jnp.where(plot == 0, kvt[hs, 0:patches], kvt[hs, patches:states])
            dq.append(nn(kt, grad))
        dqtok[...] += nn((jnp.concatenate(dq, axis=0) * SCALE).astype(BF), order)
        dv = nn(jnp.concatenate(ps, axis=1), head_block(dct.T, heads))
        dk = nn(jnp.concatenate(ds, axis=1), head_block(qt.T, heads))
        for j in range(2):
            part = slice(j * patches, (j + 1) * patches)
            dva[part, :] += jnp.where(plot == j, dv, 0.0)
            dka[part, :] += jnp.where(plot == j, dk, 0.0)
        if reduce:
            for k in range(1, n // 2):
                pl.when(s == min(k - 1, slots.count - 1))(functools.partial(rest_u.step, k))
        return carry

    lax.fori_loop(0, slots.count, one_slot, 0)
    dqc_ref[...] = dqtok[...].T.astype(BF)
    dk_ref[...] = dka[...].astype(BF)
    dv_ref[...] = dva[...].astype(BF)
    blk_ref[...] = (x2[...] + block.end()).astype(BF)
    if reduce:
        du_out[...] = rest_u.end()
        rest_u.sent()


def call_cross_backward(n, reduce, plot_ids, seg, e2, gb, qct, kv, kvt, ct, lse, f, x2, wn, du):
    width, length = qct.shape
    states = kv.shape[0]
    _, tile, width_d = x2.shape
    out_shape = [
        sds((length, width), BF),
        sds((states, width), BF),
        sds((states, width), BF),
        sds((tile, width_d), BF),
    ]
    scratch = []
    if reduce:
        shard = width_d // n
        out_shape.append(sds((shard, du.shape[1]), F32))
        scratch += [pltpu.VMEM((n, shard, du.shape[1]), BF)] + RowSum.scratch(n, shard, du.shape[1])
        du = du.reshape(n, shard, du.shape[1])
    scratch += [
        pltpu.VMEM((states, width), F32),
        pltpu.VMEM((states, width), F32),
        pltpu.VMEM((width, length), BF),
        pltpu.VMEM((width, length), F32),
        pltpu.VMEM((states, width), BF),
        pltpu.VMEM(e2.shape, BF),
        pltpu.VMEM(gb.shape, BF),
        pltpu.VMEM(kv.shape, BF),
        pltpu.VMEM((width, states), BF),
        pltpu.VMEM(f.shape, BF),
        pltpu.VMEM((tile, width_d), F32),
        pltpu.VMEM(wn.shape, BF),
        DMA((8,)),
    ] + TensorSum.scratch(tile, width_d, BF)
    return pl.pallas_call(
        functools.partial(cross_backward_kernel, n, reduce, width // HEAD),
        out_shape=out_shape,
        in_specs=[SM] + [VM] * 4 + [ANY] * 8,
        out_specs=[VM] * len(out_shape),
        scratch_shapes=scratch,
        compiler_params=pltpu.CompilerParams(collective_id=4, has_side_effects=True, vmem_limit_bytes=VLIMIT),
        name="cross_backward",
    )(plot_ids, seg, qct, ct, lse, e2, gb, kv, kvt, f, x2, wn, du)


class RowSum:
    def __init__(self, place, mine, refs):
        self.p = place
        self.mine = mine
        self.near, self.far, self.xs, self.xr, self.zs, self.zr = refs
        self.steps = place.n // 2

    @staticmethod
    def scratch(n, shard, width):
        return [pltpu.VMEM((n // 2, shard, width), BF)] * 2 + [DMA((n // 2,))] * 4

    def slot(self, k):
        return lax.rem(self.p.d + 2 * k, self.p.n)

    def xcopy(self, k):
        there = lax.rem(self.p.dx + 2 * k, self.p.n)
        return rcopy(self.mine.at[there], self.near.at[k], self.xs.at[k], self.xr.at[k], self.p.x)

    def zcopy(self, k):
        return rcopy(self.near.at[k], self.far.at[k], self.zs.at[k], self.zr.at[k], self.p.z(k))

    def begin(self):
        for k in list(range(1, self.steps)) + [0]:
            self.xcopy(k).start()

    def step(self, k):
        self.xcopy(k).wait_recv()
        self.near[k] = (self.mine[self.slot(k)].astype(F32) + self.near[k].astype(F32)).astype(BF)
        self.zcopy(k).start()

    def end(self):
        self.xcopy(0).wait_recv()
        total = self.mine[self.p.d].astype(F32) + self.near[0].astype(F32)
        for k in range(1, self.steps):
            self.zcopy(k).wait_recv()
            total = total + self.far[k].astype(F32)
        return total

    def sent(self):
        for k in range(1, self.steps):
            self.zcopy(k).wait_send()
        for k in range(self.steps):
            self.xcopy(k).wait_send()


def squares_of(x):
    return jnp.sum(jnp.sum(x * x, axis=1, keepdims=True), axis=0, keepdims=True)


class EveryoneSum:
    def __init__(self, place, refs):
        self.p = place
        self.bt, self.bd, self.ts, self.tr, self.ds, self.dr = refs
        n = place.n
        self.tensor_peers = [(place.d, lax.rem(place.t + k, 4)) for k in range(1, 4)]
        self.dp_peers = [(lax.rem(place.d + k, n), place.t) for k in range(1, n)]

    @staticmethod
    def scratch(n, width):
        return [pltpu.VMEM((4, 8, width), F32), pltpu.VMEM((n, 8, width), F32), DMA((4,)), DMA((4,)), DMA((n,)), DMA((n,))]

    def hop(self, buf, ss, rs, peers, me):
        count = len(peers) + 1
        copies = [rcopy(buf.at[0], buf.at[k], ss.at[k], rs.at[k], peers[k - 1]) for k in range(1, count)]
        for c in copies:
            c.start()
        for c in copies:
            c.wait_recv()
        total = buf[lax.rem(me + count, count)]
        for j in range(1, count):
            total = total + buf[lax.rem(me - j + count, count)]
        for c in copies:
            c.wait_send()
        return total

    def run(self, mine):
        self.bt[0] = mine
        self.bd[0] = self.hop(self.bt, self.ts, self.tr, self.tensor_peers, self.p.t)
        return self.hop(self.bd, self.ds, self.dr, self.dp_peers, self.p.d)


def self_backward_kernel(n, reduce, heads, x0_ref, x1_ref, g2_ref, gain_ref, dgain2_ref, seg_ref, dqc_ref, dk_ref, dv_ref, du_ref,
                         e2_hbm, h1_hbm, h0_hbm, m_hbm, ga_hbm, gb_hbm, c_hbm, a_hbm, qkv_hbm, qkvt_hbm,
                         at_hbm, lse_hbm, wa3_hbm, *rest):
    rest = list(rest)

    def take(count):
        got = rest[:count]
        del rest[:count]
        return got

    p = Place(n)
    _, tile, width_d = x1_ref.shape
    width = heads * HEAD
    if reduce:
        res_ref, mem_ref, stat_ref, gb_out, go_out, ga_out = take(6)
        mine_b, mine_o, mine_a = take(3)
        rest_b, rest_o, rest_a = (RowSum(p, m, take(6)) for m in (mine_b, mine_o, mine_a))
        everyone = EveryoneSum(p, take(6))
    else:
        res_ref, mem_ref, stat_ref, mine_b, mine_o, mine_a = take(6)
    ga, gb, c, a, qkv, qkvt, att, lse, wa3, ring, e1, dqkv, dka, dva, tr, lsem, rsem = take(17)
    length = e1.shape[0]
    tiles = length // tile
    pairs = [(wa3_hbm, wa3), (gb_hbm, gb), (c_hbm, c), (a_hbm, a), (qkv_hbm, qkv), (qkvt_hbm, qkvt), (at_hbm, att), (lse_hbm, lse), (ga_hbm, ga)]
    loads = [pltpu.make_async_copy(s, d, lsem.at[i]) for i, (s, d) in enumerate(pairs)]
    states = dk_ref.shape[0]
    wanted = [m_hbm.at[i * length : (i + 1) * length] for i in range(states // length)] + [h1_hbm, e2_hbm, h0_hbm]
    turns = [pltpu.make_async_copy(s, ring.at[i % 2], rsem.at[i % 2]) for i, s in enumerate(wanted)]
    loads[0].start()
    loads[1].start()
    turns[0].start()
    for load in loads[2:]:
        load.start()

    def turn(i):
        turns[i].wait()
        if i + 1 < len(turns):
            turns[i + 1].start()
        tr[...] = ring[i % 2].T

    heads_in, hs, hr = take(3)
    exchange = HeadExchange(p, dqc_ref, heads_in, (hs, hr), tile)
    share = CoreShare(p, e1, take(2), tile)
    last = TensorSum(p, take(9))
    ms0, ms1, mr0, mr1, myr, mss, mrs = take(7)
    if reduce:
        greet([p.x] + [p.z(k) for k in range(1, n // 2)] + everyone.tensor_peers + [
            (lax.rem(p.d + k, n), p.t) for k in range(1, n)
        ])
    else:
        greet([p.core, p.y, (p.d, p.tcy)])
    exchange.begin()

    def pair(k):
        return rows((p.t, p.ty)[k], tile)

    def put(mine, i, value):
        mine[:, :, i * width : (i + 1) * width] = value.astype(BF).reshape(mine.shape[0], -1, width)

    plots = mem_ref.shape[0]
    patches = states // plots
    blocks = patches // 4 // 256

    def mem_part(owner, b):
        at = pl.ds(pl.multiple_of(b // blocks * patches + owner * (patches // 4) + b % blocks * 256, 256), 256)
        return nt(dk_ref[at, :], flat(gb)[:, 0:width]) + nt(dv_ref[at, :], flat(gb)[:, width : 2 * width])

    total_blocks = plots * blocks
    mc0 = [rcopy(ms0.at[b], mr0.at[b], mss.at[0, b], mrs.at[0, b], p.core) for b in range(total_blocks)]
    mc1 = [rcopy(ms1.at[b], mr1.at[b], mss.at[1, b], mrs.at[1, b], p.core) for b in range(total_blocks)]
    mcy = [rcopy(ms0.at[b], myr.at[b], mss.at[2, b], mrs.at[2, b], p.y) for b in range(total_blocks)]
    loads[1].wait()
    for b in range(total_blocks):
        ms0[b] = mem_part(p.tcy, b).astype(BF)
        mc0[b].start()
    for b in range(total_blocks):
        ms1[b] = mem_part(p.tc, b).astype(BF)
        mc1[b].start()

    for i in range(states // length):
        part = slice(i * length, (i + 1) * length)
        turn(i)
        if i == 0:
            dka[...] = nn(tr[...], dk_ref[part, :])
            dva[...] = nn(tr[...], dv_ref[part, :])
        else:
            dka[...] += nn(tr[...], dk_ref[part, :])
            dva[...] += nn(tr[...], dv_ref[part, :])
    put(mine_b, 0, dka[...])
    put(mine_b, 1, dva[...])

    loads[0].wait()
    g1 = []
    dgain1 = None
    for k in (0, 1):
        exchange.arrive(k)
        dv1, dgain = norm_back(x1_ref[k], gain_ref[1:2, :], exchange.project(k, wa3))
        dgain1 = dgain if k == 0 else dgain1
        g1.append(g2_ref[k] + dv1)
        e1[pair(k), :] = g1[k].astype(BF)
        share.begin(k)
    for b in range(total_blocks):
        mc0[b].wait_recv()
        mc0[b].wait_send()
        ms0[b] = (mem_part(p.ty, b) + mr0[b].astype(F32)).astype(BF)
        mcy[b].start()
    turn(states // length)
    put(mine_b, 2, nn(tr[...], dqc_ref[...]))
    turn(states // length + 1)
    loads[2].wait()
    put(mine_b, 3, nn(tr[...], c[...]))
    if reduce:
        rest_b.begin()
    for load in loads[3:]:
        load.wait()
    share.end()
    tr[...] = e1[...].T
    put(mine_o, 0, nn(tr[...], a[...]))
    if reduce:
        rest_o.begin()

    start = segment_starts(seg_ref[...])
    wo = flat(ga)[:, 3 * width : 4 * width]
    for i in range(tiles):
        at = slice(i * tile, (i + 1) * tile)
        keys = (i + 1) * tile
        da = nn(e1[at, :], wo)
        dar = da.astype(BF)
        dat = da.T.astype(BF).astype(F32)
        qt = qkvt[0:width, at].astype(F32) * SCALE
        allowed = causal_mask(keys, tile, i, start[:, at])
        kk = qkv[0:keys, width : 2 * width]
        vv = qkv[0:keys, 2 * width : 3 * width]
        ps, ds, dq = [], [], []
        for h in range(heads):
            hs = slice(h * HEAD, (h + 1) * HEAD)
            inner = jnp.sum(dat[hs, :] * att[hs, at], axis=0, keepdims=True)
            prob = jnp.where(allowed, jnp.exp(nn(kk, head_rows(qt, h)) - lse[h : h + 1, at]), 0.0)
            grad = (prob * (nn(vv, head_rows(dat, h)) - inner)).astype(BF)
            ps.append(prob.astype(BF))
            ds.append(grad)
            dq.append(nn(qkvt[width + h * HEAD : width + (h + 1) * HEAD, 0:keys], grad))
        dqkv[at, 0:width] = (jnp.concatenate(dq, axis=0) * SCALE).T
        dk = nn(jnp.concatenate(ds, axis=1), head_block(qkv[at, 0:width].astype(F32) * SCALE, heads))
        dv = nn(jnp.concatenate(ps, axis=1), head_block(dar.astype(F32), heads))
        if i:
            dqkv[0 : keys - tile, width : 2 * width] += dk[0 : keys - tile]
            dqkv[0 : keys - tile, 2 * width : 3 * width] += dv[0 : keys - tile]
        dqkv[at, width : 2 * width] = dk[keys - tile :]
        dqkv[at, 2 * width : 3 * width] = dv[keys - tile :]
        if reduce and 0 < i < n // 2:
            rest_b.step(i)
    turn(states // length + 2)
    mine_a[...] = nn(tr[...], dqkv[...].astype(BF)).astype(BF).reshape(mine_a.shape)
    if reduce:
        rest_a.begin()
    last.begin(lambda j: nt(dqkv[rows(j, tile), :].astype(BF), flat(ga)[:, 0 : 3 * width]))
    if reduce:
        for k in range(tiles, n // 2):
            rest_b.step(k)
        for k in range(1, n // 2):
            rest_o.step(k)
        for k in range(1, n // 2):
            rest_a.step(k)
    for b in range(total_blocks):
        mc1[b].wait_recv()
        mcy[b].wait_recv()
        own = mem_part(p.t, b) + mr1[b].astype(F32) + myr[b].astype(F32)
        mem_ref[b // blocks, (b % blocks) * 256 : (b % blocks + 1) * 256, :] = own.astype(BF)
    dv0, dgain0 = norm_back(x0_ref[...].astype(F32), gain_ref[0:1, :], last.end())
    res_ref[...] = (g1[0] + dv0).astype(BF)
    row = lax.broadcasted_iota(jnp.int32, (8, width_d), 0)
    stat = jnp.where(row == 0, dgain0, jnp.where(row == 1, dgain1, jnp.where(row == 2, dgain2_ref[...], 0.0)))
    if reduce:
        total_b = rest_b.end()
        gb_out[...] = total_b
        squares = squares_of(total_b)
        total_o = rest_o.end()
        go_out[...] = total_o
        squares = squares + squares_of(total_o)
        total_a = rest_a.end()
        ga_out[...] = total_a
        squares = squares + squares_of(total_a)
        stat = everyone.run(jnp.where(row == 3, squares + squares_of(du_ref[...]), stat))
        for r in (rest_b, rest_o, rest_a):
            r.sent()
    stat_ref[...] = stat
    exchange.sent()
    for cpy in mc1 + mcy:
        cpy.wait_send()


def call_self_backward(n, reduce, plots, x0, x1, g2, gain, dgain2, seg, dqc, dk, dv, du,
                       e2, h1, h0, mem, ga, gb, c, a, qkv, qkvt, att, lse, wa3):
    _, tile, width_d = x1.shape
    length, width = dqc.shape
    states = mem.shape[0]
    patches = states // plots
    total_blocks = plots * (patches // 4 // 256)
    shard = width_d // n
    widths = (4 * width, width, 3 * width)
    out_shape = [
        sds((tile, width_d), BF),
        sds((plots, patches // 4, width_d), BF),
        sds((8, width_d), F32),
    ]
    scratch = []
    if reduce:
        out_shape += [sds((shard, w), F32) for w in widths]
        scratch += [pltpu.VMEM((n, shard, w), BF) for w in widths]
        for w in widths:
            scratch += RowSum.scratch(n, shard, w)
        scratch += EveryoneSum.scratch(n, width_d)
    else:
        out_shape += [sds((8, width_d // 8, w), BF) for w in widths]
    scratch += [pltpu.VMEM(v.shape, v.dtype) for v in (ga, gb, c, a, qkv, qkvt, att, lse, wa3)]
    scratch += [
        pltpu.VMEM((2, length, width_d), BF),
        pltpu.VMEM((length, width_d), BF),
        pltpu.VMEM((length, 3 * width), F32),
        pltpu.VMEM((width_d, width), F32),
        pltpu.VMEM((width_d, width), F32),
        pltpu.VMEM((width_d, length), BF),
        DMA((13,)),
        DMA((2,)),
    ]
    scratch += HeadExchange.scratch(tile, width) + CoreShare.scratch()
    scratch += TensorSum.scratch(tile, width_d)
    scratch += [pltpu.VMEM((total_blocks, 256, width_d), BF)] * 5 + [DMA((3, total_blocks))] * 2
    return pl.pallas_call(
        functools.partial(self_backward_kernel, n, reduce, width // HEAD),
        out_shape=out_shape,
        in_specs=[VM] * 10 + [ANY] * 13,
        out_specs=[VM] * len(out_shape),
        scratch_shapes=scratch,
        compiler_params=pltpu.CompilerParams(collective_id=3, has_side_effects=True, vmem_limit_bytes=VLIMIT),
        name="self_backward",
    )(x0, x1, g2, gain, dgain2, seg, dqc, dk, dv, du, e2, h1, h0, mem, ga, gb, c, a, qkv, qkvt, att, lse, wa3)


def adam_step(master, moment, second, gradient, step_rate, decay_rate):
    moment_new = BETA_ONE * moment + (1.0 - BETA_ONE) * gradient
    second_new = BETA_TWO * second + (1.0 - BETA_TWO) * gradient * gradient
    moment_hat = moment_new / (1.0 - BETA_ONE**STEP)
    second_hat = second_new / (1.0 - BETA_TWO**STEP)
    master_new = master - step_rate * (
        moment_hat / (jnp.sqrt(second_hat) + ADAM_EPS) + decay_rate * master
    )
    return (master_new, moment_new, second_new)


def update_kernel(width, hidden, *refs):
    stat_ref, u_ref, b_ref, o_ref, a_ref = refs[0:5]
    params = [refs[5 + 3 * i : 8 + 3 * i] for i in range(6)]
    passed = refs[23:26]
    norm_ref = refs[26]
    outs = [refs[27 + 4 * i : 31 + 4 * i] for i in range(5)]
    gain_outs = refs[47:50]
    for src, dst in zip(passed, refs[50:53]):
        dst[...] = src[...]
    gains = stat_ref[0:3, :]
    grad_norm = jnp.sqrt(stat_ref[3:4, 0:1] + squares_of(gains))
    norm_ref[...] = grad_norm
    factor = jnp.minimum(1.0, CLIP / (grad_norm + 1e-06))

    def columns(ref, i, size):
        return ref[:, i * size : (i + 1) * size]

    grads = (
        [columns(a_ref, 0, width), columns(a_ref, 1, width), columns(a_ref, 2, width), columns(b_ref, 2, width)],
        [columns(b_ref, 0, width), columns(b_ref, 1, width)],
        [o_ref[...].T, columns(b_ref, 3, width).T],
        [columns(u_ref, 0, hidden), columns(u_ref, 1, hidden)],
        [columns(u_ref, 2, hidden)],
    )
    rates = (RATE_INNER, RATE_INNER, RATE_OUTER, RATE_INNER, RATE_INNER)
    for (master, moment, second), out, parts, rate in zip(params[0:5], outs, grads, rates):
        for i, g in enumerate(parts):
            at = i if len(master.shape) == 3 else Ellipsis
            new = adam_step(master[at], moment[at], second[at], g * factor, rate, DECAY)
            for ref, value in zip(out, new + (new[0],)):
                ref[at] = value.astype(ref.dtype)
    new = adam_step(*(r[...] for r in params[5]), gains * factor, RATE_GAIN, 0.0)
    for ref, value in zip(gain_outs, new):
        ref[...] = value


def call_update(stat, own, weights, passed):
    flat_weights = [w for group in weights for w in group]
    out_shape = [sds((1, 1), F32)]
    for group in weights[0:5]:
        out_shape += [sds(group[0].shape, F32)] * 3 + [sds(group[0].shape, BF)]
    out_shape += [sds(weights[5][0].shape, F32)] * 3
    out_shape += [sds(v.shape, BF) for v in passed]
    return pl.pallas_call(
        functools.partial(update_kernel, weights[0][0].shape[2], weights[3][0].shape[2]),
        out_shape=out_shape,
        in_specs=[VM] * 26,
        out_specs=[VM] * 27,
        compiler_params=pltpu.CompilerParams(vmem_limit_bytes=VLIMIT),
        name="update",
    )(stat, *own, *flat_weights, *passed)


def local(
    n,
    residual,
    cotangent,
    memory,
    segment_ids,
    plot_ids,
    attend_weight,
    attend_first,
    attend_second,
    recall_weight,
    recall_first,
    recall_second,
    outward_weight,
    outward_first,
    outward_second,
    expand_weight,
    expand_first,
    expand_second,
    narrow_weight,
    narrow_first,
    narrow_second,
    gain_weight,
    gain_first,
    gain_second,
):
    _, plots, patches, width_d = memory.shape
    shard = attend_weight.shape[1]
    aligned = shard % 16 == 0
    length = segment_ids.shape[1]

    def by_rows(w):
        return jnp.transpose(w, (1, 0, 2)).reshape(w.shape[1], -1)

    out_rows = jnp.transpose(outward_weight, (2, 0, 1))
    sa = jnp.concatenate([by_rows(attend_weight[0:3]), out_rows[:, 0]], axis=1).astype(BF)
    sb = jnp.concatenate([by_rows(recall_weight), attend_weight[3], out_rows[:, 1]], axis=1).astype(BF)
    sc = by_rows(expand_weight).astype(BF)
    sd = narrow_weight.T.astype(BF)
    if not aligned:
        sa, sb, sc, sd = (
            lax.all_gather(s, "dp", axis=0, tiled=True).reshape(8, width_d // 8, s.shape[1]) for s in (sa, sb, sc, sd)
        )
    mem = memory.reshape(plots * patches, width_d)
    x0 = residual[0]
    plot_row = plot_ids.reshape(-1)
    outs = call_first(
        n, aligned, plot_row, x0, cotangent[0], gain_weight, segment_ids, sa, sb, sc, sd, mem
    )
    lse, qct, c, ct, lse_c, qkv, qkvt, a, att, x1, ga, gb, gc, wn, h0, h1, e3, kv, kvt, wo1, wa3 = outs
    dgain2, f, g2, e2, du, x2 = call_ffn(n, c, x1, gain_weight, wo1, gc, wn, e3)
    outs = call_cross_backward(n, aligned, plot_row, segment_ids, e2, gb, qct, kv, kvt, ct, lse_c, f, x2, wn, du)
    dqc, dk, dv, block_out = outs[0:4]
    own_u = outs[4] if aligned else du[0 : width_d // n].astype(F32)
    outs = call_self_backward(
        n, aligned, plots, x0, x1, g2, gain_weight, dgain2, segment_ids, dqc, dk, dv, own_u,
        e2, h1, h0, mem, ga, gb, c, a, qkv, qkvt, att, lse, wa3
    )
    residual_grad, memory_grad, stat = outs[0:3]
    if aligned:
        own = (own_u,) + tuple(outs[3:6])
    else:
        own = tuple(
            lax.psum_scatter(g.reshape(width_d, -1).astype(F32), "dp", scatter_dimension=0, tiled=True)
            for g in (du,) + tuple(outs[3:6])
        )
        squares = sum(jnp.sum(g * g) for g in own)
        stat = lax.psum(stat.at[3, :].set(squares), ("dp", "tensor"))
    weights = (
        (attend_weight, attend_first, attend_second),
        (recall_weight, recall_first, recall_second),
        (outward_weight, outward_first, outward_second),
        (expand_weight, expand_first, expand_second),
        (narrow_weight.T, narrow_first.T, narrow_second.T),
        (gain_weight, gain_first, gain_second),
    )
    new = call_update(stat, own, weights, (block_out, residual_grad, memory_grad))
    narrow_new = tuple(v.T for v in new[17:21])
    return (
        (new[24][None], new[25][None], new[26][None], new[0].reshape(())) + tuple(new[1:17]) + narrow_new + tuple(new[21:24])
    )


def solution(mesh):
    rows_in = P("dp", "tensor", None)
    inner = P(None, "dp", "tensor")
    outer = P(None, "tensor", "dp")
    narrow = P("tensor", "dp")
    in_specs = (
        (rows_in, rows_in, P("dp", None, None, None), P("dp", None), P("dp", None))
        + (inner,) * 3
        + (inner,) * 3
        + (outer,) * 3
        + (inner,) * 3
        + (narrow,) * 3
        + (P(),) * 3
    )
    out_specs = (
        (rows_in, rows_in, P("dp", None, "tensor", None), P())
        + (inner,) * 4
        + (inner,) * 4
        + (outer,) * 4
        + (inner,) * 4
        + (narrow,) * 4
        + (P(),) * 3
    )
    return jax.shard_map(
        functools.partial(local, mesh.shape["dp"]),
        mesh=mesh,
        in_specs=in_specs,
        out_specs=out_specs,
        check_vma=False,
    )
```

```python
import functools

import jax
import jax.numpy as jnp
from jax import lax
from jax.experimental import pallas as pl
from jax.experimental.pallas import tpu as pltpu
from jax.sharding import PartitionSpec as P

HEAD = 64
SEGS = 4
STEP = 10
NORM_EPS = 1e-06
ADAM_EPS = 1e-08
BETA_ONE = 0.9
BETA_TWO = 0.999
DECAY = 0.1
RATE_INNER = 0.05
RATE_OUTER = 0.4
RATE_GAIN = 0.5
CLIP = 1.0
MASKED = -1e30
SCALE = HEAD ** (-0.5)

MESH = pl.DeviceIdType.MESH
BF = jnp.bfloat16
F32 = jnp.float32
VLIMIT = 62 * 2**20
VM = pl.BlockSpec(memory_space=pltpu.VMEM)
ANY = pl.BlockSpec(memory_space=pl.ANY)
SM = pl.BlockSpec(memory_space=pltpu.SMEM)
DMA = pltpu.SemaphoreType.DMA


def sds(shape, dtype):
    return jax.ShapeDtypeStruct(shape, dtype)


def nn(a, b):
    return lax.dot_general(a, b, (((1,), (0,)), ((), ())), preferred_element_type=F32)


def nt(a, b):
    return lax.dot_general(a, b, (((1,), (1,)), ((), ())), preferred_element_type=F32)


def rows(i, size):
    return pl.ds(pl.multiple_of(i * size, size), size)


def flat(ref):
    return ref[...].reshape(ref.shape[0] * ref.shape[1], ref.shape[2])


def norm(v, g):
    return v * lax.rsqrt(jnp.mean(v * v, axis=-1, keepdims=True) + NORM_EPS) * g


def norm_back(v, g, dy):
    r = lax.rsqrt(jnp.mean(v * v, axis=-1, keepdims=True) + NORM_EPS)
    n = v * r
    dn = dy * g
    dv = r * (dn - n * jnp.mean(dn * n, axis=-1, keepdims=True))
    return dv, jnp.sum(dy * n, axis=0, keepdims=True)


class Place:
    def __init__(self, n):
        self.n = n
        self.d = lax.axis_index("dp")
        self.t = lax.axis_index("tensor")
        self.tc = self.t + 1 - 2 * lax.rem(self.t, 2)
        self.ty = lax.rem(self.t + 2, 4)
        self.tcy = lax.rem(self.tc + 2, 4)
        self.core = (self.d, self.tc)
        self.y = (self.d, self.ty)
        self.dx = self.d + 1 - 2 * lax.rem(self.d, 2)
        self.x = (self.dx, self.t)

    def z(self, k):
        return (lax.rem(self.d + 2 * k, self.n), self.t)

    def from_z(self, k):
        return lax.rem(self.d - 2 * k + 2 * self.n, self.n)

    def x_from_z(self, k):
        return lax.rem(self.dx - 2 * k + 2 * self.n, self.n)


def greet(devices):
    bar = pltpu.get_barrier_semaphore()
    for dev in devices:
        pl.semaphore_signal(bar, inc=1, device_id=dev, device_id_type=MESH)
    pl.semaphore_wait(bar, len(devices))


class Puts:
    def __init__(self, sems):
        self.sems = sems
        self.all = []

    def __call__(self, src, dst):
        c = pltpu.make_async_copy(src, dst, self.sems.at[len(self.all)])
        c.start()
        self.all.append(c)

    def end(self):
        for c in self.all:
            c.wait()


def rcopy(src, dst, ss, rs, dev):
    return pltpu.make_async_remote_copy(
        src_ref=src, dst_ref=dst, send_sem=ss, recv_sem=rs, device_id=dev, device_id_type=MESH
    )


class TensorSum:
    def __init__(self, place, refs):
        self.p = place
        self.s0, self.s1, self.r0, self.r1, self.own, self.ys, self.yr, self.ss, self.rs = refs

    @staticmethod
    def scratch(tile, width, hop=F32):
        return [pltpu.VMEM((tile, width), hop)] * 4 + [
            pltpu.VMEM((tile, width), F32),
            pltpu.VMEM((tile, width), BF),
            pltpu.VMEM((tile, width), BF),
            DMA((3,)),
            DMA((3,)),
        ]

    def begin(self, tile_fn):
        self.send(tile_fn)
        self.pass_on(tile_fn)

    def send(self, tile_fn):
        p = self.p
        self.c0 = rcopy(self.s0, self.r0, self.ss.at[0], self.rs.at[0], p.core)
        self.c1 = rcopy(self.s1, self.r1, self.ss.at[1], self.rs.at[1], p.core)
        self.cy = rcopy(self.ys, self.yr, self.ss.at[2], self.rs.at[2], p.y)
        self.s0[...] = tile_fn(p.tcy).astype(self.s0.dtype)
        self.c0.start()
        self.s1[...] = tile_fn(p.tc).astype(self.s1.dtype)
        self.c1.start()

    def pass_on(self, tile_fn):
        p = self.p
        part = tile_fn(p.ty)
        self.c0.wait_recv()
        self.ys[...] = (part + self.r0[...].astype(F32)).astype(BF)
        self.cy.start()
        self.own[...] = tile_fn(p.t)

    def end(self):
        self.c1.wait_recv()
        self.cy.wait_recv()
        total = self.own[...] + self.r1[...].astype(F32) + self.yr[...].astype(F32)
        self.c0.wait_send()
        self.c1.wait_send()
        self.cy.wait_send()
        return total


class TensorGather:
    def __init__(self, place, full, sems):
        self.p = p = place
        self.full = full
        ss, rs = sems
        mine, far, near, cross = (full.at[i] for i in (p.t, p.ty, p.tc, p.tcy))
        self.cc = rcopy(mine, mine, ss.at[0], rs.at[0], p.core)
        self.cy = rcopy(mine, mine, ss.at[1], rs.at[1], p.y)
        self.cf = rcopy(far, far, ss.at[2], rs.at[2], p.core)
        self.wc = rcopy(near, near, ss.at[0], rs.at[0], p.core)
        self.wy = rcopy(far, far, ss.at[1], rs.at[1], p.y)
        self.wf = rcopy(cross, cross, ss.at[2], rs.at[2], p.core)

    @staticmethod
    def scratch():
        return [DMA((3,)), DMA((3,))]

    def begin(self, own):
        self.full[self.p.t] = own
        self.cy.start()
        self.cc.start()

    def forward(self):
        self.wy.wait_recv()
        self.cf.start()

    def end(self):
        self.wc.wait_recv()
        self.wf.wait_recv()
        self.cy.wait_send()
        self.cc.wait_send()
        self.cf.wait_send()


class TileSwap:
    def __init__(self, place, full, sems, tile):
        self.p = p = place
        ss, rs = sems
        mine = full.at[rows(p.t, tile)]
        far = full.at[rows(p.ty, tile)]
        self.out = rcopy(mine, mine, ss.at[0], rs.at[0], p.y)
        self.back = rcopy(far, far, ss.at[0], rs.at[0], p.y)

    @staticmethod
    def scratch():
        return [DMA((1,)), DMA((1,))]

    def begin(self):
        self.out.start()

    def end(self):
        self.back.wait_recv()
        self.out.wait_send()


class CoreShare:
    def __init__(self, place, full, sems, tile):
        self.p = p = place
        ss, rs = sems
        self.out = [rcopy(full.at[rows(i, tile)], full.at[rows(i, tile)], ss.at[k], rs.at[k], p.core)
                    for k, i in enumerate((p.t, p.ty))]
        self.back = [rcopy(full.at[rows(i, tile)], full.at[rows(i, tile)], ss.at[k], rs.at[k], p.core)
                     for k, i in enumerate((p.tc, p.tcy))]

    @staticmethod
    def scratch():
        return [DMA((2,)), DMA((2,))]

    def begin(self, k):
        self.out[k].start()

    def arrive(self, k):
        self.back[k].wait_recv()

    def sent(self):
        for c in self.out:
            c.wait_send()

    def end(self):
        self.arrive(0)
        self.arrive(1)
        self.sent()


class HeadExchange:
    def __init__(self, place, own, got, sems, tile):
        self.p = p = place
        self.own, self.got, self.tile = own, got, tile
        ss, rs = sems
        peers = ((p.core, (p.tc, p.tcy), p.tc), (p.y, (p.ty, p.t), p.ty), ((p.d, p.tcy), (p.tcy, p.tc), p.tcy))
        self.out = [[rcopy(own.at[rows(tiles[k], tile)], got.at[p.t, k], ss.at[i, k], rs.at[i, k], dev) for k in (0, 1)]
                    for i, (dev, tiles, _) in enumerate(peers)]
        self.back = [[rcopy(got.at[src, k], got.at[src, k], ss.at[i, k], rs.at[i, k], dev) for k in (0, 1)]
                     for i, (dev, _, src) in enumerate(peers)]

    @staticmethod
    def scratch(tile, width):
        return [pltpu.VMEM((4, 2, tile, width), BF), DMA((3, 2)), DMA((3, 2))]

    def begin(self):
        for k in (0, 1):
            for i in (1, 2, 0):
                self.out[i][k].start()
        self.got[self.p.t, 0] = self.own[rows(self.p.t, self.tile), :]
        self.got[self.p.t, 1] = self.own[rows(self.p.ty, self.tile), :]

    def arrive(self, k):
        for i in (0, 1, 2):
            self.back[i][k].wait_recv()

    def sent(self):
        for group in self.out:
            for c in group:
                c.wait_send()

    def project(self, k, weights):
        total = nt(self.got[0, k], weights[0])
        for s in range(1, 4):
            total = total + nt(self.got[s, k], weights[s])
        return total


class ChipSum:
    def __init__(self, place, refs):
        self.p = p = place
        self.s, self.r, self.ys, self.yr, self.ss, self.rs = refs
        self.core = [rcopy(self.s.at[k], self.r.at[k], self.ss.at[k], self.rs.at[k], p.core) for k in (0, 1)]
        self.y = [rcopy(self.ys.at[k], self.yr.at[1 - k], self.ss.at[2 + k], self.rs.at[3 - k], p.y) for k in (0, 1)]
        self.yback = [rcopy(self.ys.at[k], self.yr.at[k], self.ss.at[2 + k], self.rs.at[2 + k], p.y) for k in (0, 1)]

    @staticmethod
    def scratch(tile, width, hop=F32):
        return [pltpu.VMEM((2, tile, width), hop)] * 2 + [pltpu.VMEM((2, tile, width), BF)] * 2 + [DMA((4,)), DMA((4,))]

    def send(self, k, tile_fn):
        self.s[k] = tile_fn((self.p.tc, self.p.tcy)[k]).astype(self.s.dtype)
        self.core[k].start()

    def pass_on(self, k, tile_fn):
        part = tile_fn((self.p.t, self.p.ty)[k])
        self.core[k].wait_recv()
        self.ys[k] = (part + self.r[k].astype(F32)).astype(BF)
        self.y[k].start()

    def end(self, k):
        self.yback[k].wait_recv()
        return self.ys[k].astype(F32) + self.yr[k].astype(F32)

    def sent(self):
        for c in self.core + self.y:
            c.wait_send()


class RowGather:
    def __init__(self, place, full, sems):
        self.p = place
        self.full = full
        self.zs, self.zr, self.xs, self.xr = sems
        self.steps = place.n // 2

    @staticmethod
    def scratch(n):
        return [DMA((n // 2,))] * 4

    def zcopy(self, k, slot):
        return rcopy(self.full.at[slot], self.full.at[slot], self.zs.at[k], self.zr.at[k], self.p.z(k))

    def xcopy(self, k, slot):
        return rcopy(self.full.at[slot], self.full.at[slot], self.xs.at[k], self.xr.at[k], self.p.x)

    def begin_far(self):
        for k in range(1, self.steps):
            self.zcopy(k, self.p.d).start()

    def begin_near(self):
        self.xcopy(0, self.p.d).start()

    def sent(self):
        for k in range(1, self.steps):
            self.zcopy(k, self.p.d).wait_send()

    def forward(self, k):
        slot = self.p.from_z(k)
        self.zcopy(k, slot).wait_recv()
        self.xcopy(k, slot).start()

    def forward_all(self):
        for k in range(1, self.steps):
            self.forward(k)

    def end(self):
        for k in range(self.steps):
            self.xcopy(k, self.p.x_from_z(k)).wait_recv()
            self.xcopy(k, self.p.from_z(k)).wait_send()


def head_rows(qt, head):
    ids = lax.broadcasted_iota(jnp.int32, qt.shape, 0)
    return jnp.where((ids >= head * HEAD) & (ids < (head + 1) * HEAD), qt, 0.0).astype(BF)


def head_block(x, heads):
    ids = lax.broadcasted_iota(jnp.int32, x.shape, 1)
    return jnp.concatenate(
        [jnp.where((ids >= h * HEAD) & (ids < (h + 1) * HEAD), x, 0.0).astype(BF) for h in range(heads)], axis=0
    )


def segment_starts(seg):
    start = jnp.zeros(seg.shape, jnp.int32)
    for s in range(SEGS - 1):
        count = jnp.sum(jnp.where(seg == s, 1, 0), axis=1, keepdims=True)
        start = start + jnp.where(seg > s, count, 0)
    return start


def causal_mask(keys, tile, tau, start):
    key_place = lax.broadcasted_iota(jnp.int32, (keys, tile), 0)
    query_place = lax.broadcasted_iota(jnp.int32, (keys, tile), 1) + tau * tile
    return (key_place <= query_place) & (key_place >= start)


def plot_order(seg, plot_ref):
    counts = [jnp.sum(jnp.where(seg == s, 1, 0), axis=1, keepdims=True) for s in range(SEGS)]
    place = lax.broadcasted_iota(jnp.int32, seg.shape, 1)
    first = jnp.zeros((1, 1), jnp.int32)
    for s in range(SEGS):
        shift = jnp.zeros((1, 1), jnp.int32)
        for o in range(SEGS):
            if o != s:
                ahead = plot_ref[o] < plot_ref[s] if o > s else plot_ref[o] <= plot_ref[s]
                shift = shift + counts[o] * (ahead.astype(jnp.int32) - (1 if o < s else 0))
        place = place + jnp.where(seg == s, shift, 0)
        first = first + counts[s] * (plot_ref[s] == 0).astype(jnp.int32)
    return place, first


def order_tile(place, i, tile):
    spot = lax.broadcasted_iota(jnp.int32, (tile, place.shape[1]), 0) + i * tile
    return jnp.where(place == spot, 1.0, 0.0).astype(BF)


class Slots:
    tile = 256

    def __init__(self, place, first):
        self.place = place
        self.split = jnp.sum(first)
        self.zero_tiles = lax.div(self.split + (self.tile - 1), self.tile)
        self.shared = self.zero_tiles - lax.div(self.split, self.tile)
        self.count = place.shape[1] // self.tile + 1

    def at(self, s):
        plot = (s >= self.zero_tiles).astype(jnp.int32)
        i = s - plot * self.shared
        spot = lax.broadcasted_iota(jnp.int32, (1, self.tile), 1) + i * self.tile
        side = (spot >= self.split).astype(jnp.int32)
        counts = (side == plot) & (spot < self.place.shape[1])
        return plot, order_tile(self.place, i, self.tile), counts


def first_kernel(n, gather, heads, plot_ref, x0_ref, cot_ref, gain_ref, seg_ref, *more):
    more = list(more)
    weights = [more.pop(0) for _ in range(5)]
    (m_hbm, lse_ref, qct_ref, c_ref, ct_ref, lsec_ref, qkv_out, qkvt_out, a_out, at_out, x1_out, ga_out,
     gr_out, gb_out, gc_out, gd_out, h0_out, h1_out, e3_out, kk_out, vv_out, kt_out, wo1_out, wa3_out, qkv_ref, qkvt_ref, a_ref, at_ref, x1_ref,
     ga, gr, gb, gc, gd, h0, h1, e3, kk, vv, kt, wo0, wo1, wa3, xf, m_ref, vte, ctok, score, raised, lsem, osem), rest = more[:51], more[51:]

    def take(count):
        got = rest[:count]
        del rest[:count]
        return got

    p = Place(n)
    tile = x0_ref.shape[0]
    width = heads * HEAD
    tiles = h0.shape[0] // tile
    load_m = pltpu.make_async_copy(m_hbm, m_ref, lsem.at[0])
    load_m.start()
    swaps = [TileSwap(p, full, take(2), tile) for full in (xf, e3)]
    shares = [CoreShare(p, full, take(2), tile) for full in (h0, e3, h1)]
    spreads = [TensorGather(p, full, take(2)) for full in (wo0, wo1, wa3)]
    heads_in, hs, hr = take(3)
    exchange = HeadExchange(p, a_ref, heads_in, (hs, hr), tile)
    xf[rows(p.t, tile), :] = x0_ref[...]
    e3[rows(p.t, tile), :] = cot_ref[...]
    if gather:
        parts = [RowGather(p, full, take(4)) for full in (ga, gr, gb, gc, gd)]
        part_a, part_r, part_b, part_c, part_d = parts
        aw, rw, ow, ew, nw = weights

        def fill(full, *mats):
            full[p.d] = jnp.concatenate(mats, axis=1).astype(BF)

        fill(ga, aw[0], aw[1], aw[2], ow[0].T)
        greet([p.core, p.y, (p.d, p.tcy), p.x] + [p.z(k) for k in range(1, n // 2)])
        swaps[0].begin()
        part_a.begin_near()
        part_a.begin_far()
        fill(gr, rw[0], rw[1])
        fill(gb, aw[3], ow[1].T)
        fill(gc, ew[0], ew[1])
        gd[p.d] = nw[...].astype(BF)
    else:
        copies = [pltpu.make_async_copy(s, f, lsem.at[1 + i]) for i, (s, f) in
                  enumerate(zip(weights, (ga, gr, gb, gc, gd)))]
        for c in copies:
            c.start()
        greet([p.core, p.y, (p.d, p.tcy)])
        swaps[0].begin()

    def normed(v, i):
        return norm(v, gain_ref[i : i + 1, :]).astype(BF)

    def pair(k):
        return rows((p.t, p.ty)[k], tile)

    h0[pair(0), :] = normed(x0_ref[...].astype(F32), 0)
    shares[0].begin(0)
    start = segment_starts(seg_ref[...])
    states = kk.shape[0]
    ext = HEAD + 16
    for h in range(heads):
        vte[h * ext + HEAD : (h + 1) * ext, :] = jnp.ones((16, states), BF)
    ctok[...] = jnp.zeros(ctok.shape, F32)
    lsec_ref[...] = jnp.zeros(lsec_ref.shape, F32)
    swaps[0].end()
    swaps[1].begin()
    h0[pair(1), :] = normed(xf[pair(1), :].astype(F32), 0)
    shares[0].begin(1)
    if gather:
        part_a.forward_all()
        part_r.begin_near()
        part_r.begin_far()
        part_b.begin_far()
    shares[0].end()
    if gather:
        part_a.end()
    else:
        for c in copies:
            c.wait()
    spreads[0].begin(flat(ga)[:, 3 * width : 4 * width])

    wa = flat(ga)
    for i in range(tiles):
        at = slice(i * tile, (i + 1) * tile)
        x = nn(h0[at, :], wa[:, : 3 * width])
        qkv_ref[at, :] = x.astype(BF)
        qkvt_ref[:, at] = x.T.astype(BF)
    put = Puts(osem)
    put(ga, ga_out)
    put(h0, h0_out)
    put(qkv_ref, qkv_out)
    put(qkvt_ref, qkvt_out)
    swaps[1].end()
    shares[1].begin(0)
    shares[1].begin(1)
    if gather:
        part_c.begin_far()

    for i in range(tiles):
        at = slice(i * tile, (i + 1) * tile)
        keys = (i + 1) * tile
        own_keys = qkv_ref[0:keys, width : 2 * width]
        qt = qkvt_ref[0:width, at].astype(F32) * SCALE
        allowed = causal_mask(keys, tile, i, start[:, at])
        for h in range(heads):
            s = jnp.where(allowed, nn(own_keys, head_rows(qt, h)), MASKED)
            peak = jnp.max(s, axis=0, keepdims=True)
            e = jnp.exp(s - peak)
            total = jnp.sum(e, axis=0, keepdims=True)
            w = (e * (1.0 / total)).astype(BF)
            vt = qkvt_ref[2 * width + h * HEAD : 2 * width + (h + 1) * HEAD, 0:keys]
            at_ref[h * HEAD : (h + 1) * HEAD, at] = nn(vt, w)
            lse_ref[h : h + 1, at] = peak + jnp.log(total)
        a_ref[at, :] = at_ref[:, at].T.astype(BF)
        if i == 1:
            spreads[0].forward()
        if gather and i < 3:
            part_r.forward(i + 1)
    exchange.begin()
    put(a_ref, a_out)
    put(at_ref, at_out)
    if gather:
        for k in range(4, n // 2):
            part_r.forward(k)
        part_b.begin_near()
        part_b.forward_all()
    shares[1].end()
    put(e3, e3_out)
    spreads[0].end()
    if gather:
        part_c.begin_near()
        part_r.end()
        part_d.begin_far()
    put(gr, gr_out)
    load_m.wait()
    mtiles = m_ref.shape[0] // 256

    def project_memory(i, carry):
        at = rows(i, 256)
        x = nn(m_ref[at, :], flat(gr))
        kk[at, :] = x[:, 0:width].astype(BF)
        vv[at, :] = x[:, width : 2 * width].astype(BF)
        xt = x.T.astype(BF)
        kt[:, at] = xt[0:width]
        for h in range(heads):
            vte[h * ext : h * ext + HEAD, at] = xt[width + h * HEAD : width + (h + 1) * HEAD]
        return carry

    lax.fori_loop(0, mtiles, project_memory, 0)
    put(kk, kk_out)
    put(vv, vv_out)
    put(kt, kt_out)
    for k in (0, 1):
        exchange.arrive(k)
        if gather:
            part_c.forward(k + 1)
        x1 = xf[pair(k), :].astype(F32) + exchange.project(k, wo0)
        x1_ref[k] = x1
        h1[pair(k), :] = normed(x1, 1)
        shares[2].begin(k)
    put(x1_ref, x1_out)
    if gather:
        for k in range(3, n // 2):
            part_c.forward(k)
        part_d.begin_near()
    if gather:
        part_b.end()
    put(gb, gb_out)
    spreads[1].begin(flat(gb)[:, width : 2 * width])
    spreads[2].begin(flat(gb)[:, 0:width])
    shares[2].end()
    put(h1, h1_out)
    wq = flat(gb)[:, 0:width]
    for i in range(tiles):
        at = slice(i * tile, (i + 1) * tile)
        qct_ref[:, at] = nn(h1[at, :], wq).T.astype(BF)

    patches = states // 2
    slots = Slots(*plot_order(seg_ref[...], plot_ref))

    def one_slot(s, carry):
        plot, order, counts = slots.at(s)
        qt = nt(qct_ref[...], order) * SCALE
        q = [head_rows(qt, h) for h in range(heads)]

        def scores(h, c, peak):
            near, far = slice(c * 256, (c + 1) * 256), slice(patches + c * 256, patches + (c + 1) * 256)
            x = nn(jnp.where(plot == 0, kk[near, :], kk[far, :]), q[h])
            score[h % 2, near] = x
            top = jnp.max(x, axis=0, keepdims=True)
            return top if peak is None else jnp.maximum(peak, top)

        chunks = patches // 256
        peak = None
        for c in range(chunks):
            peak = scores(0, c, peak)
        for h in range(heads):
            ahead = None
            for c in range(chunks):
                if h + 1 < heads:
                    ahead = scores(h + 1, c, ahead)
                near = slice(c * 256, (c + 1) * 256)
                raised[h % 2, near] = jnp.exp(score[h % 2, near] - peak).astype(BF)
            hs = slice(h * ext, (h + 1) * ext)
            acc = nn(jnp.where(plot == 0, vte[hs, 0:patches], vte[hs, patches:states]), raised[h % 2])
            total = acc[HEAD : HEAD + 1, :]
            ct_ref[s, h * HEAD : (h + 1) * HEAD, :] = jnp.where(counts, acc[0:HEAD, :] * (1.0 / total), 0.0)
            lsec_ref[s, h : h + 1, :] = jnp.where(counts, peak + jnp.log(total), -MASKED)
            peak = ahead
        ctok[...] += nn(ct_ref[s].astype(BF), order)
        if gather:
            for k in range(1, n // 2):
                pl.when(s == min(k - 1, slots.count - 1))(functools.partial(part_d.forward, k))
        return carry

    lax.fori_loop(0, slots.count, one_slot, 0)
    c_ref[...] = ctok[...].T.astype(BF)
    spreads[1].forward()
    spreads[2].forward()
    spreads[1].end()
    put(wo1, wo1_out)
    spreads[2].end()
    put(wa3, wa3_out)
    exchange.sent()
    if gather:
        for part in parts:
            part.sent()
        part_c.end()
        part_d.end()
    put(gc, gc_out)
    put(gd, gd_out)
    put.end()


def call_first(n, gather, plot_ids, x0, cot, gain, seg, weights, mem):
    tile, width_d = x0.shape
    length = seg.shape[1]
    states = mem.shape[0]
    if gather:
        width, hidden = weights[0].shape[2], weights[4].shape[1]
    else:
        width, hidden = weights[0].shape[2] // 4, weights[4].shape[2]
    heads = width // HEAD
    shapes = [(8, width_d // 8, w) for w in (4 * width, 2 * width, 2 * width, 2 * hidden, hidden)]
    spread = (4, width_d, width)
    early = [
        sds((length, 3 * width), BF),
        sds((3 * width, length), BF),
        sds((length, width), BF),
        sds((width, length), F32),
        sds((2, tile, width_d), F32),
    ]
    late = [
        sds(shapes[0], BF),
        sds(shapes[1], BF),
        sds(shapes[2], BF),
        sds(shapes[3], BF),
        sds(shapes[4], BF),
        sds((length, width_d), BF),
        sds((length, width_d), BF),
        sds((length, width_d), BF),
        sds((states, width), BF),
        sds((states, width), BF),
        sds((width, states), BF),
        sds(spread, BF),
        sds(spread, BF),
    ]
    out_shape = [
        sds((8, length), F32),
        sds((width, length), BF),
        sds((length, width), BF),
        sds((length // 256 + 1, width, 256), F32),
        sds((length // 256 + 1, 8, 256), F32),
    ] + early + late
    scratch = [pltpu.VMEM(s.shape, s.dtype) for s in early] + [pltpu.VMEM(s, BF) for s in shapes]
    scratch += [pltpu.VMEM((length, width_d), BF)] * 3
    scratch += [
        pltpu.VMEM((states, width), BF),
        pltpu.VMEM((states, width), BF),
        pltpu.VMEM((width, states), BF),
        pltpu.VMEM(spread, BF),
        pltpu.VMEM(spread, BF),
        pltpu.VMEM(spread, BF),
        pltpu.VMEM((length, width_d), BF),
        pltpu.VMEM((states, width_d), BF),
        pltpu.VMEM((heads * (HEAD + 16), states), BF),
        pltpu.VMEM((width, length), F32),
        pltpu.VMEM((2, states // 2, 256), F32),
        pltpu.VMEM((2, states // 2, 256), BF),
        DMA((6,)),
        DMA((len(early + late),)),
    ]
    scratch += TileSwap.scratch() * 2 + CoreShare.scratch() * 3 + TensorGather.scratch() * 3
    scratch += HeadExchange.scratch(tile, width)
    if gather:
        scratch += RowGather.scratch(n) * 5
    shard = VM if gather else ANY
    return pl.pallas_call(
        functools.partial(first_kernel, n, gather, heads),
        out_shape=out_shape,
        in_specs=[SM, VM, VM, VM, VM] + [shard] * len(weights) + [ANY],
        out_specs=[VM] * 5 + [ANY] * len(early + late),
        scratch_shapes=scratch,
        compiler_params=pltpu.CompilerParams(collective_id=1, has_side_effects=True, vmem_limit_bytes=VLIMIT),
        name="attention_forward",
    )(plot_ids, x0, cot, gain, seg, *weights, mem)


def ffn_kernel(n, c_ref, gain_ref, x1_hbm, wo_hbm, gc_hbm, wn_hbm, e3_hbm,
               dgain_ref, f_out, g2_out, e2_out, du_out, x2_out,
               x1, wo, gc, wn, e3, f, g2, e2, du, x2, h2, dg, h2t, e3t, lsem, osem, *rest):
    rest = list(rest)

    def take(count):
        got = rest[:count]
        del rest[:count]
        return got

    p = Place(n)
    _, tile, width_d = x1.shape
    hidden = f.shape[1]
    heads_in, hs, hr = take(3)
    exchange = HeadExchange(p, c_ref, heads_in, (hs, hr), tile)
    shares = [CoreShare(p, full, take(2), tile) for full in (h2, e2)]
    total = ChipSum(p, take(6))
    put = Puts(osem)
    loads = [pltpu.make_async_copy(s, d, lsem.at[i]) for i, (s, d) in
             enumerate(((e3_hbm, e3), (wo_hbm, wo), (x1_hbm, x1), (gc_hbm, gc), (wn_hbm, wn)))]
    for load in loads:
        load.start()
    greet([p.core, p.y, (p.d, p.tcy)])
    exchange.begin()
    loads[0].wait()
    e3t[...] = e3[...].T

    def pair(k):
        return rows((p.t, p.ty)[k], tile)

    def hidden_tile(j):
        at = rows(j, tile)
        gate = nn(h2[at, :], flat(gc)[:, 0:hidden])
        up = nn(h2[at, :], flat(gc)[:, hidden : 2 * hidden])
        df = nn(e3[at, :], flat(wn))
        sq = gate * gate
        th = jnp.tanh(0.7978845608 * gate * (1.0 + 0.044715 * sq))
        half = 0.5 * (1.0 + th)
        act = gate * half
        slope = half + 0.5 * gate * (1.0 - th * th) * (0.7978845608 * (1.0 + 3.0 * 0.044715 * sq))
        f[at, :] = (act * up).astype(BF)
        dg[at, 0:hidden] = (df * up * slope).astype(BF)
        dg[at, hidden : 2 * hidden] = (df * act).astype(BF)

    def back_tile(j):
        return nt(dg[rows(j, tile), :], flat(gc)[:, 0 : 2 * hidden])

    for load in loads[1:]:
        load.wait()
    for k in (0, 1):
        exchange.arrive(k)
        x2[k] = x1[k] + exchange.project(k, wo)
        h2[pair(k), :] = norm(x2[k], gain_ref[2:3, :]).astype(BF)
        shares[0].begin(k)
    put(x2, x2_out)
    for k in (0, 1):
        hidden_tile((p.t, p.ty)[k])
        shares[0].arrive(k)
        hidden_tile((p.tc, p.tcy)[k])
        total.send(k, back_tile)
        if k == 1:
            total.pass_on(0, back_tile)
    total.pass_on(1, back_tile)
    put(f, f_out)
    h2t[...] = h2[...].T
    for i in range(2 * hidden // 256):
        cs = slice(i * 256, (i + 1) * 256)
        du[:, cs] = nn(h2t[...], dg[:, cs]).astype(BF)
    for i in range(hidden // 256):
        cs = slice(i * 256, (i + 1) * 256)
        du[:, 2 * hidden + i * 256 : 2 * hidden + (i + 1) * 256] = nn(e3t[...], f[:, cs]).astype(BF)
    put(du, du_out)
    for k in (0, 1):
        dv, dgain = norm_back(x2[k], gain_ref[2:3, :], total.end(k))
        if k == 0:
            dgain_ref[...] = dgain
        g2[k] = e3[pair(k), :].astype(F32) + dv
        e2[pair(k), :] = g2[k].astype(BF)
        shares[1].begin(k)
    put(g2, g2_out)
    shares[0].sent()
    exchange.sent()
    total.sent()
    shares[1].end()
    put(e2, e2_out)
    put.end()


def call_ffn(n, c, x1, gain, wo, gc, wn, e3):
    _, tile, width_d = x1.shape
    length, width = c.shape
    hidden = gc.shape[2] // 2
    late = [
        sds((length, hidden), BF),
        sds((2, tile, width_d), F32),
        sds((length, width_d), BF),
        sds((width_d, 3 * hidden), BF),
        sds((2, tile, width_d), F32),
    ]
    scratch = [pltpu.VMEM(v.shape, v.dtype) for v in [x1, wo, gc, wn, e3] + late]
    scratch += [
        pltpu.VMEM((length, width_d), BF),
        pltpu.VMEM((length, 2 * hidden), BF),
        pltpu.VMEM((width_d, length), BF),
        pltpu.VMEM((width_d, length), BF),
        DMA((5,)),
        DMA((len(late),)),
    ]
    scratch += HeadExchange.scratch(tile, width) + CoreShare.scratch() * 2 + ChipSum.scratch(tile, width_d)
    return pl.pallas_call(
        functools.partial(ffn_kernel, n),
        out_shape=[sds((1, width_d), F32)] + late,
        in_specs=[VM] * 2 + [ANY] * 5,
        out_specs=[VM] + [ANY] * len(late),
        scratch_shapes=scratch,
        compiler_params=pltpu.CompilerParams(collective_id=2, has_side_effects=True, vmem_limit_bytes=VLIMIT),
        name="ffn",
    )(c, gain, x1, wo, gc, wn, e3)


def cross_backward_kernel(n, reduce, heads, plot_ref, seg_ref, qct_ref, ct_ref, lse_ref, e2_hbm, gb_hbm, kk_hbm, vv_hbm, kt_hbm,
                          f_hbm, x2_hbm, wn_hbm, du_hbm, dqc_ref, dk_ref, dv_ref, blk_ref, *rest):
    rest = list(rest)

    def take(count):
        got = rest[:count]
        del rest[:count]
        return got

    p = Place(n)
    width = heads * HEAD
    states = kk_hbm.shape[0]
    patches = states // 2
    length = qct_ref.shape[1]
    hidden = f_hbm.shape[1]
    if reduce:
        du_out, mine_u = take(2)
        rest_u = RowSum(p, mine_u, take(6))
    dka, dva, dct_all, dqtok, e2, gb, kk, vv, kt, f, x2, wn, lsem = take(13)
    tile = x2.shape[0]
    block = TensorSum(p, take(9))
    pairs = [(f_hbm, f), (wn_hbm, wn), (e2_hbm, e2), (gb_hbm, gb), (kk_hbm, kk), (vv_hbm, vv),
             (kt_hbm, kt), (x2_hbm.at[0], x2)]
    if reduce:
        pairs.insert(0, (du_hbm, mine_u))
    loads = [pltpu.make_async_copy(s, d, lsem.at[i]) for i, (s, d) in enumerate(pairs)]
    for load in loads:
        load.start()
    greet([p.core, p.y] + ([p.x] + [p.z(k) for k in range(1, n // 2)] if reduce else []))
    if reduce:
        loads.pop(0).wait()
        rest_u.begin()
    loads[0].wait()
    loads[1].wait()

    def out_tile(j):
        return nt(f[rows(j, tile), :], flat(wn))

    block.send(out_tile)
    for load in loads[2:]:
        load.wait()
    dka[...] = jnp.zeros(dka.shape, F32)
    dva[...] = jnp.zeros(dva.shape, F32)
    dqtok[...] = jnp.zeros(dqtok.shape, F32)
    wo = flat(gb)[:, width : 2 * width]
    for i in range(length // 256):
        at = slice(i * 256, (i + 1) * 256)
        dct_all[:, at] = nn(e2[at, :], wo).T.astype(BF)
    block.pass_on(out_tile)
    if reduce:
        rest_u.step(1)
    slots = Slots(*plot_order(seg_ref[...], plot_ref))

    def one_slot(s, carry):
        plot, order, _ = slots.at(s)
        dct = nt(dct_all[...], order)
        qt = nt(qct_ref[...], order) * SCALE
        keys = jnp.where(plot == 0, kk[0:patches, :], kk[patches:states, :])
        values = jnp.where(plot == 0, vv[0:patches, :], vv[patches:states, :])
        ps, ds, dq = [], [], []
        for h in range(heads):
            hs = slice(h * HEAD, (h + 1) * HEAD)
            inner = jnp.sum(dct[hs, :] * ct_ref[s, hs, :], axis=0, keepdims=True)
            prob = jnp.exp(nn(keys, head_rows(qt, h)) - lse_ref[s, h : h + 1, :])
            grad = (prob * (nn(values, head_rows(dct, h)) - inner)).astype(BF)
            ps.append(prob.astype(BF))
            ds.append(grad)
            dq.append(nn(jnp.where(plot == 0, kt[hs, 0:patches], kt[hs, patches:states]), grad))
        dqtok[...] += nn((jnp.concatenate(dq, axis=0) * SCALE).astype(BF), order)
        dv = nn(jnp.concatenate(ps, axis=1), head_block(dct.T, heads))
        dk = nn(jnp.concatenate(ds, axis=1), head_block(qt.T, heads))
        for j in range(2):
            part = slice(j * patches, (j + 1) * patches)
            dva[part, :] += jnp.where(plot == j, dv, 0.0)
            dka[part, :] += jnp.where(plot == j, dk, 0.0)
        if reduce:
            for k in range(1, n // 2):
                if k > 1:
                    pl.when(s == min(k - 2, slots.count - 1))(functools.partial(rest_u.step, k))
        return carry

    lax.fori_loop(0, slots.count, one_slot, 0)
    dqc_ref[...] = dqtok[...].T.astype(BF)
    dk_ref[...] = dka[...].astype(BF)
    dv_ref[...] = dva[...].astype(BF)
    blk_ref[...] = (x2[...] + block.end()).astype(BF)
    if reduce:
        du_out[...] = rest_u.end()
        rest_u.sent()


def call_cross_backward(n, reduce, plot_ids, seg, e2, gb, qct, kk, vv, kt, ct, lse, f, x2, wn, du):
    width, length = qct.shape
    states = kk.shape[0]
    _, tile, width_d = x2.shape
    out_shape = [
        sds((length, width), BF),
        sds((states, width), BF),
        sds((states, width), BF),
        sds((tile, width_d), BF),
    ]
    scratch = []
    if reduce:
        shard = width_d // n
        out_shape.append(sds((shard, du.shape[1]), F32))
        scratch += [pltpu.VMEM((n, shard, du.shape[1]), BF)] + RowSum.scratch(n, shard, du.shape[1])
        du = du.reshape(n, shard, du.shape[1])
    scratch += [
        pltpu.VMEM((states, width), F32),
        pltpu.VMEM((states, width), F32),
        pltpu.VMEM((width, length), BF),
        pltpu.VMEM((width, length), F32),
        pltpu.VMEM(e2.shape, BF),
        pltpu.VMEM(gb.shape, BF),
        pltpu.VMEM((states, width), BF),
        pltpu.VMEM((states, width), BF),
        pltpu.VMEM((width, states), BF),
        pltpu.VMEM(f.shape, BF),
        pltpu.VMEM((tile, width_d), F32),
        pltpu.VMEM(wn.shape, BF),
        DMA((9,)),
    ] + TensorSum.scratch(tile, width_d, BF)
    return pl.pallas_call(
        functools.partial(cross_backward_kernel, n, reduce, width // HEAD),
        out_shape=out_shape,
        in_specs=[SM] + [VM] * 4 + [ANY] * 9,
        out_specs=[VM] * len(out_shape),
        scratch_shapes=scratch,
        compiler_params=pltpu.CompilerParams(collective_id=4, has_side_effects=True, vmem_limit_bytes=VLIMIT),
        name="cross_backward",
    )(plot_ids, seg, qct, ct, lse, e2, gb, kk, vv, kt, f, x2, wn, du)


class RowSum:
    def __init__(self, place, mine, refs):
        self.p = place
        self.mine = mine
        self.near, self.far, self.xs, self.xr, self.zs, self.zr = refs
        self.steps = place.n // 2

    @staticmethod
    def scratch(n, shard, width):
        return [pltpu.VMEM((n // 2, shard, width), BF)] * 2 + [DMA((n // 2,))] * 4

    def slot(self, k):
        return lax.rem(self.p.d + 2 * k, self.p.n)

    def xcopy(self, k):
        there = lax.rem(self.p.dx + 2 * k, self.p.n)
        return rcopy(self.mine.at[there], self.near.at[k], self.xs.at[k], self.xr.at[k], self.p.x)

    def zcopy(self, k):
        return rcopy(self.near.at[k], self.far.at[k], self.zs.at[k], self.zr.at[k], self.p.z(k))

    def begin(self):
        for k in list(range(1, self.steps)) + [0]:
            self.xcopy(k).start()

    def step(self, k):
        self.xcopy(k).wait_recv()
        self.near[k] = (self.mine[self.slot(k)].astype(F32) + self.near[k].astype(F32)).astype(BF)
        self.zcopy(k).start()

    def end(self):
        self.xcopy(0).wait_recv()
        total = self.mine[self.p.d].astype(F32) + self.near[0].astype(F32)
        for k in range(1, self.steps):
            self.zcopy(k).wait_recv()
            total = total + self.far[k].astype(F32)
        return total

    def sent(self):
        for k in range(1, self.steps):
            self.zcopy(k).wait_send()
        for k in range(self.steps):
            self.xcopy(k).wait_send()


def squares_of(x):
    return jnp.sum(jnp.sum(x * x, axis=1, keepdims=True), axis=0, keepdims=True)


def lanes(v):
    return jnp.concatenate([v[:, i * 128 : (i + 1) * 128] for i in range(v.shape[1] // 128)], axis=0)


class EveryoneSum:
    def __init__(self, place, refs):
        self.p = place
        self.bt, self.bd, self.ts, self.tr, self.ds, self.dr = refs
        n = place.n
        self.tensor_peers = [(place.d, lax.rem(place.t + k, 4)) for k in range(1, 4)]
        self.dp_peers = [(lax.rem(place.d + k, n), place.t) for k in range(1, n)]

    @staticmethod
    def scratch(n, height):
        return [pltpu.VMEM((4, height, 128), F32), pltpu.VMEM((n, height, 128), F32), DMA((4,)), DMA((4,)), DMA((n,)), DMA((n,))]

    def copies(self, buf, ss, rs, peers):
        return [rcopy(buf.at[0], buf.at[k + 1], ss.at[k + 1], rs.at[k + 1], dev) for k, dev in enumerate(peers)]

    def total(self, buf, copies, me):
        for c in copies:
            c.wait_recv()
        count = len(copies) + 1
        total = buf[lax.rem(me + count, count)]
        for j in range(1, count):
            total = total + buf[lax.rem(me - j + count, count)]
        return total

    def begin(self, mine):
        self.bt[0] = mine
        self.first = self.copies(self.bt, self.ts, self.tr, self.tensor_peers)
        for c in self.first:
            c.start()

    def pass_on(self):
        self.bd[0] = self.total(self.bt, self.first, self.p.t)
        self.second = self.copies(self.bd, self.ds, self.dr, self.dp_peers)
        for c in self.second:
            c.start()

    def end(self):
        total = self.total(self.bd, self.second, self.p.d)
        for c in self.first + self.second:
            c.wait_send()
        return total


def self_backward_kernel(n, reduce, heads, x0_ref, gain_ref, dgain2_ref, seg_ref, dqc_ref,
                         x1_hbm, g2_hbm, dk_hbm, dv_hbm, du_hbm, e2_hbm, h1_hbm, h0_hbm, m_hbm, ga_hbm, gb_hbm, c_hbm, a_hbm, qkv_hbm, qkvt_hbm,
                         at_hbm, lse_hbm, wa3_hbm, *rest):
    rest = list(rest)

    def take(count):
        got = rest[:count]
        del rest[:count]
        return got

    p = Place(n)
    tile, width_d = x0_ref.shape
    width = heads * HEAD
    if reduce:
        res_ref, mem_ref, stat_ref = take(3)
        own_outs = take(4)
        mine_r, mine_b, mine_o, mine_a = take(4)
        sums = [RowSum(p, m, take(6)) for m in (mine_r, mine_b, mine_o, mine_a)]
        rest_r, rest_b, rest_o, rest_a = sums
        early, late = EveryoneSum(p, take(6)), EveryoneSum(p, take(6))
    else:
        res_ref, mem_ref, stat_ref, mine_r, mine_b, mine_o, mine_a = take(7)
    ga, gb, c, a, qkv, qkvt, att, lse, wa3, x1, g2, dk_in, dv_in, du_own = take(14)
    ring, e1, dqkv, dka, dva, tr, lsem, rsem = take(8)
    length = e1.shape[0]
    tiles = length // tile
    pairs = [(wa3_hbm, wa3), (gb_hbm, gb), (c_hbm, c), (a_hbm, a), (qkv_hbm, qkv), (qkvt_hbm, qkvt),
             (at_hbm, att), (lse_hbm, lse), (ga_hbm, ga), (du_hbm, du_own)]
    first = [pltpu.make_async_copy(s, d, lsem.at[len(pairs) + i])
             for i, (s, d) in enumerate(((dk_hbm, dk_in), (dv_hbm, dv_in), (x1_hbm, x1), (g2_hbm, g2)))]
    loads = [pltpu.make_async_copy(s, d, lsem.at[i]) for i, (s, d) in enumerate(pairs)]
    states = dk_in.shape[0]
    wanted = [m_hbm.at[i * length : (i + 1) * length] for i in range(states // length)] + [h1_hbm, e2_hbm, h0_hbm]
    turns = [pltpu.make_async_copy(s, ring.at[i % 2], rsem.at[i % 2]) for i, s in enumerate(wanted)]
    loads[1].start()
    first[0].start()
    first[1].start()
    turns[0].start()
    loads[0].start()
    first[2].start()
    first[3].start()
    for load in loads[2:]:
        load.start()

    def turn(i):
        turns[i].wait()
        if i + 1 < len(turns):
            turns[i + 1].start()
        tr[...] = ring[i % 2].T

    heads_in, hs, hr = take(3)
    exchange = HeadExchange(p, dqc_ref, heads_in, (hs, hr), tile)
    share = CoreShare(p, e1, take(2), tile)
    last = TensorSum(p, take(9))
    ms0, ms1, mr0, mr1, myr, mss, mrs = take(7)
    if reduce:
        greet([p.x] + [p.z(k) for k in range(1, n // 2)] + late.tensor_peers + [
            (lax.rem(p.d + k, n), p.t) for k in range(1, n)
        ])
    else:
        greet([p.core, p.y, (p.d, p.tcy)])
    exchange.begin()

    def pair(k):
        return rows((p.t, p.ty)[k], tile)

    def put(mine, i, value):
        mine[:, :, i * width : (i + 1) * width] = value.astype(BF).reshape(mine.shape[0], -1, width)

    plots = mem_ref.shape[0]
    patches = states // plots
    blocks = patches // 4 // 256

    def mem_part(owner, b):
        at = pl.ds(pl.multiple_of(b // blocks * patches + owner * (patches // 4) + b % blocks * 256, 256), 256)
        return nt(dk_in[at, :], flat(gb)[:, 0:width]) + nt(dv_in[at, :], flat(gb)[:, width : 2 * width])

    total_blocks = plots * blocks
    mc0 = [rcopy(ms0.at[b], mr0.at[b], mss.at[0, b], mrs.at[0, b], p.core) for b in range(total_blocks)]
    mc1 = [rcopy(ms1.at[b], mr1.at[b], mss.at[1, b], mrs.at[1, b], p.core) for b in range(total_blocks)]
    mcy = [rcopy(ms0.at[b], myr.at[b], mss.at[2, b], mrs.at[2, b], p.y) for b in range(total_blocks)]
    loads[1].wait()
    first[0].wait()
    first[1].wait()
    for b in range(total_blocks):
        ms0[b] = mem_part(p.tcy, b).astype(BF)
        mc0[b].start()
    for b in range(total_blocks):
        ms1[b] = mem_part(p.tc, b).astype(BF)
        mc1[b].start()

    for i in range(states // length):
        part = slice(i * length, (i + 1) * length)
        turn(i)
        if i == 0:
            dka[...] = nn(tr[...], dk_in[part, :])
            dva[...] = nn(tr[...], dv_in[part, :])
        else:
            dka[...] += nn(tr[...], dk_in[part, :])
            dva[...] += nn(tr[...], dv_in[part, :])
    put(mine_r, 0, dka[...])
    put(mine_r, 1, dva[...])
    if reduce:
        rest_r.begin()

    loads[0].wait()
    first[2].wait()
    first[3].wait()
    g1 = []
    dgain1 = None
    for k in (0, 1):
        exchange.arrive(k)
        dv1, dgain = norm_back(x1[k], gain_ref[1:2, :], exchange.project(k, wa3))
        dgain1 = dgain if k == 0 else dgain1
        g1.append(g2[k] + dv1)
        e1[pair(k), :] = g1[k].astype(BF)
        share.begin(k)
    for b in range(total_blocks):
        mc0[b].wait_recv()
        mc0[b].wait_send()
        ms0[b] = (mem_part(p.ty, b) + mr0[b].astype(F32)).astype(BF)
        if b + 1 < total_blocks:
            mcy[b].start()
    turn(states // length)
    put(mine_b, 0, nn(tr[...], dqc_ref[...]))
    turn(states // length + 1)
    loads[2].wait()
    put(mine_b, 1, nn(tr[...], c[...]))
    if reduce:
        rest_b.begin()
        early.begin(jnp.concatenate([lanes(dgain1), lanes(dgain2_ref[...]), jnp.zeros((16 - width_d // 64, 128), F32)], axis=0))
        rest_r.step(1)
    for load in loads[3:]:
        load.wait()
    share.end()
    tr[...] = e1[...].T
    put(mine_o, 0, nn(tr[...], a[...]))
    if reduce:
        rest_o.begin()
        for k in range(2, n // 2):
            rest_r.step(k)

    start = segment_starts(seg_ref[...])
    wo = flat(ga)[:, 3 * width : 4 * width]
    for i in range(tiles):
        at = slice(i * tile, (i + 1) * tile)
        keys = (i + 1) * tile
        da = nn(e1[at, :], wo)
        dar = da.astype(BF)
        dat = da.T.astype(BF).astype(F32)
        qt = qkvt[0:width, at].astype(F32) * SCALE
        allowed = causal_mask(keys, tile, i, start[:, at])
        kk = qkv[0:keys, width : 2 * width]
        vv = qkv[0:keys, 2 * width : 3 * width]
        ps, ds, dq = [], [], []
        for h in range(heads):
            hs = slice(h * HEAD, (h + 1) * HEAD)
            inner = jnp.sum(dat[hs, :] * att[hs, at], axis=0, keepdims=True)
            prob = jnp.where(allowed, jnp.exp(nn(kk, head_rows(qt, h)) - lse[h : h + 1, at]), 0.0)
            grad = (prob * (nn(vv, head_rows(dat, h)) - inner)).astype(BF)
            ps.append(prob.astype(BF))
            ds.append(grad)
            dq.append(nn(qkvt[width + h * HEAD : width + (h + 1) * HEAD, 0:keys], grad))
        dqkv[at, 0:width] = (jnp.concatenate(dq, axis=0) * SCALE).T
        dk = nn(jnp.concatenate(ds, axis=1), head_block(qkv[at, 0:width].astype(F32) * SCALE, heads))
        dv = nn(jnp.concatenate(ps, axis=1), head_block(dar.astype(F32), heads))
        if i:
            dqkv[0 : keys - tile, width : 2 * width] += dk[0 : keys - tile]
            dqkv[0 : keys - tile, 2 * width : 3 * width] += dv[0 : keys - tile]
        dqkv[at, width : 2 * width] = dk[keys - tile :]
        dqkv[at, 2 * width : 3 * width] = dv[keys - tile :]
        if reduce and 0 < i < n // 2:
            rest_b.step(i)
    turn(states // length + 2)
    mine_a[...] = nn(tr[...], dqkv[...].astype(BF)).astype(BF).reshape(mine_a.shape)
    if reduce:
        rest_a.begin()
    last.begin(lambda j: nt(dqkv[rows(j, tile), :].astype(BF), flat(ga)[:, 0 : 3 * width]))
    if reduce:
        for k in range(tiles, n // 2):
            rest_b.step(k)
        for k in range(1, n // 2):
            rest_o.step(k)
        for k in range(1, n // 2):
            rest_a.step(k)
    dv0, dgain0 = norm_back(x0_ref[...].astype(F32), gain_ref[0:1, :], last.end())
    res_ref[...] = (g1[0] + dv0).astype(BF)
    tail = lanes(dgain0)
    if reduce:
        squares = squares_of(du_own[...])
        for r, out in zip(sums, own_outs):
            total = r.end()
            out[...] = total
            squares = squares + squares_of(total)
        late.begin(jnp.concatenate([tail, jnp.broadcast_to(squares, (8 - width_d // 128, 128))], axis=0))
    mcy[total_blocks - 1].start()
    if reduce:
        early.pass_on()
        late.pass_on()
    for b in range(total_blocks):
        mc1[b].wait_recv()
        mcy[b].wait_recv()
        own = mem_part(p.t, b) + mr1[b].astype(F32) + myr[b].astype(F32)
        mem_ref[b // blocks, (b % blocks) * 256 : (b % blocks + 1) * 256, :] = own.astype(BF)
    if reduce:
        stat_ref[0:8, :] = late.end()
        stat_ref[8:24, :] = early.end()
        for r in sums:
            r.sent()
    else:
        stat_ref[...] = jnp.concatenate(
            [tail, jnp.zeros((8 - width_d // 128, 128), F32), lanes(dgain1), lanes(dgain2_ref[...]),
             jnp.zeros((16 - width_d // 64, 128), F32)], axis=0)
    exchange.sent()
    for cpy in mc1 + mcy:
        cpy.wait_send()


def call_self_backward(n, reduce, plots, x0, x1, g2, gain, dgain2, seg, dqc, dk, dv, du,
                       e2, h1, h0, mem, ga, gb, c, a, qkv, qkvt, att, lse, wa3):
    _, tile, width_d = x1.shape
    length, width = dqc.shape
    states = mem.shape[0]
    patches = states // plots
    total_blocks = plots * (patches // 4 // 256)
    shard = width_d // n
    widths = (2 * width, 2 * width, width, 3 * width)
    out_shape = [
        sds((tile, width_d), BF),
        sds((plots, patches // 4, width_d), BF),
        sds((24, 128), F32),
    ]
    scratch = []
    if reduce:
        out_shape += [sds((shard, w), F32) for w in widths]
        scratch += [pltpu.VMEM((n, shard, w), BF) for w in widths]
        for w in widths:
            scratch += RowSum.scratch(n, shard, w)
        scratch += EveryoneSum.scratch(n, 16) + EveryoneSum.scratch(n, 8)
    else:
        out_shape += [sds((8, width_d // 8, w), BF) for w in widths]
    scratch += [pltpu.VMEM(v.shape, v.dtype) for v in (ga, gb, c, a, qkv, qkvt, att, lse, wa3, x1, g2, dk, dv, du)]
    scratch += [
        pltpu.VMEM((2, length, width_d), BF),
        pltpu.VMEM((length, width_d), BF),
        pltpu.VMEM((length, 3 * width), F32),
        pltpu.VMEM((width_d, width), F32),
        pltpu.VMEM((width_d, width), F32),
        pltpu.VMEM((width_d, length), BF),
        DMA((14,)),
        DMA((2,)),
    ]
    scratch += HeadExchange.scratch(tile, width) + CoreShare.scratch()
    scratch += TensorSum.scratch(tile, width_d)
    scratch += [pltpu.VMEM((total_blocks, 256, width_d), BF)] * 5 + [DMA((3, total_blocks))] * 2
    return pl.pallas_call(
        functools.partial(self_backward_kernel, n, reduce, width // HEAD),
        out_shape=out_shape,
        in_specs=[VM] * 5 + [ANY] * 18,
        out_specs=[VM] * len(out_shape),
        scratch_shapes=scratch,
        compiler_params=pltpu.CompilerParams(collective_id=3, has_side_effects=True, vmem_limit_bytes=VLIMIT),
        name="self_backward",
    )(x0, gain, dgain2, seg, dqc, x1, g2, dk, dv, du, e2, h1, h0, mem, ga, gb, c, a, qkv, qkvt, att, lse, wa3)


def adam_step(master, moment, second, gradient, step_rate, decay_rate):
    moment_new = BETA_ONE * moment + (1.0 - BETA_ONE) * gradient
    second_new = BETA_TWO * second + (1.0 - BETA_TWO) * gradient * gradient
    moment_hat = moment_new / (1.0 - BETA_ONE**STEP)
    second_hat = second_new / (1.0 - BETA_TWO**STEP)
    master_new = master - step_rate * (
        moment_hat / (jnp.sqrt(second_hat) + ADAM_EPS) + decay_rate * master
    )
    return (master_new, moment_new, second_new)


def update_kernel(width, hidden, *refs):
    stat_ref, u_ref, r_ref, b_ref, o_ref, a_ref = refs[0:6]
    params = [refs[6 + 3 * i : 9 + 3 * i] for i in range(6)]
    passed = refs[24:27]
    norm_ref = refs[27]
    outs = [refs[28 + 4 * i : 32 + 4 * i] for i in range(5)]
    gain_outs = refs[48:51]
    for src, dst in zip(passed, refs[51:54]):
        dst[...] = src[...]
    count = params[5][0].shape[1] // 128
    gains = jnp.concatenate(
        [jnp.concatenate([stat_ref[at + i : at + i + 1, :] for i in range(count)], axis=1) for at in (0, 8, 8 + count)],
        axis=0,
    )
    grad_norm = jnp.sqrt(stat_ref[count : count + 1, 0:1] + squares_of(gains))
    norm_ref[...] = grad_norm
    factor = jnp.minimum(1.0, CLIP / (grad_norm + 1e-06))

    def columns(ref, i, size):
        return ref[:, i * size : (i + 1) * size]

    grads = (
        [columns(a_ref, 0, width), columns(a_ref, 1, width), columns(a_ref, 2, width), columns(b_ref, 0, width)],
        [columns(r_ref, 0, width), columns(r_ref, 1, width)],
        [o_ref[...].T, columns(b_ref, 1, width).T],
        [columns(u_ref, 0, hidden), columns(u_ref, 1, hidden)],
        [columns(u_ref, 2, hidden)],
    )
    rates = (RATE_INNER, RATE_INNER, RATE_OUTER, RATE_INNER, RATE_INNER)
    for (master, moment, second), out, parts, rate in zip(params[0:5], outs, grads, rates):
        for i, g in enumerate(parts):
            at = i if len(master.shape) == 3 else Ellipsis
            new = adam_step(master[at], moment[at], second[at], g * factor, rate, DECAY)
            for ref, value in zip(out, new + (new[0],)):
                ref[at] = value.astype(ref.dtype)
    new = adam_step(*(r[...] for r in params[5]), gains * factor, RATE_GAIN, 0.0)
    for ref, value in zip(gain_outs, new):
        ref[...] = value


def call_update(stat, own, weights, passed):
    flat_weights = [w for group in weights for w in group]
    out_shape = [sds((1, 1), F32)]
    for group in weights[0:5]:
        out_shape += [sds(group[0].shape, F32)] * 3 + [sds(group[0].shape, BF)]
    out_shape += [sds(weights[5][0].shape, F32)] * 3
    out_shape += [sds(v.shape, BF) for v in passed]
    return pl.pallas_call(
        functools.partial(update_kernel, weights[0][0].shape[2], weights[3][0].shape[2]),
        out_shape=out_shape,
        in_specs=[VM] * 27,
        out_specs=[VM] * 27,
        compiler_params=pltpu.CompilerParams(vmem_limit_bytes=VLIMIT),
        name="update",
    )(stat, *own, *flat_weights, *passed)


def local(
    n,
    residual,
    cotangent,
    memory,
    segment_ids,
    plot_ids,
    attend_weight,
    attend_first,
    attend_second,
    recall_weight,
    recall_first,
    recall_second,
    outward_weight,
    outward_first,
    outward_second,
    expand_weight,
    expand_first,
    expand_second,
    narrow_weight,
    narrow_first,
    narrow_second,
    gain_weight,
    gain_first,
    gain_second,
):
    _, plots, patches, width_d = memory.shape
    shard = attend_weight.shape[1]
    aligned = shard % 16 == 0
    length = segment_ids.shape[1]

    def by_rows(w):
        return jnp.transpose(w, (1, 0, 2)).reshape(w.shape[1], -1)

    if aligned:
        shards = (attend_weight, recall_weight, outward_weight, expand_weight, narrow_weight.T)
    else:
        out_rows = jnp.transpose(outward_weight, (2, 0, 1))
        shards = (
            jnp.concatenate([by_rows(attend_weight[0:3]), out_rows[:, 0]], axis=1),
            by_rows(recall_weight),
            jnp.concatenate([attend_weight[3], out_rows[:, 1]], axis=1),
            by_rows(expand_weight),
            narrow_weight.T,
        )
        shards = tuple(
            lax.all_gather(s.astype(BF), "dp", axis=0, tiled=True).reshape(8, width_d // 8, s.shape[1]) for s in shards
        )
    mem = memory.reshape(plots * patches, width_d)
    x0 = residual[0]
    plot_row = plot_ids.reshape(-1)
    outs = call_first(
        n, aligned, plot_row, x0, cotangent[0], gain_weight, segment_ids, shards, mem
    )
    lse, qct, c, ct, lse_c, qkv, qkvt, a, att, x1, ga, gr, gb, gc, wn, h0, h1, e3, kk, vv, kt, wo1, wa3 = outs
    dgain2, f, g2, e2, du, x2 = call_ffn(n, c, x1, gain_weight, wo1, gc, wn, e3)
    outs = call_cross_backward(n, aligned, plot_row, segment_ids, e2, gb, qct, kk, vv, kt, ct, lse_c, f, x2, wn, du)
    dqc, dk, dv, block_out = outs[0:4]
    own_u = outs[4] if aligned else du[0 : width_d // n].astype(F32)
    outs = call_self_backward(
        n, aligned, plots, x0, x1, g2, gain_weight, dgain2, segment_ids, dqc, dk, dv, own_u,
        e2, h1, h0, mem, ga, gr, c, a, qkv, qkvt, att, lse, wa3
    )
    residual_grad, memory_grad, stat = outs[0:3]
    if aligned:
        own = (own_u,) + tuple(outs[3:7])
    else:
        own = tuple(
            lax.psum_scatter(g.reshape(width_d, -1).astype(F32), "dp", scatter_dimension=0, tiled=True)
            for g in (du,) + tuple(outs[3:7])
        )
        squares = sum(jnp.sum(g * g) for g in own)
        stat = lax.psum(stat.at[width_d // 128, :].set(squares), ("dp", "tensor"))
    weights = (
        (attend_weight, attend_first, attend_second),
        (recall_weight, recall_first, recall_second),
        (outward_weight, outward_first, outward_second),
        (expand_weight, expand_first, expand_second),
        (narrow_weight.T, narrow_first.T, narrow_second.T),
        (gain_weight, gain_first, gain_second),
    )
    new = call_update(stat, own, weights, (block_out, residual_grad, memory_grad))
    narrow_new = tuple(v.T for v in new[17:21])
    return (
        (new[24][None], new[25][None], new[26][None], new[0].reshape(())) + tuple(new[1:17]) + narrow_new + tuple(new[21:24])
    )


def solution(mesh):
    rows_in = P("dp", "tensor", None)
    inner = P(None, "dp", "tensor")
    outer = P(None, "tensor", "dp")
    narrow = P("tensor", "dp")
    in_specs = (
        (rows_in, rows_in, P("dp", None, None, None), P("dp", None), P("dp", None))
        + (inner,) * 3
        + (inner,) * 3
        + (outer,) * 3
        + (inner,) * 3
        + (narrow,) * 3
        + (P(),) * 3
    )
    out_specs = (
        (rows_in, rows_in, P("dp", None, "tensor", None), P())
        + (inner,) * 4
        + (inner,) * 4
        + (outer,) * 4
        + (inner,) * 4
        + (narrow,) * 4
        + (P(),) * 3
    )
    return jax.shard_map(
        functools.partial(local, mesh.shape["dp"]),
        mesh=mesh,
        in_specs=in_specs,
        out_specs=out_specs,
        check_vma=False,
    )
```

```python
import functools

import jax
import jax.numpy as jnp
from jax import lax
from jax.experimental import pallas as pl
from jax.experimental.pallas import tpu as pltpu
from jax.sharding import PartitionSpec as P

HEAD = 64
SEGS = 4
STEP = 10
NORM_EPS = 1e-06
ADAM_EPS = 1e-08
BETA_ONE = 0.9
BETA_TWO = 0.999
DECAY = 0.1
RATE_INNER = 0.05
RATE_OUTER = 0.4
RATE_GAIN = 0.5
CLIP = 1.0
MASKED = -1e30
SCALE = HEAD ** (-0.5)

MESH = pl.DeviceIdType.MESH
BF = jnp.bfloat16
F32 = jnp.float32
VLIMIT = 62 * 2**20
VM = pl.BlockSpec(memory_space=pltpu.VMEM)
ANY = pl.BlockSpec(memory_space=pl.ANY)
SM = pl.BlockSpec(memory_space=pltpu.SMEM)
DMA = pltpu.SemaphoreType.DMA


def sds(shape, dtype):
    return jax.ShapeDtypeStruct(shape, dtype)


def nn(a, b):
    return lax.dot_general(a, b, (((1,), (0,)), ((), ())), preferred_element_type=F32)


def nt(a, b):
    return lax.dot_general(a, b, (((1,), (1,)), ((), ())), preferred_element_type=F32)


def rows(i, size):
    return pl.ds(pl.multiple_of(i * size, size), size)


def flat(ref):
    return ref[...].reshape(ref.shape[0] * ref.shape[1], ref.shape[2])


def norm(v, g):
    return v * lax.rsqrt(jnp.mean(v * v, axis=-1, keepdims=True) + NORM_EPS) * g


def norm_back(v, g, dy):
    r = lax.rsqrt(jnp.mean(v * v, axis=-1, keepdims=True) + NORM_EPS)
    n = v * r
    dn = dy * g
    dv = r * (dn - n * jnp.mean(dn * n, axis=-1, keepdims=True))
    return dv, jnp.sum(dy * n, axis=0, keepdims=True)


class Place:
    def __init__(self, n):
        self.n = n
        self.d = lax.axis_index("dp")
        self.t = lax.axis_index("tensor")
        self.tc = self.t + 1 - 2 * lax.rem(self.t, 2)
        self.ty = lax.rem(self.t + 2, 4)
        self.tcy = lax.rem(self.tc + 2, 4)
        self.core = (self.d, self.tc)
        self.y = (self.d, self.ty)
        self.dx = self.d + 1 - 2 * lax.rem(self.d, 2)
        self.x = (self.dx, self.t)

    def z(self, k):
        return (lax.rem(self.d + 2 * k, self.n), self.t)

    def from_z(self, k):
        return lax.rem(self.d - 2 * k + 2 * self.n, self.n)

    def x_from_z(self, k):
        return lax.rem(self.dx - 2 * k + 2 * self.n, self.n)


def greet(devices):
    bar = pltpu.get_barrier_semaphore()
    for dev in devices:
        pl.semaphore_signal(bar, inc=1, device_id=dev, device_id_type=MESH)
    pl.semaphore_wait(bar, len(devices))


class Puts:
    def __init__(self, sems):
        self.sems = sems
        self.all = []

    def __call__(self, src, dst):
        c = pltpu.make_async_copy(src, dst, self.sems.at[len(self.all)])
        c.start()
        self.all.append(c)

    def end(self):
        for c in self.all:
            c.wait()


def rcopy(src, dst, ss, rs, dev):
    return pltpu.make_async_remote_copy(
        src_ref=src, dst_ref=dst, send_sem=ss, recv_sem=rs, device_id=dev, device_id_type=MESH
    )


class TensorSum:
    def __init__(self, place, refs):
        self.p = place
        self.s0, self.s1, self.r0, self.r1, self.own, self.ys, self.yr, self.ss, self.rs = refs

    @staticmethod
    def scratch(tile, width, hop=F32):
        return [pltpu.VMEM((tile, width), hop)] * 4 + [
            pltpu.VMEM((tile, width), F32),
            pltpu.VMEM((tile, width), BF),
            pltpu.VMEM((tile, width), BF),
            DMA((3,)),
            DMA((3,)),
        ]

    def begin(self, tile_fn):
        self.send(tile_fn)
        self.pass_on(tile_fn)

    def send(self, tile_fn):
        p = self.p
        self.c0 = rcopy(self.s0, self.r0, self.ss.at[0], self.rs.at[0], p.core)
        self.c1 = rcopy(self.s1, self.r1, self.ss.at[1], self.rs.at[1], p.core)
        self.cy = rcopy(self.ys, self.yr, self.ss.at[2], self.rs.at[2], p.y)
        self.s0[...] = tile_fn(p.tcy).astype(self.s0.dtype)
        self.c0.start()
        self.s1[...] = tile_fn(p.tc).astype(self.s1.dtype)
        self.c1.start()

    def pass_on(self, tile_fn):
        p = self.p
        part = tile_fn(p.ty)
        self.c0.wait_recv()
        self.ys[...] = (part + self.r0[...].astype(F32)).astype(BF)
        self.cy.start()
        self.own[...] = tile_fn(p.t)

    def end(self):
        self.c1.wait_recv()
        self.cy.wait_recv()
        total = self.own[...] + self.r1[...].astype(F32) + self.yr[...].astype(F32)
        self.c0.wait_send()
        self.c1.wait_send()
        self.cy.wait_send()
        return total


class TensorGather:
    def __init__(self, place, full, sems):
        self.p = p = place
        self.full = full
        ss, rs = sems
        mine, far, near, cross = (full.at[i] for i in (p.t, p.ty, p.tc, p.tcy))
        self.cc = rcopy(mine, mine, ss.at[0], rs.at[0], p.core)
        self.cy = rcopy(mine, mine, ss.at[1], rs.at[1], p.y)
        self.cf = rcopy(far, far, ss.at[2], rs.at[2], p.core)
        self.wc = rcopy(near, near, ss.at[0], rs.at[0], p.core)
        self.wy = rcopy(far, far, ss.at[1], rs.at[1], p.y)
        self.wf = rcopy(cross, cross, ss.at[2], rs.at[2], p.core)

    @staticmethod
    def scratch():
        return [DMA((3,)), DMA((3,))]

    def begin(self, own):
        self.full[self.p.t] = own
        self.cy.start()
        self.cc.start()

    def forward(self):
        self.wy.wait_recv()
        self.cf.start()

    def end(self):
        self.wc.wait_recv()
        self.wf.wait_recv()
        self.cy.wait_send()
        self.cc.wait_send()
        self.cf.wait_send()


class TileSwap:
    def __init__(self, place, full, sems, tile):
        self.p = p = place
        ss, rs = sems
        mine = full.at[rows(p.t, tile)]
        far = full.at[rows(p.ty, tile)]
        self.out = rcopy(mine, mine, ss.at[0], rs.at[0], p.y)
        self.back = rcopy(far, far, ss.at[0], rs.at[0], p.y)

    @staticmethod
    def scratch():
        return [DMA((1,)), DMA((1,))]

    def begin(self):
        self.out.start()

    def end(self):
        self.back.wait_recv()
        self.out.wait_send()


class CoreShare:
    def __init__(self, place, full, sems, tile):
        self.p = p = place
        ss, rs = sems
        self.out = [rcopy(full.at[rows(i, tile)], full.at[rows(i, tile)], ss.at[k], rs.at[k], p.core)
                    for k, i in enumerate((p.t, p.ty))]
        self.back = [rcopy(full.at[rows(i, tile)], full.at[rows(i, tile)], ss.at[k], rs.at[k], p.core)
                     for k, i in enumerate((p.tc, p.tcy))]

    @staticmethod
    def scratch():
        return [DMA((2,)), DMA((2,))]

    def begin(self, k):
        self.out[k].start()

    def arrive(self, k):
        self.back[k].wait_recv()

    def sent(self):
        for c in self.out:
            c.wait_send()

    def end(self):
        self.arrive(0)
        self.arrive(1)
        self.sent()


class HeadExchange:
    def __init__(self, place, own, got, sems, tile):
        self.p = p = place
        self.own, self.got, self.tile = own, got, tile
        ss, rs = sems
        peers = ((p.core, (p.tc, p.tcy), p.tc), (p.y, (p.ty, p.t), p.ty), ((p.d, p.tcy), (p.tcy, p.tc), p.tcy))
        self.out = [[rcopy(own.at[rows(tiles[k], tile)], got.at[p.t, k], ss.at[i, k], rs.at[i, k], dev) for k in (0, 1)]
                    for i, (dev, tiles, _) in enumerate(peers)]
        self.back = [[rcopy(got.at[src, k], got.at[src, k], ss.at[i, k], rs.at[i, k], dev) for k in (0, 1)]
                     for i, (dev, _, src) in enumerate(peers)]

    @staticmethod
    def scratch(tile, width):
        return [pltpu.VMEM((4, 2, tile, width), BF), DMA((3, 2)), DMA((3, 2))]

    def begin(self):
        for k in (0, 1):
            for i in (1, 2, 0):
                self.out[i][k].start()
        self.got[self.p.t, 0] = self.own[rows(self.p.t, self.tile), :]
        self.got[self.p.t, 1] = self.own[rows(self.p.ty, self.tile), :]

    def arrive(self, k):
        for i in (0, 1, 2):
            self.back[i][k].wait_recv()

    def sent(self):
        for group in self.out:
            for c in group:
                c.wait_send()

    def project(self, k, weights):
        total = nt(self.got[0, k], weights[0])
        for s in range(1, 4):
            total = total + nt(self.got[s, k], weights[s])
        return total


class ChipSum:
    def __init__(self, place, refs):
        self.p = p = place
        self.s, self.r, self.ys, self.yr, self.ss, self.rs = refs
        self.core = [rcopy(self.s.at[k], self.r.at[k], self.ss.at[k], self.rs.at[k], p.core) for k in (0, 1)]
        self.y = [rcopy(self.ys.at[k], self.yr.at[1 - k], self.ss.at[2 + k], self.rs.at[3 - k], p.y) for k in (0, 1)]
        self.yback = [rcopy(self.ys.at[k], self.yr.at[k], self.ss.at[2 + k], self.rs.at[2 + k], p.y) for k in (0, 1)]

    @staticmethod
    def scratch(tile, width, hop=F32):
        return [pltpu.VMEM((2, tile, width), hop)] * 2 + [pltpu.VMEM((2, tile, width), BF)] * 2 + [DMA((4,)), DMA((4,))]

    def send(self, k, tile_fn):
        self.s[k] = tile_fn((self.p.tc, self.p.tcy)[k]).astype(self.s.dtype)
        self.core[k].start()

    def pass_on(self, k, tile_fn):
        part = tile_fn((self.p.t, self.p.ty)[k])
        self.core[k].wait_recv()
        self.ys[k] = (part + self.r[k].astype(F32)).astype(BF)
        self.y[k].start()

    def end(self, k):
        self.yback[k].wait_recv()
        return self.ys[k].astype(F32) + self.yr[k].astype(F32)

    def sent(self):
        for c in self.core + self.y:
            c.wait_send()


class RowGather:
    def __init__(self, place, full, sems):
        self.p = place
        self.full = full
        self.zs, self.zr, self.xs, self.xr = sems
        self.steps = place.n // 2

    @staticmethod
    def scratch(n):
        return [DMA((n // 2,))] * 4

    def zcopy(self, k, slot):
        return rcopy(self.full.at[slot], self.full.at[slot], self.zs.at[k], self.zr.at[k], self.p.z(k))

    def xcopy(self, k, slot):
        return rcopy(self.full.at[slot], self.full.at[slot], self.xs.at[k], self.xr.at[k], self.p.x)

    def begin_far(self):
        for k in range(1, self.steps):
            self.zcopy(k, self.p.d).start()

    def begin_near(self):
        self.xcopy(0, self.p.d).start()

    def sent(self):
        for k in range(1, self.steps):
            self.zcopy(k, self.p.d).wait_send()

    def forward(self, k):
        slot = self.p.from_z(k)
        self.zcopy(k, slot).wait_recv()
        self.xcopy(k, slot).start()

    def forward_all(self):
        for k in range(1, self.steps):
            self.forward(k)

    def end(self):
        for k in range(self.steps):
            self.xcopy(k, self.p.x_from_z(k)).wait_recv()
            self.xcopy(k, self.p.from_z(k)).wait_send()


def head_rows(qt, head):
    ids = lax.broadcasted_iota(jnp.int32, qt.shape, 0)
    return jnp.where((ids >= head * HEAD) & (ids < (head + 1) * HEAD), qt, 0.0).astype(BF)


def head_block(x, heads):
    ids = lax.broadcasted_iota(jnp.int32, x.shape, 1)
    return jnp.concatenate(
        [jnp.where((ids >= h * HEAD) & (ids < (h + 1) * HEAD), x, 0.0).astype(BF) for h in range(heads)], axis=0
    )


def segment_starts(seg):
    start = jnp.zeros(seg.shape, jnp.int32)
    for s in range(SEGS - 1):
        count = jnp.sum(jnp.where(seg == s, 1, 0), axis=1, keepdims=True)
        start = start + jnp.where(seg > s, count, 0)
    return start


def causal_mask(keys, tile, tau, start):
    key_place = lax.broadcasted_iota(jnp.int32, (keys, tile), 0)
    query_place = lax.broadcasted_iota(jnp.int32, (keys, tile), 1) + tau * tile
    return (key_place <= query_place) & (key_place >= start)


def plot_order(seg, plot_ref):
    counts = [jnp.sum(jnp.where(seg == s, 1, 0), axis=1, keepdims=True) for s in range(SEGS)]
    place = lax.broadcasted_iota(jnp.int32, seg.shape, 1)
    first = jnp.zeros((1, 1), jnp.int32)
    for s in range(SEGS):
        shift = jnp.zeros((1, 1), jnp.int32)
        for o in range(SEGS):
            if o != s:
                ahead = plot_ref[o] < plot_ref[s] if o > s else plot_ref[o] <= plot_ref[s]
                shift = shift + counts[o] * (ahead.astype(jnp.int32) - (1 if o < s else 0))
        place = place + jnp.where(seg == s, shift, 0)
        first = first + counts[s] * (plot_ref[s] == 0).astype(jnp.int32)
    return place, first


def order_tile(place, i, tile):
    spot = lax.broadcasted_iota(jnp.int32, (tile, place.shape[1]), 0) + i * tile
    return jnp.where(place == spot, 1.0, 0.0).astype(BF)


class Slots:
    tile = 256

    def __init__(self, place, first):
        self.place = place
        self.split = jnp.sum(first)
        self.zero_tiles = lax.div(self.split + (self.tile - 1), self.tile)
        self.shared = self.zero_tiles - lax.div(self.split, self.tile)
        self.count = place.shape[1] // self.tile + 1

    def at(self, s):
        plot = (s >= self.zero_tiles).astype(jnp.int32)
        i = s - plot * self.shared
        spot = lax.broadcasted_iota(jnp.int32, (1, self.tile), 1) + i * self.tile
        side = (spot >= self.split).astype(jnp.int32)
        counts = (side == plot) & (spot < self.place.shape[1])
        return plot, order_tile(self.place, i, self.tile), counts


def first_kernel(n, gather, heads, plot_ref, x0_ref, cot_ref, gain_ref, seg_ref, *more):
    more = list(more)
    weights = [more.pop(0) for _ in range(5)]
    (m_hbm, lse_ref, qct_ref, c_ref, ct_ref, lsec_ref, qkv_out, qkvt_out, a_out, at_out, x1_out, ga_out,
     gr_out, gb_out, gc_out, gd_out, h0_out, h1_out, e3_out, kk_out, vv_out, kt_out, wo1_out, wa3_out, qkv_ref, qkvt_ref, a_ref, at_ref, x1_ref,
     ga, gr, gb, gc, gd, h0, h1, e3, kk, vv, kt, wo0, wo1, wa3, xf, m_ref, vte, ctok, score, raised, lsem, osem), rest = more[:51], more[51:]

    def take(count):
        got = rest[:count]
        del rest[:count]
        return got

    p = Place(n)
    tile = x0_ref.shape[0]
    width = heads * HEAD
    tiles = h0.shape[0] // tile
    load_m = pltpu.make_async_copy(m_hbm, m_ref, lsem.at[0])
    load_m.start()
    swaps = [TileSwap(p, full, take(2), tile) for full in (xf, e3)]
    shares = [CoreShare(p, full, take(2), tile) for full in (h0, e3, h1)]
    spreads = [TensorGather(p, full, take(2)) for full in (wo0, wo1, wa3)]
    heads_in, hs, hr = take(3)
    exchange = HeadExchange(p, a_ref, heads_in, (hs, hr), tile)
    xf[rows(p.t, tile), :] = x0_ref[...]
    e3[rows(p.t, tile), :] = cot_ref[...]
    if gather:
        parts = [RowGather(p, full, take(4)) for full in (ga, gr, gb, gc, gd)]
        part_a, part_r, part_b, part_c, part_d = parts
        aw, rw, ow, ew, nw = weights

        def fill(full, *mats):
            full[p.d] = jnp.concatenate(mats, axis=1).astype(BF)

        fill(ga, aw[0], aw[1], aw[2], ow[0].T)
        greet([p.core, p.y, (p.d, p.tcy), p.x] + [p.z(k) for k in range(1, n // 2)])
        swaps[0].begin()
        part_a.begin_near()
        part_a.begin_far()
        fill(gr, rw[0], rw[1])
        fill(gb, aw[3], ow[1].T)
        fill(gc, ew[0], ew[1])
        gd[p.d] = nw[...].astype(BF)
    else:
        copies = [pltpu.make_async_copy(s, f, lsem.at[1 + i]) for i, (s, f) in
                  enumerate(zip(weights, (ga, gr, gb, gc, gd)))]
        for c in copies:
            c.start()
        greet([p.core, p.y, (p.d, p.tcy)])
        swaps[0].begin()

    def normed(v, i):
        return norm(v, gain_ref[i : i + 1, :]).astype(BF)

    def pair(k):
        return rows((p.t, p.ty)[k], tile)

    h0[pair(0), :] = normed(x0_ref[...].astype(F32), 0)
    shares[0].begin(0)
    start = segment_starts(seg_ref[...])
    states = kk.shape[0]
    ext = HEAD + 16
    for h in range(heads):
        vte[h * ext + HEAD : (h + 1) * ext, :] = jnp.ones((16, states), BF)
    ctok[...] = jnp.zeros(ctok.shape, F32)
    lsec_ref[...] = jnp.zeros(lsec_ref.shape, F32)
    swaps[0].end()
    swaps[1].begin()
    h0[pair(1), :] = normed(xf[pair(1), :].astype(F32), 0)
    shares[0].begin(1)
    if gather:
        part_a.forward_all()
        part_r.begin_near()
        part_r.begin_far()
        part_b.begin_far()
    shares[0].end()
    if gather:
        part_a.end()
    else:
        for c in copies:
            c.wait()
    spreads[0].begin(flat(ga)[:, 3 * width : 4 * width])

    wa = flat(ga)
    for i in range(tiles):
        at = slice(i * tile, (i + 1) * tile)
        x = nn(h0[at, :], wa[:, : 3 * width])
        qkv_ref[at, :] = x.astype(BF)
        qkvt_ref[:, at] = x.T.astype(BF)
    put = Puts(osem)
    put(ga, ga_out)
    put(h0, h0_out)
    put(qkv_ref, qkv_out)
    put(qkvt_ref, qkvt_out)
    swaps[1].end()
    shares[1].begin(0)
    shares[1].begin(1)
    if gather:
        part_c.begin_far()

    for i in range(tiles):
        at = slice(i * tile, (i + 1) * tile)
        keys = (i + 1) * tile
        own_keys = qkv_ref[0:keys, width : 2 * width]
        qt = qkvt_ref[0:width, at].astype(F32) * SCALE
        allowed = causal_mask(keys, tile, i, start[:, at])
        for h in range(heads):
            s = jnp.where(allowed, nn(own_keys, head_rows(qt, h)), MASKED)
            peak = jnp.max(s, axis=0, keepdims=True)
            e = jnp.exp(s - peak)
            total = jnp.sum(e, axis=0, keepdims=True)
            w = (e * (1.0 / total)).astype(BF)
            vt = qkvt_ref[2 * width + h * HEAD : 2 * width + (h + 1) * HEAD, 0:keys]
            at_ref[h * HEAD : (h + 1) * HEAD, at] = nn(vt, w)
            lse_ref[h : h + 1, at] = peak + jnp.log(total)
        a_ref[at, :] = at_ref[:, at].T.astype(BF)
        if i == 1:
            spreads[0].forward()
        if gather and i < 3:
            part_r.forward(i + 1)
    exchange.begin()
    put(a_ref, a_out)
    put(at_ref, at_out)
    if gather:
        for k in range(4, n // 2):
            part_r.forward(k)
        part_b.begin_near()
        part_b.forward_all()
    shares[1].end()
    put(e3, e3_out)
    spreads[0].end()
    if gather:
        part_c.begin_near()
        part_r.end()
        part_d.begin_far()
    put(gr, gr_out)
    load_m.wait()
    mtiles = m_ref.shape[0] // 256

    def project_memory(i, carry):
        at = rows(i, 256)
        x = nn(m_ref[at, :], flat(gr))
        kk[at, :] = x[:, 0:width].astype(BF)
        vv[at, :] = x[:, width : 2 * width].astype(BF)
        xt = x.T.astype(BF)
        kt[:, at] = xt[0:width]
        for h in range(heads):
            vte[h * ext : h * ext + HEAD, at] = xt[width + h * HEAD : width + (h + 1) * HEAD]
        return carry

    lax.fori_loop(0, mtiles, project_memory, 0)
    put(kk, kk_out)
    put(vv, vv_out)
    put(kt, kt_out)
    for k in (0, 1):
        exchange.arrive(k)
        if gather:
            part_c.forward(k + 1)
        x1 = xf[pair(k), :].astype(F32) + exchange.project(k, wo0)
        x1_ref[k] = x1
        h1[pair(k), :] = normed(x1, 1)
        shares[2].begin(k)
    put(x1_ref, x1_out)
    if gather:
        for k in range(3, n // 2):
            part_c.forward(k)
        part_d.begin_near()
    if gather:
        part_b.end()
    put(gb, gb_out)
    spreads[1].begin(flat(gb)[:, width : 2 * width])
    spreads[2].begin(flat(gb)[:, 0:width])
    shares[2].end()
    put(h1, h1_out)
    wq = flat(gb)[:, 0:width]
    for i in range(tiles):
        at = slice(i * tile, (i + 1) * tile)
        qct_ref[:, at] = nn(h1[at, :], wq).T.astype(BF)

    patches = states // 2
    slots = Slots(*plot_order(seg_ref[...], plot_ref))

    def one_slot(s, carry):
        plot, order, counts = slots.at(s)
        qt = nt(qct_ref[...], order) * SCALE
        q = [head_rows(qt, h) for h in range(heads)]

        def scores(h, c, peak):
            near, far = slice(c * 256, (c + 1) * 256), slice(patches + c * 256, patches + (c + 1) * 256)
            x = nn(jnp.where(plot == 0, kk[near, :], kk[far, :]), q[h])
            score[h % 2, near] = x
            top = jnp.max(x, axis=0, keepdims=True)
            return top if peak is None else jnp.maximum(peak, top)

        chunks = patches // 256
        peak = None
        for c in range(chunks):
            peak = scores(0, c, peak)
        for h in range(heads):
            ahead = None
            for c in range(chunks):
                if h + 1 < heads:
                    ahead = scores(h + 1, c, ahead)
                near = slice(c * 256, (c + 1) * 256)
                raised[h % 2, near] = jnp.exp(score[h % 2, near] - peak).astype(BF)
            hs = slice(h * ext, (h + 1) * ext)
            acc = nn(jnp.where(plot == 0, vte[hs, 0:patches], vte[hs, patches:states]), raised[h % 2])
            total = acc[HEAD : HEAD + 1, :]
            ct_ref[s, h * HEAD : (h + 1) * HEAD, :] = jnp.where(counts, acc[0:HEAD, :] * (1.0 / total), 0.0)
            lsec_ref[s, h : h + 1, :] = jnp.where(counts, peak + jnp.log(total), -MASKED)
            peak = ahead
        ctok[...] += nn(ct_ref[s].astype(BF), order)
        if gather:
            for k in range(1, n // 2):
                pl.when(s == min(k - 1, slots.count - 1))(functools.partial(part_d.forward, k))

        @pl.when(s == 3)
        def _():
            spreads[1].forward()
            spreads[2].forward()

        return carry

    lax.fori_loop(0, slots.count, one_slot, 0)
    c_ref[...] = ctok[...].T.astype(BF)
    spreads[1].end()
    put(wo1, wo1_out)
    spreads[2].end()
    put(wa3, wa3_out)
    exchange.sent()
    if gather:
        for part in parts:
            part.sent()
        part_c.end()
        part_d.end()
    put(gc, gc_out)
    put(gd, gd_out)
    put.end()


def call_first(n, gather, plot_ids, x0, cot, gain, seg, weights, mem):
    tile, width_d = x0.shape
    length = seg.shape[1]
    states = mem.shape[0]
    if gather:
        width, hidden = weights[0].shape[2], weights[4].shape[1]
    else:
        width, hidden = weights[0].shape[2] // 4, weights[4].shape[2]
    heads = width // HEAD
    shapes = [(8, width_d // 8, w) for w in (4 * width, 2 * width, 2 * width, 2 * hidden, hidden)]
    spread = (4, width_d, width)
    early = [
        sds((length, 3 * width), BF),
        sds((3 * width, length), BF),
        sds((length, width), BF),
        sds((width, length), F32),
        sds((2, tile, width_d), F32),
    ]
    late = [
        sds(shapes[0], BF),
        sds(shapes[1], BF),
        sds(shapes[2], BF),
        sds(shapes[3], BF),
        sds(shapes[4], BF),
        sds((length, width_d), BF),
        sds((length, width_d), BF),
        sds((length, width_d), BF),
        sds((states, width), BF),
        sds((states, width), BF),
        sds((width, states), BF),
        sds(spread, BF),
        sds(spread, BF),
    ]
    out_shape = [
        sds((8, length), F32),
        sds((width, length), BF),
        sds((length, width), BF),
        sds((length // 256 + 1, width, 256), F32),
        sds((length // 256 + 1, 8, 256), F32),
    ] + early + late
    scratch = [pltpu.VMEM(s.shape, s.dtype) for s in early] + [pltpu.VMEM(s, BF) for s in shapes]
    scratch += [pltpu.VMEM((length, width_d), BF)] * 3
    scratch += [
        pltpu.VMEM((states, width), BF),
        pltpu.VMEM((states, width), BF),
        pltpu.VMEM((width, states), BF),
        pltpu.VMEM(spread, BF),
        pltpu.VMEM(spread, BF),
        pltpu.VMEM(spread, BF),
        pltpu.VMEM((length, width_d), BF),
        pltpu.VMEM((states, width_d), BF),
        pltpu.VMEM((heads * (HEAD + 16), states), BF),
        pltpu.VMEM((width, length), F32),
        pltpu.VMEM((2, states // 2, 256), F32),
        pltpu.VMEM((2, states // 2, 256), BF),
        DMA((6,)),
        DMA((len(early + late),)),
    ]
    scratch += TileSwap.scratch() * 2 + CoreShare.scratch() * 3 + TensorGather.scratch() * 3
    scratch += HeadExchange.scratch(tile, width)
    if gather:
        scratch += RowGather.scratch(n) * 5
    shard = VM if gather else ANY
    return pl.pallas_call(
        functools.partial(first_kernel, n, gather, heads),
        out_shape=out_shape,
        in_specs=[SM, VM, VM, VM, VM] + [shard] * len(weights) + [ANY],
        out_specs=[VM] * 5 + [ANY] * len(early + late),
        scratch_shapes=scratch,
        compiler_params=pltpu.CompilerParams(collective_id=1, has_side_effects=True, vmem_limit_bytes=VLIMIT),
        name="attention_forward",
    )(plot_ids, x0, cot, gain, seg, *weights, mem)


def ffn_kernel(n, c_ref, gain_ref, x1_hbm, wo_hbm, gc_hbm, wn_hbm, e3_hbm,
               dgain_ref, f_out, g2_out, e2_out, du_out, x2_out,
               x1, wo, gc, wn, e3, f, g2, e2, du, x2, h2, dg, h2t, e3t, lsem, osem, *rest):
    rest = list(rest)

    def take(count):
        got = rest[:count]
        del rest[:count]
        return got

    p = Place(n)
    _, tile, width_d = x1.shape
    hidden = f.shape[1]
    heads_in, hs, hr = take(3)
    exchange = HeadExchange(p, c_ref, heads_in, (hs, hr), tile)
    shares = [CoreShare(p, full, take(2), tile) for full in (h2, e2)]
    total = ChipSum(p, take(6))
    put = Puts(osem)
    loads = [pltpu.make_async_copy(s, d, lsem.at[i]) for i, (s, d) in
             enumerate(((e3_hbm, e3), (wo_hbm, wo), (x1_hbm, x1), (gc_hbm, gc), (wn_hbm, wn)))]
    for load in loads:
        load.start()
    greet([p.core, p.y, (p.d, p.tcy)])
    exchange.begin()
    loads[0].wait()
    e3t[...] = e3[...].T

    def pair(k):
        return rows((p.t, p.ty)[k], tile)

    def hidden_tile(j):
        at = rows(j, tile)
        gate = nn(h2[at, :], flat(gc)[:, 0:hidden])
        up = nn(h2[at, :], flat(gc)[:, hidden : 2 * hidden])
        df = nn(e3[at, :], flat(wn))
        sq = gate * gate
        th = jnp.tanh(0.7978845608 * gate * (1.0 + 0.044715 * sq))
        half = 0.5 * (1.0 + th)
        act = gate * half
        slope = half + 0.5 * gate * (1.0 - th * th) * (0.7978845608 * (1.0 + 3.0 * 0.044715 * sq))
        f[at, :] = (act * up).astype(BF)
        dg[at, 0:hidden] = (df * up * slope).astype(BF)
        dg[at, hidden : 2 * hidden] = (df * act).astype(BF)

    def back_tile(j):
        return nt(dg[rows(j, tile), :], flat(gc)[:, 0 : 2 * hidden])

    for load in loads[1:]:
        load.wait()
    for k in (0, 1):
        exchange.arrive(k)
        x2[k] = x1[k] + exchange.project(k, wo)
        h2[pair(k), :] = norm(x2[k], gain_ref[2:3, :]).astype(BF)
        shares[0].begin(k)
    put(x2, x2_out)
    for k in (0, 1):
        hidden_tile((p.t, p.ty)[k])
        shares[0].arrive(k)
        hidden_tile((p.tc, p.tcy)[k])
        total.send(k, back_tile)
        if k == 1:
            total.pass_on(0, back_tile)
    total.pass_on(1, back_tile)
    put(f, f_out)
    h2t[...] = h2[...].T
    for i in range(2 * hidden // 256):
        cs = slice(i * 256, (i + 1) * 256)
        du[:, cs] = nn(h2t[...], dg[:, cs]).astype(BF)
    for i in range(hidden // 256):
        cs = slice(i * 256, (i + 1) * 256)
        du[:, 2 * hidden + i * 256 : 2 * hidden + (i + 1) * 256] = nn(e3t[...], f[:, cs]).astype(BF)
    put(du, du_out)
    for k in (0, 1):
        dv, dgain = norm_back(x2[k], gain_ref[2:3, :], total.end(k))
        if k == 0:
            dgain_ref[...] = dgain
        g2[k] = e3[pair(k), :].astype(F32) + dv
        e2[pair(k), :] = g2[k].astype(BF)
        shares[1].begin(k)
    put(g2, g2_out)
    shares[0].sent()
    exchange.sent()
    total.sent()
    shares[1].end()
    put(e2, e2_out)
    put.end()


def call_ffn(n, c, x1, gain, wo, gc, wn, e3):
    _, tile, width_d = x1.shape
    length, width = c.shape
    hidden = gc.shape[2] // 2
    late = [
        sds((length, hidden), BF),
        sds((2, tile, width_d), F32),
        sds((length, width_d), BF),
        sds((width_d, 3 * hidden), BF),
        sds((2, tile, width_d), F32),
    ]
    scratch = [pltpu.VMEM(v.shape, v.dtype) for v in [x1, wo, gc, wn, e3] + late]
    scratch += [
        pltpu.VMEM((length, width_d), BF),
        pltpu.VMEM((length, 2 * hidden), BF),
        pltpu.VMEM((width_d, length), BF),
        pltpu.VMEM((width_d, length), BF),
        DMA((5,)),
        DMA((len(late),)),
    ]
    scratch += HeadExchange.scratch(tile, width) + CoreShare.scratch() * 2 + ChipSum.scratch(tile, width_d)
    return pl.pallas_call(
        functools.partial(ffn_kernel, n),
        out_shape=[sds((1, width_d), F32)] + late,
        in_specs=[VM] * 2 + [ANY] * 5,
        out_specs=[VM] + [ANY] * len(late),
        scratch_shapes=scratch,
        compiler_params=pltpu.CompilerParams(collective_id=2, has_side_effects=True, vmem_limit_bytes=VLIMIT),
        name="ffn",
    )(c, gain, x1, wo, gc, wn, e3)


def cross_backward_kernel(n, reduce, heads, plot_ref, seg_ref, qct_ref, ct_ref, lse_ref, e2_hbm, gb_hbm, kk_hbm, vv_hbm, kt_hbm,
                          f_hbm, x2_hbm, wn_hbm, du_hbm, dqc_ref, dk_ref, dv_ref, blk_ref, *rest):
    rest = list(rest)

    def take(count):
        got = rest[:count]
        del rest[:count]
        return got

    p = Place(n)
    width = heads * HEAD
    states = kk_hbm.shape[0]
    patches = states // 2
    length = qct_ref.shape[1]
    hidden = f_hbm.shape[1]
    if reduce:
        du_out, mine_u = take(2)
        rest_u = RowSum(p, mine_u, take(6))
    dka, dva, dct_all, dqtok, e2, gb, kk, vv, kt, f, x2, wn, lsem = take(13)
    tile = x2.shape[0]
    block = TensorSum(p, take(9))
    pairs = [(f_hbm, f), (wn_hbm, wn), (e2_hbm, e2), (gb_hbm, gb), (kk_hbm, kk), (vv_hbm, vv),
             (kt_hbm, kt), (x2_hbm.at[0], x2)]
    if reduce:
        pairs.insert(0, (du_hbm, mine_u))
    loads = [pltpu.make_async_copy(s, d, lsem.at[i]) for i, (s, d) in enumerate(pairs)]
    for load in loads:
        load.start()
    greet([p.core, p.y] + ([p.x] + [p.z(k) for k in range(1, n // 2)] if reduce else []))
    if reduce:
        loads.pop(0).wait()
        rest_u.begin()
    loads[0].wait()
    loads[1].wait()

    def out_tile(j):
        return nt(f[rows(j, tile), :], flat(wn))

    block.send(out_tile)
    for load in loads[2:]:
        load.wait()
    dka[...] = jnp.zeros(dka.shape, F32)
    dva[...] = jnp.zeros(dva.shape, F32)
    dqtok[...] = jnp.zeros(dqtok.shape, F32)
    wo = flat(gb)[:, width : 2 * width]
    for i in range(length // 256):
        at = slice(i * 256, (i + 1) * 256)
        dct_all[:, at] = nn(e2[at, :], wo).T.astype(BF)
    block.pass_on(out_tile)
    if reduce:
        rest_u.step(1)
    slots = Slots(*plot_order(seg_ref[...], plot_ref))

    def one_slot(s, carry):
        plot, order, _ = slots.at(s)
        dct = nt(dct_all[...], order)
        qt = nt(qct_ref[...], order) * SCALE
        keys = jnp.where(plot == 0, kk[0:patches, :], kk[patches:states, :])
        values = jnp.where(plot == 0, vv[0:patches, :], vv[patches:states, :])
        ps, ds, dq = [], [], []
        for h in range(heads):
            hs = slice(h * HEAD, (h + 1) * HEAD)
            inner = jnp.sum(dct[hs, :] * ct_ref[s, hs, :], axis=0, keepdims=True)
            prob = jnp.exp(nn(keys, head_rows(qt, h)) - lse_ref[s, h : h + 1, :])
            grad = (prob * (nn(values, head_rows(dct, h)) - inner)).astype(BF)
            ps.append(prob.astype(BF))
            ds.append(grad)
            dq.append(nn(jnp.where(plot == 0, kt[hs, 0:patches], kt[hs, patches:states]), grad))
        dqtok[...] += nn((jnp.concatenate(dq, axis=0) * SCALE).astype(BF), order)
        dv = nn(jnp.concatenate(ps, axis=1), head_block(dct.T, heads))
        dk = nn(jnp.concatenate(ds, axis=1), head_block(qt.T, heads))
        for j in range(2):
            part = slice(j * patches, (j + 1) * patches)
            dva[part, :] += jnp.where(plot == j, dv, 0.0)
            dka[part, :] += jnp.where(plot == j, dk, 0.0)
        if reduce:
            for k in range(1, n // 2):
                if k > 1:
                    pl.when(s == min(k - 2, slots.count - 1))(functools.partial(rest_u.step, k))
        return carry

    lax.fori_loop(0, slots.count, one_slot, 0)
    dqc_ref[...] = dqtok[...].T.astype(BF)
    dk_ref[...] = dka[...].astype(BF)
    dv_ref[...] = dva[...].astype(BF)
    blk_ref[...] = (x2[...] + block.end()).astype(BF)
    if reduce:
        du_out[...] = rest_u.end()
        rest_u.sent()


def call_cross_backward(n, reduce, plot_ids, seg, e2, gb, qct, kk, vv, kt, ct, lse, f, x2, wn, du):
    width, length = qct.shape
    states = kk.shape[0]
    _, tile, width_d = x2.shape
    out_shape = [
        sds((length, width), BF),
        sds((states, width), BF),
        sds((states, width), BF),
        sds((tile, width_d), BF),
    ]
    scratch = []
    if reduce:
        shard = width_d // n
        out_shape.append(sds((shard, du.shape[1]), F32))
        scratch += [pltpu.VMEM((n, shard, du.shape[1]), BF)] + RowSum.scratch(n, shard, du.shape[1])
        du = du.reshape(n, shard, du.shape[1])
    scratch += [
        pltpu.VMEM((states, width), F32),
        pltpu.VMEM((states, width), F32),
        pltpu.VMEM((width, length), BF),
        pltpu.VMEM((width, length), F32),
        pltpu.VMEM(e2.shape, BF),
        pltpu.VMEM(gb.shape, BF),
        pltpu.VMEM((states, width), BF),
        pltpu.VMEM((states, width), BF),
        pltpu.VMEM((width, states), BF),
        pltpu.VMEM(f.shape, BF),
        pltpu.VMEM((tile, width_d), F32),
        pltpu.VMEM(wn.shape, BF),
        DMA((9,)),
    ] + TensorSum.scratch(tile, width_d, BF)
    return pl.pallas_call(
        functools.partial(cross_backward_kernel, n, reduce, width // HEAD),
        out_shape=out_shape,
        in_specs=[SM] + [VM] * 4 + [ANY] * 9,
        out_specs=[VM] * len(out_shape),
        scratch_shapes=scratch,
        compiler_params=pltpu.CompilerParams(collective_id=4, has_side_effects=True, vmem_limit_bytes=VLIMIT),
        name="cross_backward",
    )(plot_ids, seg, qct, ct, lse, e2, gb, kk, vv, kt, f, x2, wn, du)


class RowSum:
    def __init__(self, place, mine, refs):
        self.p = place
        self.mine = mine
        self.near, self.far, self.xs, self.xr, self.zs, self.zr = refs
        self.steps = place.n // 2

    @staticmethod
    def scratch(n, shard, width):
        return [pltpu.VMEM((n // 2, shard, width), BF)] * 2 + [DMA((n // 2,))] * 4

    def slot(self, k):
        return lax.rem(self.p.d + 2 * k, self.p.n)

    def xcopy(self, k):
        there = lax.rem(self.p.dx + 2 * k, self.p.n)
        return rcopy(self.mine.at[there], self.near.at[k], self.xs.at[k], self.xr.at[k], self.p.x)

    def zcopy(self, k):
        return rcopy(self.near.at[k], self.far.at[k], self.zs.at[k], self.zr.at[k], self.p.z(k))

    def begin(self):
        for k in list(range(1, self.steps)) + [0]:
            self.xcopy(k).start()

    def step(self, k):
        self.xcopy(k).wait_recv()
        self.near[k] = (self.mine[self.slot(k)].astype(F32) + self.near[k].astype(F32)).astype(BF)
        self.zcopy(k).start()

    def end(self):
        self.xcopy(0).wait_recv()
        total = self.mine[self.p.d].astype(F32) + self.near[0].astype(F32)
        for k in range(1, self.steps):
            self.zcopy(k).wait_recv()
            total = total + self.far[k].astype(F32)
        return total

    def sent(self):
        for k in range(1, self.steps):
            self.zcopy(k).wait_send()
        for k in range(self.steps):
            self.xcopy(k).wait_send()


def squares_of(x):
    return jnp.sum(jnp.sum(x * x, axis=1, keepdims=True), axis=0, keepdims=True)


def lanes(v):
    return jnp.concatenate([v[:, i * 128 : (i + 1) * 128] for i in range(v.shape[1] // 128)], axis=0)


class EveryoneSum:
    def __init__(self, place, refs):
        self.p = place
        self.bt, self.bd, self.ts, self.tr, self.ds, self.dr = refs
        n = place.n
        self.tensor_peers = [(place.d, lax.rem(place.t + k, 4)) for k in range(1, 4)]
        self.dp_peers = [(lax.rem(place.d + k, n), place.t) for k in range(1, n)]

    @staticmethod
    def scratch(n, height):
        return [pltpu.VMEM((4, height, 128), F32), pltpu.VMEM((n, height, 128), F32), DMA((4,)), DMA((4,)), DMA((n,)), DMA((n,))]

    def copies(self, buf, ss, rs, peers):
        return [rcopy(buf.at[0], buf.at[k + 1], ss.at[k + 1], rs.at[k + 1], dev) for k, dev in enumerate(peers)]

    def total(self, buf, copies, me):
        for c in copies:
            c.wait_recv()
        count = len(copies) + 1
        total = buf[lax.rem(me + count, count)]
        for j in range(1, count):
            total = total + buf[lax.rem(me - j + count, count)]
        return total

    def begin(self, mine):
        self.bt[0] = mine
        self.first = self.copies(self.bt, self.ts, self.tr, self.tensor_peers)
        for c in self.first:
            c.start()

    def pass_on(self):
        self.bd[0] = self.total(self.bt, self.first, self.p.t)
        self.second = self.copies(self.bd, self.ds, self.dr, self.dp_peers)
        for c in self.second:
            c.start()

    def end(self):
        total = self.total(self.bd, self.second, self.p.d)
        for c in self.first + self.second:
            c.wait_send()
        return total


def self_backward_kernel(n, reduce, heads, x0_ref, gain_ref, dgain2_ref, seg_ref, dqc_ref,
                         x1_hbm, g2_hbm, dk_hbm, dv_hbm, du_hbm, e2_hbm, h1_hbm, h0_hbm, m_hbm, ga_hbm, gb_hbm, c_hbm, a_hbm, qkv_hbm, qkvt_hbm,
                         at_hbm, lse_hbm, wa3_hbm, *rest):
    rest = list(rest)

    def take(count):
        got = rest[:count]
        del rest[:count]
        return got

    p = Place(n)
    tile, width_d = x0_ref.shape
    width = heads * HEAD
    if reduce:
        res_ref, mem_ref, stat_ref = take(3)
        own_outs = take(4)
        mine_r, mine_b, mine_o, mine_a = take(4)
        sums = [RowSum(p, m, take(6)) for m in (mine_r, mine_b, mine_o, mine_a)]
        rest_r, rest_b, rest_o, rest_a = sums
        early, late = EveryoneSum(p, take(6)), EveryoneSum(p, take(6))
    else:
        res_ref, mem_ref, stat_ref, mine_r, mine_b, mine_o, mine_a = take(7)
    ga, gb, c, a, qkv, qkvt, att, lse, wa3, x1, g2, dk_in, dv_in, du_own = take(14)
    ring, e1, dqkv, dka, dva, tr, lsem, rsem = take(8)
    length = e1.shape[0]
    tiles = length // tile
    pairs = [(wa3_hbm, wa3), (gb_hbm, gb), (c_hbm, c), (a_hbm, a), (qkv_hbm, qkv), (qkvt_hbm, qkvt),
             (at_hbm, att), (lse_hbm, lse), (ga_hbm, ga), (du_hbm, du_own)]
    first = [pltpu.make_async_copy(s, d, lsem.at[len(pairs) + i])
             for i, (s, d) in enumerate(((dk_hbm, dk_in), (dv_hbm, dv_in), (x1_hbm, x1), (g2_hbm, g2)))]
    loads = [pltpu.make_async_copy(s, d, lsem.at[i]) for i, (s, d) in enumerate(pairs)]
    states = dk_in.shape[0]
    wanted = [m_hbm.at[i * length : (i + 1) * length] for i in range(states // length)] + [h1_hbm, e2_hbm, h0_hbm]
    turns = [pltpu.make_async_copy(s, ring.at[i % 2], rsem.at[i % 2]) for i, s in enumerate(wanted)]
    loads[1].start()
    first[0].start()
    first[1].start()
    turns[0].start()
    loads[0].start()
    first[2].start()
    first[3].start()
    for load in loads[2:]:
        load.start()

    def turn(i):
        turns[i].wait()
        if i + 1 < len(turns):
            turns[i + 1].start()
        tr[...] = ring[i % 2].T

    heads_in, hs, hr = take(3)
    exchange = HeadExchange(p, dqc_ref, heads_in, (hs, hr), tile)
    share = CoreShare(p, e1, take(2), tile)
    last = TensorSum(p, take(9))
    ms0, ms1, mr0, mr1, myr, mss, mrs = take(7)
    if reduce:
        greet([p.x] + [p.z(k) for k in range(1, n // 2)] + late.tensor_peers + [
            (lax.rem(p.d + k, n), p.t) for k in range(1, n)
        ])
    else:
        greet([p.core, p.y, (p.d, p.tcy)])
    exchange.begin()

    def pair(k):
        return rows((p.t, p.ty)[k], tile)

    def put(mine, i, value):
        mine[:, :, i * width : (i + 1) * width] = value.astype(BF).reshape(mine.shape[0], -1, width)

    plots = mem_ref.shape[0]
    patches = states // plots
    blocks = patches // 4 // 256

    def mem_part(owner, b):
        at = pl.ds(pl.multiple_of(b // blocks * patches + owner * (patches // 4) + b % blocks * 256, 256), 256)
        return nt(dk_in[at, :], flat(gb)[:, 0:width]) + nt(dv_in[at, :], flat(gb)[:, width : 2 * width])

    total_blocks = plots * blocks
    mc0 = [rcopy(ms0.at[b], mr0.at[b], mss.at[0, b], mrs.at[0, b], p.core) for b in range(total_blocks)]
    mc1 = [rcopy(ms1.at[b], mr1.at[b], mss.at[1, b], mrs.at[1, b], p.core) for b in range(total_blocks)]
    mcy = [rcopy(ms0.at[b], myr.at[b], mss.at[2, b], mrs.at[2, b], p.y) for b in range(total_blocks)]
    loads[1].wait()
    first[0].wait()
    first[1].wait()
    for b in range(total_blocks):
        ms0[b] = mem_part(p.tcy, b).astype(BF)
        mc0[b].start()
    for b in range(total_blocks):
        ms1[b] = mem_part(p.tc, b).astype(BF)
        mc1[b].start()
    for b in range(total_blocks):
        mc0[b].wait_recv()
        mc0[b].wait_send()
        ms0[b] = (mem_part(p.ty, b) + mr0[b].astype(F32)).astype(BF)
        if b + 1 < total_blocks:
            mcy[b].start()

    for i in range(states // length):
        part = slice(i * length, (i + 1) * length)
        turn(i)
        if i == 0:
            dka[...] = nn(tr[...], dk_in[part, :])
            dva[...] = nn(tr[...], dv_in[part, :])
        else:
            dka[...] += nn(tr[...], dk_in[part, :])
            dva[...] += nn(tr[...], dv_in[part, :])
    put(mine_r, 0, dka[...])
    put(mine_r, 1, dva[...])
    if reduce:
        rest_r.begin()

    loads[0].wait()
    first[2].wait()
    first[3].wait()
    g1 = []
    dgain1 = None
    for k in (0, 1):
        exchange.arrive(k)
        dv1, dgain = norm_back(x1[k], gain_ref[1:2, :], exchange.project(k, wa3))
        dgain1 = dgain if k == 0 else dgain1
        g1.append(g2[k] + dv1)
        e1[pair(k), :] = g1[k].astype(BF)
        share.begin(k)
    turn(states // length)
    put(mine_b, 0, nn(tr[...], dqc_ref[...]))
    turn(states // length + 1)
    loads[2].wait()
    put(mine_b, 1, nn(tr[...], c[...]))
    if reduce:
        rest_b.begin()
        early.begin(jnp.concatenate([lanes(dgain1), lanes(dgain2_ref[...]), jnp.zeros((16 - width_d // 64, 128), F32)], axis=0))
        rest_r.step(1)
    for load in loads[3:]:
        load.wait()
    share.end()
    tr[...] = e1[...].T
    put(mine_o, 0, nn(tr[...], a[...]))
    if reduce:
        rest_o.begin()
        for k in range(2, n // 2):
            rest_r.step(k)

    start = segment_starts(seg_ref[...])
    wo = flat(ga)[:, 3 * width : 4 * width]
    for i in range(tiles):
        at = slice(i * tile, (i + 1) * tile)
        keys = (i + 1) * tile
        da = nn(e1[at, :], wo)
        dar = da.astype(BF)
        dat = da.T.astype(BF).astype(F32)
        qt = qkvt[0:width, at].astype(F32) * SCALE
        allowed = causal_mask(keys, tile, i, start[:, at])
        kk = qkv[0:keys, width : 2 * width]
        vv = qkv[0:keys, 2 * width : 3 * width]
        ps, ds, dq = [], [], []
        for h in range(heads):
            hs = slice(h * HEAD, (h + 1) * HEAD)
            inner = jnp.sum(dat[hs, :] * att[hs, at], axis=0, keepdims=True)
            prob = jnp.where(allowed, jnp.exp(nn(kk, head_rows(qt, h)) - lse[h : h + 1, at]), 0.0)
            grad = (prob * (nn(vv, head_rows(dat, h)) - inner)).astype(BF)
            ps.append(prob.astype(BF))
            ds.append(grad)
            dq.append(nn(qkvt[width + h * HEAD : width + (h + 1) * HEAD, 0:keys], grad))
        dqkv[at, 0:width] = (jnp.concatenate(dq, axis=0) * SCALE).T
        dk = nn(jnp.concatenate(ds, axis=1), head_block(qkv[at, 0:width].astype(F32) * SCALE, heads))
        dv = nn(jnp.concatenate(ps, axis=1), head_block(dar.astype(F32), heads))
        if i:
            dqkv[0 : keys - tile, width : 2 * width] += dk[0 : keys - tile]
            dqkv[0 : keys - tile, 2 * width : 3 * width] += dv[0 : keys - tile]
        dqkv[at, width : 2 * width] = dk[keys - tile :]
        dqkv[at, 2 * width : 3 * width] = dv[keys - tile :]
        if reduce and 0 < i < n // 2:
            rest_b.step(i)
    turn(states // length + 2)
    mine_a[...] = nn(tr[...], dqkv[...].astype(BF)).astype(BF).reshape(mine_a.shape)
    if reduce:
        rest_a.begin()
    last.begin(lambda j: nt(dqkv[rows(j, tile), :].astype(BF), flat(ga)[:, 0 : 3 * width]))
    if reduce:
        for k in range(tiles, n // 2):
            rest_b.step(k)
        for k in range(1, n // 2):
            rest_o.step(k)
        for k in range(1, n // 2):
            rest_a.step(k)
    dv0, dgain0 = norm_back(x0_ref[...].astype(F32), gain_ref[0:1, :], last.end())
    res_ref[...] = (g1[0] + dv0).astype(BF)
    tail = lanes(dgain0)
    if reduce:
        squares = squares_of(du_own[...])
        for r, out in zip(sums, own_outs):
            total = r.end()
            out[...] = total
            squares = squares + squares_of(total)
        late.begin(jnp.concatenate([tail, jnp.broadcast_to(squares, (8 - width_d // 128, 128))], axis=0))
    mcy[total_blocks - 1].start()
    if reduce:
        early.pass_on()
        late.pass_on()
    for b in range(total_blocks):
        mc1[b].wait_recv()
        mcy[b].wait_recv()
        own = mem_part(p.t, b) + mr1[b].astype(F32) + myr[b].astype(F32)
        mem_ref[b // blocks, (b % blocks) * 256 : (b % blocks + 1) * 256, :] = own.astype(BF)
    if reduce:
        stat_ref[0:8, :] = late.end()
        stat_ref[8:24, :] = early.end()
        for r in sums:
            r.sent()
    else:
        stat_ref[...] = jnp.concatenate(
            [tail, jnp.zeros((8 - width_d // 128, 128), F32), lanes(dgain1), lanes(dgain2_ref[...]),
             jnp.zeros((16 - width_d // 64, 128), F32)], axis=0)
    exchange.sent()
    for cpy in mc1 + mcy:
        cpy.wait_send()


def call_self_backward(n, reduce, plots, x0, x1, g2, gain, dgain2, seg, dqc, dk, dv, du,
                       e2, h1, h0, mem, ga, gb, c, a, qkv, qkvt, att, lse, wa3):
    _, tile, width_d = x1.shape
    length, width = dqc.shape
    states = mem.shape[0]
    patches = states // plots
    total_blocks = plots * (patches // 4 // 256)
    shard = width_d // n
    widths = (2 * width, 2 * width, width, 3 * width)
    out_shape = [
        sds((tile, width_d), BF),
        sds((plots, patches // 4, width_d), BF),
        sds((24, 128), F32),
    ]
    scratch = []
    if reduce:
        out_shape += [sds((shard, w), F32) for w in widths]
        scratch += [pltpu.VMEM((n, shard, w), BF) for w in widths]
        for w in widths:
            scratch += RowSum.scratch(n, shard, w)
        scratch += EveryoneSum.scratch(n, 16) + EveryoneSum.scratch(n, 8)
    else:
        out_shape += [sds((8, width_d // 8, w), BF) for w in widths]
    scratch += [pltpu.VMEM(v.shape, v.dtype) for v in (ga, gb, c, a, qkv, qkvt, att, lse, wa3, x1, g2, dk, dv, du)]
    scratch += [
        pltpu.VMEM((2, length, width_d), BF),
        pltpu.VMEM((length, width_d), BF),
        pltpu.VMEM((length, 3 * width), F32),
        pltpu.VMEM((width_d, width), F32),
        pltpu.VMEM((width_d, width), F32),
        pltpu.VMEM((width_d, length), BF),
        DMA((14,)),
        DMA((2,)),
    ]
    scratch += HeadExchange.scratch(tile, width) + CoreShare.scratch()
    scratch += TensorSum.scratch(tile, width_d)
    scratch += [pltpu.VMEM((total_blocks, 256, width_d), BF)] * 5 + [DMA((3, total_blocks))] * 2
    return pl.pallas_call(
        functools.partial(self_backward_kernel, n, reduce, width // HEAD),
        out_shape=out_shape,
        in_specs=[VM] * 5 + [ANY] * 18,
        out_specs=[VM] * len(out_shape),
        scratch_shapes=scratch,
        compiler_params=pltpu.CompilerParams(collective_id=3, has_side_effects=True, vmem_limit_bytes=VLIMIT),
        name="self_backward",
    )(x0, gain, dgain2, seg, dqc, x1, g2, dk, dv, du, e2, h1, h0, mem, ga, gb, c, a, qkv, qkvt, att, lse, wa3)


def adam_step(master, moment, second, gradient, step_rate, decay_rate):
    moment_new = BETA_ONE * moment + (1.0 - BETA_ONE) * gradient
    second_new = BETA_TWO * second + (1.0 - BETA_TWO) * gradient * gradient
    moment_hat = moment_new * (1.0 / (1.0 - BETA_ONE**STEP))
    second_hat = second_new * (1.0 / (1.0 - BETA_TWO**STEP))
    master_new = master - step_rate * (
        moment_hat / (jnp.sqrt(second_hat) + ADAM_EPS) + decay_rate * master
    )
    return (master_new, moment_new, second_new)


def update_kernel(width, hidden, *refs):
    stat_ref, u_ref, r_ref, b_ref, o_ref, a_ref = refs[0:6]
    inputs = refs[6:27]
    norm_ref = refs[27]
    outputs = refs[28:54]
    held = refs[54:75]
    copies = refs[75:80]
    lsem, osem = refs[80:82]
    loads = [pltpu.make_async_copy(s, d, lsem.at[i]) for i, (s, d) in enumerate(zip(inputs, held))]
    for load in loads:
        load.start()
    put = Puts(osem)
    count = inputs[15].shape[1] // 128
    gains = jnp.concatenate(
        [jnp.concatenate([stat_ref[at + i : at + i + 1, :] for i in range(count)], axis=1) for at in (0, 8, 8 + count)],
        axis=0,
    )
    grad_norm = jnp.sqrt(stat_ref[count : count + 1, 0:1] + squares_of(gains))
    norm_ref[...] = grad_norm
    factor = jnp.minimum(1.0, CLIP / (grad_norm + 1e-06))

    def columns(ref, i, size):
        return ref[:, i * size : (i + 1) * size]

    grads = (
        [columns(a_ref, 0, width), columns(a_ref, 1, width), columns(a_ref, 2, width), columns(b_ref, 0, width)],
        [columns(r_ref, 0, width), columns(r_ref, 1, width)],
        [o_ref[...].T, columns(b_ref, 1, width).T],
        [columns(u_ref, 0, hidden), columns(u_ref, 1, hidden)],
        [columns(u_ref, 2, hidden)],
        [gains],
    )
    rates = (RATE_INNER, RATE_INNER, RATE_OUTER, RATE_INNER, RATE_INNER, RATE_GAIN)
    for group, (parts, rate) in enumerate(zip(grads, rates)):
        mine = held[3 * group : 3 * group + 3]
        master, moment, second = mine
        for load in loads[3 * group : 3 * group + 3]:
            load.wait()
        for i, g in enumerate(parts):
            at = i if len(master.shape) == 3 else Ellipsis
            new = adam_step(master[at], moment[at], second[at], g * factor, rate, DECAY if group < 5 else 0.0)
            for ref, value in zip(mine, new):
                ref[at] = value
            if group < 5:
                copies[group][at] = new[0].astype(BF)
        for ref, out in zip(mine + copies[group : group + 1], outputs[4 * group : 4 * group + 4]):
            put(ref, out)
    for load, ref, out in zip(loads[18:21], held[18:21], outputs[23:26]):
        load.wait()
        put(ref, out)
    put.end()


def call_update(stat, own, weights, passed):
    flat_weights = [w for group in weights for w in group]
    late = []
    for group in weights[0:5]:
        late += [sds(group[0].shape, F32)] * 3 + [sds(group[0].shape, BF)]
    late += [sds(weights[5][0].shape, F32)] * 3
    late += [sds(v.shape, BF) for v in passed]
    inputs = list(flat_weights) + list(passed)
    return pl.pallas_call(
        functools.partial(update_kernel, weights[0][0].shape[2], weights[3][0].shape[2]),
        out_shape=[sds((1, 1), F32)] + late,
        in_specs=[VM] * 6 + [ANY] * 21,
        out_specs=[VM] + [ANY] * 26,
        scratch_shapes=[pltpu.VMEM(v.shape, v.dtype) for v in inputs]
        + [pltpu.VMEM(group[0].shape, BF) for group in weights[0:5]]
        + [DMA((21,)), DMA((26,))],
        compiler_params=pltpu.CompilerParams(vmem_limit_bytes=VLIMIT),
        name="update",
    )(stat, *own, *inputs)


def local(
    n,
    residual,
    cotangent,
    memory,
    segment_ids,
    plot_ids,
    attend_weight,
    attend_first,
    attend_second,
    recall_weight,
    recall_first,
    recall_second,
    outward_weight,
    outward_first,
    outward_second,
    expand_weight,
    expand_first,
    expand_second,
    narrow_weight,
    narrow_first,
    narrow_second,
    gain_weight,
    gain_first,
    gain_second,
):
    _, plots, patches, width_d = memory.shape
    shard = attend_weight.shape[1]
    aligned = shard % 16 == 0
    length = segment_ids.shape[1]

    def by_rows(w):
        return jnp.transpose(w, (1, 0, 2)).reshape(w.shape[1], -1)

    if aligned:
        shards = (attend_weight, recall_weight, outward_weight, expand_weight, narrow_weight.T)
    else:
        out_rows = jnp.transpose(outward_weight, (2, 0, 1))
        shards = (
            jnp.concatenate([by_rows(attend_weight[0:3]), out_rows[:, 0]], axis=1),
            by_rows(recall_weight),
            jnp.concatenate([attend_weight[3], out_rows[:, 1]], axis=1),
            by_rows(expand_weight),
            narrow_weight.T,
        )
        shards = tuple(
            lax.all_gather(s.astype(BF), "dp", axis=0, tiled=True).reshape(8, width_d // 8, s.shape[1]) for s in shards
        )
    mem = memory.reshape(plots * patches, width_d)
    x0 = residual[0]
    plot_row = plot_ids.reshape(-1)
    outs = call_first(
        n, aligned, plot_row, x0, cotangent[0], gain_weight, segment_ids, shards, mem
    )
    lse, qct, c, ct, lse_c, qkv, qkvt, a, att, x1, ga, gr, gb, gc, wn, h0, h1, e3, kk, vv, kt, wo1, wa3 = outs
    dgain2, f, g2, e2, du, x2 = call_ffn(n, c, x1, gain_weight, wo1, gc, wn, e3)
    outs = call_cross_backward(n, aligned, plot_row, segment_ids, e2, gb, qct, kk, vv, kt, ct, lse_c, f, x2, wn, du)
    dqc, dk, dv, block_out = outs[0:4]
    own_u = outs[4] if aligned else du[0 : width_d // n].astype(F32)
    outs = call_self_backward(
        n, aligned, plots, x0, x1, g2, gain_weight, dgain2, segment_ids, dqc, dk, dv, own_u,
        e2, h1, h0, mem, ga, gr, c, a, qkv, qkvt, att, lse, wa3
    )
    residual_grad, memory_grad, stat = outs[0:3]
    if aligned:
        own = (own_u,) + tuple(outs[3:7])
    else:
        own = tuple(
            lax.psum_scatter(g.reshape(width_d, -1).astype(F32), "dp", scatter_dimension=0, tiled=True)
            for g in (du,) + tuple(outs[3:7])
        )
        squares = sum(jnp.sum(g * g) for g in own)
        stat = lax.psum(stat.at[width_d // 128, :].set(squares), ("dp", "tensor"))
    weights = (
        (attend_weight, attend_first, attend_second),
        (recall_weight, recall_first, recall_second),
        (outward_weight, outward_first, outward_second),
        (expand_weight, expand_first, expand_second),
        (narrow_weight.T, narrow_first.T, narrow_second.T),
        (gain_weight, gain_first, gain_second),
    )
    new = call_update(stat, own, weights, (block_out, residual_grad, memory_grad))
    narrow_new = tuple(v.T for v in new[17:21])
    return (
        (new[24][None], new[25][None], new[26][None], new[0].reshape(())) + tuple(new[1:17]) + narrow_new + tuple(new[21:24])
    )


def solution(mesh):
    rows_in = P("dp", "tensor", None)
    inner = P(None, "dp", "tensor")
    outer = P(None, "tensor", "dp")
    narrow = P("tensor", "dp")
    in_specs = (
        (rows_in, rows_in, P("dp", None, None, None), P("dp", None), P("dp", None))
        + (inner,) * 3
        + (inner,) * 3
        + (outer,) * 3
        + (inner,) * 3
        + (narrow,) * 3
        + (P(),) * 3
    )
    out_specs = (
        (rows_in, rows_in, P("dp", None, "tensor", None), P())
        + (inner,) * 4
        + (inner,) * 4
        + (outer,) * 4
        + (inner,) * 4
        + (narrow,) * 4
        + (P(),) * 3
    )
    return jax.shard_map(
        functools.partial(local, mesh.shape["dp"]),
        mesh=mesh,
        in_specs=in_specs,
        out_specs=out_specs,
        check_vma=False,
    )
```

```python
import functools

import jax
import jax.numpy as jnp
from jax import lax
from jax.experimental import pallas as pl
from jax.experimental.pallas import tpu as pltpu
from jax.sharding import PartitionSpec as P

HEAD = 64
SEGS = 4
STEP = 10
NORM_EPS = 1e-06
ADAM_EPS = 1e-08
BETA_ONE = 0.9
BETA_TWO = 0.999
DECAY = 0.1
RATE_INNER = 0.05
RATE_OUTER = 0.4
RATE_GAIN = 0.5
CLIP = 1.0
MASKED = -1e30
SCALE = HEAD ** (-0.5)

MESH = pl.DeviceIdType.MESH
BF = jnp.bfloat16
F32 = jnp.float32
VLIMIT = 62 * 2**20
VM = pl.BlockSpec(memory_space=pltpu.VMEM)
ANY = pl.BlockSpec(memory_space=pl.ANY)
SM = pl.BlockSpec(memory_space=pltpu.SMEM)
DMA = pltpu.SemaphoreType.DMA


def sds(shape, dtype):
    return jax.ShapeDtypeStruct(shape, dtype)


def nn(a, b):
    return lax.dot_general(a, b, (((1,), (0,)), ((), ())), preferred_element_type=F32)


def nt(a, b):
    return lax.dot_general(a, b, (((1,), (1,)), ((), ())), preferred_element_type=F32)


def rows(i, size):
    return pl.ds(pl.multiple_of(i * size, size), size)


def flat(ref):
    return ref[...].reshape(ref.shape[0] * ref.shape[1], ref.shape[2])


def norm(v, g):
    return v * lax.rsqrt(jnp.mean(v * v, axis=-1, keepdims=True) + NORM_EPS) * g


def norm_back(v, g, dy):
    r = lax.rsqrt(jnp.mean(v * v, axis=-1, keepdims=True) + NORM_EPS)
    n = v * r
    dn = dy * g
    dv = r * (dn - n * jnp.mean(dn * n, axis=-1, keepdims=True))
    return dv, jnp.sum(dy * n, axis=0, keepdims=True)


class Place:
    def __init__(self, n):
        self.n = n
        self.d = lax.axis_index("dp")
        self.t = lax.axis_index("tensor")
        self.tc = self.t + 1 - 2 * lax.rem(self.t, 2)
        self.ty = lax.rem(self.t + 2, 4)
        self.tcy = lax.rem(self.tc + 2, 4)
        self.core = (self.d, self.tc)
        self.y = (self.d, self.ty)
        self.dx = self.d + 1 - 2 * lax.rem(self.d, 2)
        self.x = (self.dx, self.t)

    def z(self, k):
        return (lax.rem(self.d + 2 * k, self.n), self.t)

    def from_z(self, k):
        return lax.rem(self.d - 2 * k + 2 * self.n, self.n)

    def x_from_z(self, k):
        return lax.rem(self.dx - 2 * k + 2 * self.n, self.n)


def greet(devices):
    bar = pltpu.get_barrier_semaphore()
    for dev in devices:
        pl.semaphore_signal(bar, inc=1, device_id=dev, device_id_type=MESH)
    pl.semaphore_wait(bar, len(devices))


class Puts:
    def __init__(self, sems):
        self.sems = sems
        self.all = []

    def __call__(self, src, dst):
        c = pltpu.make_async_copy(src, dst, self.sems.at[len(self.all)])
        c.start()
        self.all.append(c)

    def end(self):
        for c in self.all:
            c.wait()


def rcopy(src, dst, ss, rs, dev):
    return pltpu.make_async_remote_copy(
        src_ref=src, dst_ref=dst, send_sem=ss, recv_sem=rs, device_id=dev, device_id_type=MESH
    )


class TensorSum:
    def __init__(self, place, refs):
        self.p = place
        self.s0, self.s1, self.r0, self.r1, self.own, self.ys, self.yr, self.ss, self.rs = refs

    @staticmethod
    def scratch(tile, width, hop=F32):
        return [pltpu.VMEM((tile, width), hop)] * 4 + [
            pltpu.VMEM((tile, width), F32),
            pltpu.VMEM((tile, width), BF),
            pltpu.VMEM((tile, width), BF),
            DMA((3,)),
            DMA((3,)),
        ]

    def begin(self, tile_fn):
        self.send(tile_fn)
        self.pass_on(tile_fn)

    def send(self, tile_fn):
        p = self.p
        self.c0 = rcopy(self.s0, self.r0, self.ss.at[0], self.rs.at[0], p.core)
        self.c1 = rcopy(self.s1, self.r1, self.ss.at[1], self.rs.at[1], p.core)
        self.cy = rcopy(self.ys, self.yr, self.ss.at[2], self.rs.at[2], p.y)
        self.s0[...] = tile_fn(p.tcy).astype(self.s0.dtype)
        self.c0.start()
        self.s1[...] = tile_fn(p.tc).astype(self.s1.dtype)
        self.c1.start()

    def pass_on(self, tile_fn):
        p = self.p
        part = tile_fn(p.ty)
        self.c0.wait_recv()
        self.ys[...] = (part + self.r0[...].astype(F32)).astype(BF)
        self.cy.start()
        self.own[...] = tile_fn(p.t)

    def end(self):
        self.c1.wait_recv()
        self.cy.wait_recv()
        total = self.own[...] + self.r1[...].astype(F32) + self.yr[...].astype(F32)
        self.c0.wait_send()
        self.c1.wait_send()
        self.cy.wait_send()
        return total


class TensorGather:
    def __init__(self, place, full, sems):
        self.p = p = place
        self.full = full
        ss, rs = sems
        mine, far, near, cross = (full.at[i] for i in (p.t, p.ty, p.tc, p.tcy))
        self.cc = rcopy(mine, mine, ss.at[0], rs.at[0], p.core)
        self.cy = rcopy(mine, mine, ss.at[1], rs.at[1], p.y)
        self.cf = rcopy(far, far, ss.at[2], rs.at[2], p.core)
        self.wc = rcopy(near, near, ss.at[0], rs.at[0], p.core)
        self.wy = rcopy(far, far, ss.at[1], rs.at[1], p.y)
        self.wf = rcopy(cross, cross, ss.at[2], rs.at[2], p.core)

    @staticmethod
    def scratch():
        return [DMA((3,)), DMA((3,))]

    def begin(self, own):
        self.full[self.p.t] = own
        self.cy.start()
        self.cc.start()

    def forward(self):
        self.wy.wait_recv()
        self.cf.start()

    def end(self):
        self.wc.wait_recv()
        self.wf.wait_recv()
        self.cy.wait_send()
        self.cc.wait_send()
        self.cf.wait_send()


class TileSwap:
    def __init__(self, place, full, sems, tile):
        self.p = p = place
        ss, rs = sems
        mine = full.at[rows(p.t, tile)]
        far = full.at[rows(p.ty, tile)]
        self.out = rcopy(mine, mine, ss.at[0], rs.at[0], p.y)
        self.back = rcopy(far, far, ss.at[0], rs.at[0], p.y)

    @staticmethod
    def scratch():
        return [DMA((1,)), DMA((1,))]

    def begin(self):
        self.out.start()

    def end(self):
        self.back.wait_recv()
        self.out.wait_send()


class CoreShare:
    def __init__(self, place, full, sems, tile):
        self.p = p = place
        ss, rs = sems
        self.out = [rcopy(full.at[rows(i, tile)], full.at[rows(i, tile)], ss.at[k], rs.at[k], p.core)
                    for k, i in enumerate((p.t, p.ty))]
        self.back = [rcopy(full.at[rows(i, tile)], full.at[rows(i, tile)], ss.at[k], rs.at[k], p.core)
                     for k, i in enumerate((p.tc, p.tcy))]

    @staticmethod
    def scratch():
        return [DMA((2,)), DMA((2,))]

    def begin(self, k):
        self.out[k].start()

    def arrive(self, k):
        self.back[k].wait_recv()

    def sent(self):
        for c in self.out:
            c.wait_send()

    def end(self):
        self.arrive(0)
        self.arrive(1)
        self.sent()


class HeadExchange:
    def __init__(self, place, own, got, sems, tile):
        self.p = p = place
        self.own, self.got, self.tile = own, got, tile
        ss, rs = sems
        peers = ((p.core, (p.tc, p.tcy), p.tc), (p.y, (p.ty, p.t), p.ty), ((p.d, p.tcy), (p.tcy, p.tc), p.tcy))
        self.out = [[rcopy(own.at[rows(tiles[k], tile)], got.at[p.t, k], ss.at[i, k], rs.at[i, k], dev) for k in (0, 1)]
                    for i, (dev, tiles, _) in enumerate(peers)]
        self.back = [[rcopy(got.at[src, k], got.at[src, k], ss.at[i, k], rs.at[i, k], dev) for k in (0, 1)]
                     for i, (dev, _, src) in enumerate(peers)]

    @staticmethod
    def scratch(tile, width):
        return [pltpu.VMEM((4, 2, tile, width), BF), DMA((3, 2)), DMA((3, 2))]

    def begin(self):
        for k in (0, 1):
            for i in (1, 2, 0):
                self.out[i][k].start()
        self.got[self.p.t, 0] = self.own[rows(self.p.t, self.tile), :]
        self.got[self.p.t, 1] = self.own[rows(self.p.ty, self.tile), :]

    def arrive(self, k):
        for i in (0, 1, 2):
            self.back[i][k].wait_recv()

    def sent(self):
        for group in self.out:
            for c in group:
                c.wait_send()

    def project(self, k, weights):
        total = nt(self.got[0, k], weights[0])
        for s in range(1, 4):
            total = total + nt(self.got[s, k], weights[s])
        return total


class ChipSum:
    def __init__(self, place, refs):
        self.p = p = place
        self.s, self.r, self.ys, self.yr, self.ss, self.rs = refs
        self.core = [rcopy(self.s.at[k], self.r.at[k], self.ss.at[k], self.rs.at[k], p.core) for k in (0, 1)]
        self.y = [rcopy(self.ys.at[k], self.yr.at[1 - k], self.ss.at[2 + k], self.rs.at[3 - k], p.y) for k in (0, 1)]
        self.yback = [rcopy(self.ys.at[k], self.yr.at[k], self.ss.at[2 + k], self.rs.at[2 + k], p.y) for k in (0, 1)]

    @staticmethod
    def scratch(tile, width, hop=F32):
        return [pltpu.VMEM((2, tile, width), hop)] * 2 + [pltpu.VMEM((2, tile, width), BF)] * 2 + [DMA((4,)), DMA((4,))]

    def send(self, k, tile_fn):
        self.s[k] = tile_fn((self.p.tc, self.p.tcy)[k]).astype(self.s.dtype)
        self.core[k].start()

    def pass_on(self, k, tile_fn):
        part = tile_fn((self.p.t, self.p.ty)[k])
        self.core[k].wait_recv()
        self.ys[k] = (part + self.r[k].astype(F32)).astype(BF)
        self.y[k].start()

    def end(self, k):
        self.yback[k].wait_recv()
        return self.ys[k].astype(F32) + self.yr[k].astype(F32)

    def sent(self):
        for c in self.core + self.y:
            c.wait_send()


class RowGather:
    def __init__(self, place, full, sems):
        self.p = place
        self.full = full
        self.zs, self.zr, self.xs, self.xr = sems
        self.steps = place.n // 2

    @staticmethod
    def scratch(n):
        return [DMA((n // 2,))] * 4

    def zcopy(self, k, slot):
        return rcopy(self.full.at[slot], self.full.at[slot], self.zs.at[k], self.zr.at[k], self.p.z(k))

    def xcopy(self, k, slot):
        return rcopy(self.full.at[slot], self.full.at[slot], self.xs.at[k], self.xr.at[k], self.p.x)

    def begin_far(self):
        for k in range(1, self.steps):
            self.zcopy(k, self.p.d).start()

    def begin_near(self):
        self.xcopy(0, self.p.d).start()

    def sent(self):
        for k in range(1, self.steps):
            self.zcopy(k, self.p.d).wait_send()

    def forward(self, k):
        slot = self.p.from_z(k)
        self.zcopy(k, slot).wait_recv()
        self.xcopy(k, slot).start()

    def forward_all(self):
        for k in range(1, self.steps):
            self.forward(k)

    def end(self):
        for k in range(self.steps):
            self.xcopy(k, self.p.x_from_z(k)).wait_recv()
            self.xcopy(k, self.p.from_z(k)).wait_send()


def head_rows(qt, head):
    ids = lax.broadcasted_iota(jnp.int32, qt.shape, 0)
    return jnp.where((ids >= head * HEAD) & (ids < (head + 1) * HEAD), qt, 0.0).astype(BF)


def head_block(x, heads):
    ids = lax.broadcasted_iota(jnp.int32, x.shape, 1)
    return jnp.concatenate(
        [jnp.where((ids >= h * HEAD) & (ids < (h + 1) * HEAD), x, 0.0).astype(BF) for h in range(heads)], axis=0
    )


def segment_starts(seg):
    start = jnp.zeros(seg.shape, jnp.int32)
    for s in range(SEGS - 1):
        count = jnp.sum(jnp.where(seg == s, 1, 0), axis=1, keepdims=True)
        start = start + jnp.where(seg > s, count, 0)
    return start


def causal_mask(keys, tile, tau, start):
    key_place = lax.broadcasted_iota(jnp.int32, (keys, tile), 0)
    query_place = lax.broadcasted_iota(jnp.int32, (keys, tile), 1) + tau * tile
    return (key_place <= query_place) & (key_place >= start)


def plot_order(seg, plot_ref):
    counts = [jnp.sum(jnp.where(seg == s, 1, 0), axis=1, keepdims=True) for s in range(SEGS)]
    place = lax.broadcasted_iota(jnp.int32, seg.shape, 1)
    first = jnp.zeros((1, 1), jnp.int32)
    for s in range(SEGS):
        shift = jnp.zeros((1, 1), jnp.int32)
        for o in range(SEGS):
            if o != s:
                ahead = plot_ref[o] < plot_ref[s] if o > s else plot_ref[o] <= plot_ref[s]
                shift = shift + counts[o] * (ahead.astype(jnp.int32) - (1 if o < s else 0))
        place = place + jnp.where(seg == s, shift, 0)
        first = first + counts[s] * (plot_ref[s] == 0).astype(jnp.int32)
    return place, first


def order_tile(place, i, tile):
    spot = lax.broadcasted_iota(jnp.int32, (tile, place.shape[1]), 0) + i * tile
    return jnp.where(place == spot, 1.0, 0.0).astype(BF)


class Slots:
    tile = 256

    def __init__(self, place, first):
        self.place = place
        self.split = jnp.sum(first)
        self.zero_tiles = lax.div(self.split + (self.tile - 1), self.tile)
        self.shared = self.zero_tiles - lax.div(self.split, self.tile)
        self.count = place.shape[1] // self.tile + 1

    def at(self, s):
        plot = (s >= self.zero_tiles).astype(jnp.int32)
        i = s - plot * self.shared
        spot = lax.broadcasted_iota(jnp.int32, (1, self.tile), 1) + i * self.tile
        side = (spot >= self.split).astype(jnp.int32)
        counts = (side == plot) & (spot < self.place.shape[1])
        return plot, order_tile(self.place, i, self.tile), counts


def first_kernel(n, gather, heads, plot_ref, x0_ref, cot_ref, gain_ref, seg_ref, *more):
    more = list(more)
    weights = [more.pop(0) for _ in range(5)]
    (m_hbm, lse_ref, qct_ref, c_ref, ct_ref, lsec_ref, qkv_out, qkvt_out, a_out, at_out, x1_out, ga_out,
     gr_out, gb_out, gc_out, gd_out, h0_out, h1_out, e3_out, kk_out, vv_out, kt_out, wo1_out, wa3_out, qkv_ref, qkvt_ref, a_ref, at_ref, x1_ref,
     ga, gr, gb, gc, gd, h0, h1, e3, kk, vv, kt, wo0, wo1, wa3, xf, m_ref, vte, ctok, score, raised, lsem, osem), rest = more[:51], more[51:]

    def take(count):
        got = rest[:count]
        del rest[:count]
        return got

    p = Place(n)
    tile = x0_ref.shape[0]
    width = heads * HEAD
    tiles = h0.shape[0] // tile
    load_m = pltpu.make_async_copy(m_hbm, m_ref, lsem.at[0])
    load_m.start()
    swaps = [TileSwap(p, full, take(2), tile) for full in (xf, e3)]
    shares = [CoreShare(p, full, take(2), tile) for full in (h0, e3, h1)]
    spreads = [TensorGather(p, full, take(2)) for full in (wo0, wo1, wa3)]
    heads_in, hs, hr = take(3)
    exchange = HeadExchange(p, a_ref, heads_in, (hs, hr), tile)
    xf[rows(p.t, tile), :] = x0_ref[...]
    e3[rows(p.t, tile), :] = cot_ref[...]
    if gather:
        parts = [RowGather(p, full, take(4)) for full in (ga, gr, gb, gc, gd)]
        part_a, part_r, part_b, part_c, part_d = parts
        aw, rw, ow, ew, nw = weights

        def fill(full, *mats):
            full[p.d] = jnp.concatenate(mats, axis=1).astype(BF)

        fill(ga, aw[0], aw[1], aw[2], ow[0].T)
        greet([p.core, p.y, (p.d, p.tcy), p.x] + [p.z(k) for k in range(1, n // 2)])
        swaps[0].begin()
        part_a.begin_near()
        part_a.begin_far()
        fill(gr, rw[0], rw[1])
        fill(gb, aw[3], ow[1].T)
        fill(gc, ew[0], ew[1])
        gd[p.d] = nw[...].astype(BF)
    else:
        copies = [pltpu.make_async_copy(s, f, lsem.at[1 + i]) for i, (s, f) in
                  enumerate(zip(weights, (ga, gr, gb, gc, gd)))]
        for c in copies:
            c.start()
        greet([p.core, p.y, (p.d, p.tcy)])
        swaps[0].begin()

    def normed(v, i):
        return norm(v, gain_ref[i : i + 1, :]).astype(BF)

    def pair(k):
        return rows((p.t, p.ty)[k], tile)

    h0[pair(0), :] = normed(x0_ref[...].astype(F32), 0)
    shares[0].begin(0)
    start = segment_starts(seg_ref[...])
    states = kk.shape[0]
    ext = HEAD + 16
    for h in range(heads):
        vte[h * ext + HEAD : (h + 1) * ext, :] = jnp.ones((16, states), BF)
    ctok[...] = jnp.zeros(ctok.shape, F32)
    lsec_ref[...] = jnp.zeros(lsec_ref.shape, F32)
    swaps[0].end()
    swaps[1].begin()
    h0[pair(1), :] = normed(xf[pair(1), :].astype(F32), 0)
    shares[0].begin(1)
    if gather:
        part_a.forward_all()
        part_r.begin_near()
        part_r.begin_far()
        part_b.begin_far()
    shares[0].end()
    if gather:
        part_a.end()
    else:
        for c in copies:
            c.wait()
    spreads[0].begin(flat(ga)[:, 3 * width : 4 * width])

    wa = flat(ga)
    for i in range(tiles):
        at = slice(i * tile, (i + 1) * tile)
        x = nn(h0[at, :], wa[:, : 3 * width])
        qkv_ref[at, :] = x.astype(BF)
        qkvt_ref[:, at] = x.T.astype(BF)
    put = Puts(osem)
    put(ga, ga_out)
    put(h0, h0_out)
    put(qkv_ref, qkv_out)
    put(qkvt_ref, qkvt_out)
    swaps[1].end()
    shares[1].begin(0)
    shares[1].begin(1)
    if gather:
        part_c.begin_far()

    for i in range(tiles):
        at = slice(i * tile, (i + 1) * tile)
        keys = (i + 1) * tile
        own_keys = qkv_ref[0:keys, width : 2 * width]
        qt = qkvt_ref[0:width, at].astype(F32) * SCALE
        allowed = causal_mask(keys, tile, i, start[:, at])
        for h in range(heads):
            s = jnp.where(allowed, nn(own_keys, head_rows(qt, h)), MASKED)
            peak = jnp.max(s, axis=0, keepdims=True)
            e = jnp.exp(s - peak)
            total = jnp.sum(e, axis=0, keepdims=True)
            w = (e * (1.0 / total)).astype(BF)
            vt = qkvt_ref[2 * width + h * HEAD : 2 * width + (h + 1) * HEAD, 0:keys]
            at_ref[h * HEAD : (h + 1) * HEAD, at] = nn(vt, w)
            lse_ref[h : h + 1, at] = peak + jnp.log(total)
        a_ref[at, :] = at_ref[:, at].T.astype(BF)
        if i == 1:
            spreads[0].forward()
        if gather and i < 3:
            part_r.forward(i + 1)
    exchange.begin()
    put(a_ref, a_out)
    put(at_ref, at_out)
    if gather:
        for k in range(4, n // 2):
            part_r.forward(k)
        part_b.begin_near()
        part_b.forward_all()
    shares[1].end()
    put(e3, e3_out)
    spreads[0].end()
    if gather:
        part_c.begin_near()
        part_r.end()
        part_d.begin_far()
    put(gr, gr_out)
    load_m.wait()
    mtiles = m_ref.shape[0] // 256

    def project_memory(i, carry):
        at = rows(i, 256)
        x = nn(m_ref[at, :], flat(gr))
        kk[at, :] = x[:, 0:width].astype(BF)
        vv[at, :] = x[:, width : 2 * width].astype(BF)
        xt = x.T.astype(BF)
        kt[:, at] = xt[0:width]
        for h in range(heads):
            vte[h * ext : h * ext + HEAD, at] = xt[width + h * HEAD : width + (h + 1) * HEAD]
        return carry

    lax.fori_loop(0, mtiles, project_memory, 0)
    put(kk, kk_out)
    put(vv, vv_out)
    put(kt, kt_out)
    for k in (0, 1):
        exchange.arrive(k)
        if gather:
            part_c.forward(k + 1)
        x1 = xf[pair(k), :].astype(F32) + exchange.project(k, wo0)
        x1_ref[k] = x1
        h1[pair(k), :] = normed(x1, 1)
        shares[2].begin(k)
    put(x1_ref, x1_out)
    if gather:
        for k in range(3, n // 2):
            part_c.forward(k)
        part_d.begin_near()
    if gather:
        part_b.end()
    put(gb, gb_out)
    spreads[1].begin(flat(gb)[:, width : 2 * width])
    spreads[2].begin(flat(gb)[:, 0:width])
    shares[2].end()
    put(h1, h1_out)
    wq = flat(gb)[:, 0:width]
    for i in range(tiles):
        at = slice(i * tile, (i + 1) * tile)
        qct_ref[:, at] = nn(h1[at, :], wq).T.astype(BF)

    patches = states // 2
    slots = Slots(*plot_order(seg_ref[...], plot_ref))

    def one_slot(s, carry):
        plot, order, counts = slots.at(s)
        qt = nt(qct_ref[...], order) * SCALE
        q = [head_rows(qt, h) for h in range(heads)]

        def scores(h, c, peak):
            near, far = slice(c * 256, (c + 1) * 256), slice(patches + c * 256, patches + (c + 1) * 256)
            x = nn(jnp.where(plot == 0, kk[near, :], kk[far, :]), q[h])
            score[h % 2, near] = x
            top = jnp.max(x, axis=0, keepdims=True)
            return top if peak is None else jnp.maximum(peak, top)

        chunks = patches // 256
        peak = None
        for c in range(chunks):
            peak = scores(0, c, peak)
        for h in range(heads):
            ahead = None
            for c in range(chunks):
                if h + 1 < heads:
                    ahead = scores(h + 1, c, ahead)
                near = slice(c * 256, (c + 1) * 256)
                raised[h % 2, near] = jnp.exp(score[h % 2, near] - peak).astype(BF)
            hs = slice(h * ext, (h + 1) * ext)
            acc = nn(jnp.where(plot == 0, vte[hs, 0:patches], vte[hs, patches:states]), raised[h % 2])
            total = acc[HEAD : HEAD + 1, :]
            ct_ref[s, h * HEAD : (h + 1) * HEAD, :] = jnp.where(counts, acc[0:HEAD, :] * (1.0 / total), 0.0)
            lsec_ref[s, h : h + 1, :] = jnp.where(counts, peak + jnp.log(total), -MASKED)
            peak = ahead
        ctok[...] += nn(ct_ref[s].astype(BF), order)
        if gather:
            for k in range(1, n // 2):
                pl.when(s == min(k - 1, slots.count - 1))(functools.partial(part_d.forward, k))

        @pl.when(s == 3)
        def _():
            spreads[1].forward()
            spreads[2].forward()

        return carry

    lax.fori_loop(0, slots.count, one_slot, 0)
    c_ref[...] = ctok[...].T.astype(BF)
    spreads[1].end()
    put(wo1, wo1_out)
    spreads[2].end()
    put(wa3, wa3_out)
    exchange.sent()
    if gather:
        for part in parts:
            part.sent()
        part_c.end()
        part_d.end()
    put(gc, gc_out)
    put(gd, gd_out)
    put.end()


def call_first(n, gather, plot_ids, x0, cot, gain, seg, weights, mem):
    tile, width_d = x0.shape
    length = seg.shape[1]
    states = mem.shape[0]
    if gather:
        width, hidden = weights[0].shape[2], weights[4].shape[1]
    else:
        width, hidden = weights[0].shape[2] // 4, weights[4].shape[2]
    heads = width // HEAD
    shapes = [(8, width_d // 8, w) for w in (4 * width, 2 * width, 2 * width, 2 * hidden, hidden)]
    spread = (4, width_d, width)
    early = [
        sds((length, 3 * width), BF),
        sds((3 * width, length), BF),
        sds((length, width), BF),
        sds((width, length), F32),
        sds((2, tile, width_d), F32),
    ]
    late = [
        sds(shapes[0], BF),
        sds(shapes[1], BF),
        sds(shapes[2], BF),
        sds(shapes[3], BF),
        sds(shapes[4], BF),
        sds((length, width_d), BF),
        sds((length, width_d), BF),
        sds((length, width_d), BF),
        sds((states, width), BF),
        sds((states, width), BF),
        sds((width, states), BF),
        sds(spread, BF),
        sds(spread, BF),
    ]
    out_shape = [
        sds((8, length), F32),
        sds((width, length), BF),
        sds((length, width), BF),
        sds((length // 256 + 1, width, 256), F32),
        sds((length // 256 + 1, 8, 256), F32),
    ] + early + late
    scratch = [pltpu.VMEM(s.shape, s.dtype) for s in early] + [pltpu.VMEM(s, BF) for s in shapes]
    scratch += [pltpu.VMEM((length, width_d), BF)] * 3
    scratch += [
        pltpu.VMEM((states, width), BF),
        pltpu.VMEM((states, width), BF),
        pltpu.VMEM((width, states), BF),
        pltpu.VMEM(spread, BF),
        pltpu.VMEM(spread, BF),
        pltpu.VMEM(spread, BF),
        pltpu.VMEM((length, width_d), BF),
        pltpu.VMEM((states, width_d), BF),
        pltpu.VMEM((heads * (HEAD + 16), states), BF),
        pltpu.VMEM((width, length), F32),
        pltpu.VMEM((2, states // 2, 256), F32),
        pltpu.VMEM((2, states // 2, 256), BF),
        DMA((6,)),
        DMA((len(early + late),)),
    ]
    scratch += TileSwap.scratch() * 2 + CoreShare.scratch() * 3 + TensorGather.scratch() * 3
    scratch += HeadExchange.scratch(tile, width)
    if gather:
        scratch += RowGather.scratch(n) * 5
    shard = VM if gather else ANY
    return pl.pallas_call(
        functools.partial(first_kernel, n, gather, heads),
        out_shape=out_shape,
        in_specs=[SM, VM, VM, VM, VM] + [shard] * len(weights) + [ANY],
        out_specs=[VM] * 5 + [ANY] * len(early + late),
        scratch_shapes=scratch,
        compiler_params=pltpu.CompilerParams(collective_id=1, has_side_effects=True, vmem_limit_bytes=VLIMIT),
        name="attention_forward",
    )(plot_ids, x0, cot, gain, seg, *weights, mem)


def ffn_kernel(n, c_ref, gain_ref, x1_hbm, wo_hbm, gc_hbm, wn_hbm, e3_hbm,
               dgain_ref, f_out, g2_out, e2_out, du_out, x2_out,
               x1, wo, gc, wn, e3, f, g2, e2, du, x2, h2, dg, h2t, e3t, lsem, osem, *rest):
    rest = list(rest)

    def take(count):
        got = rest[:count]
        del rest[:count]
        return got

    p = Place(n)
    _, tile, width_d = x1.shape
    hidden = f.shape[1]
    heads_in, hs, hr = take(3)
    exchange = HeadExchange(p, c_ref, heads_in, (hs, hr), tile)
    shares = [CoreShare(p, full, take(2), tile) for full in (h2, e2)]
    total = ChipSum(p, take(6))
    put = Puts(osem)
    loads = [pltpu.make_async_copy(s, d, lsem.at[i]) for i, (s, d) in
             enumerate(((e3_hbm, e3), (wo_hbm, wo), (x1_hbm, x1), (gc_hbm, gc), (wn_hbm, wn)))]
    for load in loads:
        load.start()
    greet([p.core, p.y, (p.d, p.tcy)])
    exchange.begin()
    loads[0].wait()
    e3t[...] = e3[...].T

    def pair(k):
        return rows((p.t, p.ty)[k], tile)

    def hidden_tile(j):
        at = rows(j, tile)
        gate = nn(h2[at, :], flat(gc)[:, 0:hidden])
        up = nn(h2[at, :], flat(gc)[:, hidden : 2 * hidden])
        df = nn(e3[at, :], flat(wn))
        sq = gate * gate
        th = jnp.tanh(0.7978845608 * gate * (1.0 + 0.044715 * sq))
        half = 0.5 * (1.0 + th)
        act = gate * half
        slope = half + 0.5 * gate * (1.0 - th * th) * (0.7978845608 * (1.0 + 3.0 * 0.044715 * sq))
        f[at, :] = (act * up).astype(BF)
        dg[at, 0:hidden] = (df * up * slope).astype(BF)
        dg[at, hidden : 2 * hidden] = (df * act).astype(BF)

    def back_tile(j):
        return nt(dg[rows(j, tile), :], flat(gc)[:, 0 : 2 * hidden])

    for load in loads[1:]:
        load.wait()
    for k in (0, 1):
        exchange.arrive(k)
        x2[k] = x1[k] + exchange.project(k, wo)
        h2[pair(k), :] = norm(x2[k], gain_ref[2:3, :]).astype(BF)
        shares[0].begin(k)
    put(x2, x2_out)
    for k in (0, 1):
        hidden_tile((p.t, p.ty)[k])
        shares[0].arrive(k)
        hidden_tile((p.tc, p.tcy)[k])
        total.send(k, back_tile)
        if k == 1:
            total.pass_on(0, back_tile)
    total.pass_on(1, back_tile)
    put(f, f_out)
    h2t[...] = h2[...].T
    for i in range(2 * hidden // 256):
        cs = slice(i * 256, (i + 1) * 256)
        du[:, cs] = nn(h2t[...], dg[:, cs]).astype(BF)
    for i in range(hidden // 256):
        cs = slice(i * 256, (i + 1) * 256)
        du[:, 2 * hidden + i * 256 : 2 * hidden + (i + 1) * 256] = nn(e3t[...], f[:, cs]).astype(BF)
    put(du, du_out)
    for k in (0, 1):
        dv, dgain = norm_back(x2[k], gain_ref[2:3, :], total.end(k))
        if k == 0:
            dgain_ref[...] = dgain
        g2[k] = e3[pair(k), :].astype(F32) + dv
        e2[pair(k), :] = g2[k].astype(BF)
        shares[1].begin(k)
    put(g2, g2_out)
    shares[0].sent()
    exchange.sent()
    total.sent()
    shares[1].end()
    put(e2, e2_out)
    put.end()


def call_ffn(n, c, x1, gain, wo, gc, wn, e3):
    _, tile, width_d = x1.shape
    length, width = c.shape
    hidden = gc.shape[2] // 2
    late = [
        sds((length, hidden), BF),
        sds((2, tile, width_d), F32),
        sds((length, width_d), BF),
        sds((width_d, 3 * hidden), BF),
        sds((2, tile, width_d), F32),
    ]
    scratch = [pltpu.VMEM(v.shape, v.dtype) for v in [x1, wo, gc, wn, e3] + late]
    scratch += [
        pltpu.VMEM((length, width_d), BF),
        pltpu.VMEM((length, 2 * hidden), BF),
        pltpu.VMEM((width_d, length), BF),
        pltpu.VMEM((width_d, length), BF),
        DMA((5,)),
        DMA((len(late),)),
    ]
    scratch += HeadExchange.scratch(tile, width) + CoreShare.scratch() * 2 + ChipSum.scratch(tile, width_d)
    return pl.pallas_call(
        functools.partial(ffn_kernel, n),
        out_shape=[sds((1, width_d), F32)] + late,
        in_specs=[VM] * 2 + [ANY] * 5,
        out_specs=[VM] + [ANY] * len(late),
        scratch_shapes=scratch,
        compiler_params=pltpu.CompilerParams(collective_id=2, has_side_effects=True, vmem_limit_bytes=VLIMIT),
        name="ffn",
    )(c, gain, x1, wo, gc, wn, e3)


def cross_backward_kernel(n, reduce, heads, plot_ref, seg_ref, qct_ref, ct_ref, lse_ref, e2_hbm, gb_hbm, kk_hbm, vv_hbm, kt_hbm,
                          f_hbm, x2_hbm, wn_hbm, du_hbm, dqc_ref, dk_out, dv_out, blk_ref, *rest):
    rest = list(rest)

    def take(count):
        got = rest[:count]
        del rest[:count]
        return got

    p = Place(n)
    width = heads * HEAD
    states = kk_hbm.shape[0]
    patches = states // 2
    length = qct_ref.shape[1]
    hidden = f_hbm.shape[1]
    if reduce:
        du_out, mine_u = take(2)
        rest_u = RowSum(p, mine_u, take(6))
    dka, dva, dct_all, dqtok, e2, gb, kk, vv, kt, f, x2, wn, dk_held, dv_held, lsem, osem = take(16)
    tile = x2.shape[0]
    block = TensorSum(p, take(9))
    pairs = [(f_hbm, f), (wn_hbm, wn), (e2_hbm, e2), (gb_hbm, gb), (kk_hbm, kk), (vv_hbm, vv),
             (kt_hbm, kt), (x2_hbm.at[0], x2)]
    if reduce:
        pairs.insert(0, (du_hbm, mine_u))
    loads = [pltpu.make_async_copy(s, d, lsem.at[i]) for i, (s, d) in enumerate(pairs)]
    for load in loads:
        load.start()
    greet([p.core, p.y] + ([p.x] + [p.z(k) for k in range(1, n // 2)] if reduce else []))
    if reduce:
        loads.pop(0).wait()
        rest_u.begin()
    loads[0].wait()
    loads[1].wait()

    def out_tile(j):
        return nt(f[rows(j, tile), :], flat(wn))

    block.send(out_tile)
    dka[...] = jnp.zeros(dka.shape, F32)
    dva[...] = jnp.zeros(dva.shape, F32)
    dqtok[...] = jnp.zeros(dqtok.shape, F32)
    loads[2].wait()
    loads[3].wait()
    wo = flat(gb)[:, width : 2 * width]
    for i in range(length // 256):
        at = slice(i * 256, (i + 1) * 256)
        dct_all[:, at] = nn(e2[at, :], wo).T.astype(BF)
    block.pass_on(out_tile)
    if reduce:
        rest_u.step(1)
    for load in loads[4:]:
        load.wait()
    slots = Slots(*plot_order(seg_ref[...], plot_ref))

    def one_slot(s, carry):
        plot, order, _ = slots.at(s)
        dct = nt(dct_all[...], order)
        qt = nt(qct_ref[...], order) * SCALE
        keys = jnp.where(plot == 0, kk[0:patches, :], kk[patches:states, :])
        values = jnp.where(plot == 0, vv[0:patches, :], vv[patches:states, :])
        ps, ds, dq = [], [], []
        for h in range(heads):
            hs = slice(h * HEAD, (h + 1) * HEAD)
            inner = jnp.sum(dct[hs, :] * ct_ref[s, hs, :], axis=0, keepdims=True)
            prob = jnp.exp(nn(keys, head_rows(qt, h)) - lse_ref[s, h : h + 1, :])
            grad = (prob * (nn(values, head_rows(dct, h)) - inner)).astype(BF)
            ps.append(prob.astype(BF))
            ds.append(grad)
            dq.append(nn(jnp.where(plot == 0, kt[hs, 0:patches], kt[hs, patches:states]), grad))
        dqtok[...] += nn((jnp.concatenate(dq, axis=0) * SCALE).astype(BF), order)
        dv = nn(jnp.concatenate(ps, axis=1), head_block(dct.T, heads))
        dk = nn(jnp.concatenate(ds, axis=1), head_block(qt.T, heads))
        for j in range(2):
            part = slice(j * patches, (j + 1) * patches)
            dva[part, :] += jnp.where(plot == j, dv, 0.0)
            dka[part, :] += jnp.where(plot == j, dk, 0.0)
        if reduce:
            for k in range(1, n // 2):
                if k > 1:
                    pl.when(s == min(k - 2, slots.count - 1))(functools.partial(rest_u.step, k))
        return carry

    lax.fori_loop(0, slots.count, one_slot, 0)
    dqc_ref[...] = dqtok[...].T.astype(BF)
    put = Puts(osem)
    dk_held[...] = dka[...].astype(BF)
    put(dk_held, dk_out)
    dv_held[...] = dva[...].astype(BF)
    put(dv_held, dv_out)
    blk_ref[...] = (x2[...] + block.end()).astype(BF)
    if reduce:
        du_out[...] = rest_u.end()
        rest_u.sent()
    put.end()


def call_cross_backward(n, reduce, plot_ids, seg, e2, gb, qct, kk, vv, kt, ct, lse, f, x2, wn, du):
    width, length = qct.shape
    states = kk.shape[0]
    _, tile, width_d = x2.shape
    out_shape = [
        sds((length, width), BF),
        sds((states, width), BF),
        sds((states, width), BF),
        sds((tile, width_d), BF),
    ]
    scratch = []
    if reduce:
        shard = width_d // n
        out_shape.append(sds((shard, du.shape[1]), F32))
        scratch += [pltpu.VMEM((n, shard, du.shape[1]), BF)] + RowSum.scratch(n, shard, du.shape[1])
        du = du.reshape(n, shard, du.shape[1])
    scratch += [
        pltpu.VMEM((states, width), F32),
        pltpu.VMEM((states, width), F32),
        pltpu.VMEM((width, length), BF),
        pltpu.VMEM((width, length), F32),
        pltpu.VMEM(e2.shape, BF),
        pltpu.VMEM(gb.shape, BF),
        pltpu.VMEM((states, width), BF),
        pltpu.VMEM((states, width), BF),
        pltpu.VMEM((width, states), BF),
        pltpu.VMEM(f.shape, BF),
        pltpu.VMEM((tile, width_d), F32),
        pltpu.VMEM(wn.shape, BF),
        pltpu.VMEM((states, width), BF),
        pltpu.VMEM((states, width), BF),
        DMA((9,)),
        DMA((2,)),
    ] + TensorSum.scratch(tile, width_d, BF)
    return pl.pallas_call(
        functools.partial(cross_backward_kernel, n, reduce, width // HEAD),
        out_shape=out_shape,
        in_specs=[SM] + [VM] * 4 + [ANY] * 9,
        out_specs=[VM, ANY, ANY] + [VM] * (len(out_shape) - 3),
        scratch_shapes=scratch,
        compiler_params=pltpu.CompilerParams(collective_id=4, has_side_effects=True, vmem_limit_bytes=VLIMIT),
        name="cross_backward",
    )(plot_ids, seg, qct, ct, lse, e2, gb, kk, vv, kt, f, x2, wn, du)


class RowSum:
    def __init__(self, place, mine, refs):
        self.p = place
        self.mine = mine
        self.near, self.far, self.xs, self.xr, self.zs, self.zr = refs
        self.steps = place.n // 2

    @staticmethod
    def scratch(n, shard, width):
        return [pltpu.VMEM((n // 2, shard, width), BF)] * 2 + [DMA((n // 2,))] * 4

    def slot(self, k):
        return lax.rem(self.p.d + 2 * k, self.p.n)

    def xcopy(self, k):
        there = lax.rem(self.p.dx + 2 * k, self.p.n)
        return rcopy(self.mine.at[there], self.near.at[k], self.xs.at[k], self.xr.at[k], self.p.x)

    def zcopy(self, k):
        return rcopy(self.near.at[k], self.far.at[k], self.zs.at[k], self.zr.at[k], self.p.z(k))

    def begin(self):
        for k in list(range(1, self.steps)) + [0]:
            self.xcopy(k).start()

    def step(self, k):
        self.xcopy(k).wait_recv()
        self.near[k] = (self.mine[self.slot(k)].astype(F32) + self.near[k].astype(F32)).astype(BF)
        self.zcopy(k).start()

    def end(self):
        self.xcopy(0).wait_recv()
        total = self.mine[self.p.d].astype(F32) + self.near[0].astype(F32)
        for k in range(1, self.steps):
            self.zcopy(k).wait_recv()
            total = total + self.far[k].astype(F32)
        return total

    def sent(self):
        for k in range(1, self.steps):
            self.zcopy(k).wait_send()
        for k in range(self.steps):
            self.xcopy(k).wait_send()


def squares_of(x):
    return jnp.sum(jnp.sum(x * x, axis=1, keepdims=True), axis=0, keepdims=True)


def lanes(v):
    return jnp.concatenate([v[:, i * 128 : (i + 1) * 128] for i in range(v.shape[1] // 128)], axis=0)


class EveryoneSum:
    def __init__(self, place, refs):
        self.p = place
        self.bt, self.bd, self.ts, self.tr, self.ds, self.dr = refs
        n = place.n
        self.tensor_peers = [(place.d, lax.rem(place.t + k, 4)) for k in range(1, 4)]
        self.dp_peers = [(lax.rem(place.d + k, n), place.t) for k in range(1, n)]

    @staticmethod
    def scratch(n, height):
        return [pltpu.VMEM((4, height, 128), F32), pltpu.VMEM((n, height, 128), F32), DMA((4,)), DMA((4,)), DMA((n,)), DMA((n,))]

    def copies(self, buf, ss, rs, peers):
        return [rcopy(buf.at[0], buf.at[k + 1], ss.at[k + 1], rs.at[k + 1], dev) for k, dev in enumerate(peers)]

    def total(self, buf, copies, me):
        for c in copies:
            c.wait_recv()
        count = len(copies) + 1
        total = buf[lax.rem(me + count, count)]
        for j in range(1, count):
            total = total + buf[lax.rem(me - j + count, count)]
        return total

    def begin(self, mine):
        self.bt[0] = mine
        self.first = self.copies(self.bt, self.ts, self.tr, self.tensor_peers)
        for c in self.first:
            c.start()

    def pass_on(self):
        self.bd[0] = self.total(self.bt, self.first, self.p.t)
        self.second = self.copies(self.bd, self.ds, self.dr, self.dp_peers)
        for c in self.second:
            c.start()

    def end(self):
        total = self.total(self.bd, self.second, self.p.d)
        for c in self.first + self.second:
            c.wait_send()
        return total


def self_backward_kernel(n, reduce, heads, x0_ref, gain_ref, dgain2_ref, seg_ref, dqc_ref,
                         x1_hbm, g2_hbm, dk_hbm, dv_hbm, du_hbm, e2_hbm, h1_hbm, h0_hbm, m_hbm, ga_hbm, gb_hbm, c_hbm, a_hbm, qkv_hbm, qkvt_hbm,
                         at_hbm, lse_hbm, wa3_hbm, *rest):
    rest = list(rest)

    def take(count):
        got = rest[:count]
        del rest[:count]
        return got

    p = Place(n)
    tile, width_d = x0_ref.shape
    width = heads * HEAD
    if reduce:
        res_ref, mem_ref, stat_ref = take(3)
        own_outs = take(4)
        mine_r, mine_b, mine_o, mine_a = take(4)
        sums = [RowSum(p, m, take(6)) for m in (mine_r, mine_b, mine_o, mine_a)]
        rest_r, rest_b, rest_o, rest_a = sums
        early, late = EveryoneSum(p, take(6)), EveryoneSum(p, take(6))
    else:
        res_ref, mem_ref, stat_ref, mine_r, mine_b, mine_o, mine_a = take(7)
    ga, gb, c, a, qkv, qkvt, att, lse, wa3, x1, g2, dk_in, dv_in, du_own = take(14)
    ring, e1, dqkv, dka, dva, tr, lsem, rsem = take(8)
    length = e1.shape[0]
    tiles = length // tile
    pairs = [(wa3_hbm, wa3), (gb_hbm, gb), (c_hbm, c), (a_hbm, a), (qkv_hbm, qkv), (qkvt_hbm, qkvt),
             (at_hbm, att), (lse_hbm, lse), (ga_hbm, ga), (du_hbm, du_own)]
    first = [pltpu.make_async_copy(s, d, lsem.at[len(pairs) + i])
             for i, (s, d) in enumerate(((dk_hbm, dk_in), (dv_hbm, dv_in), (x1_hbm, x1), (g2_hbm, g2)))]
    loads = [pltpu.make_async_copy(s, d, lsem.at[i]) for i, (s, d) in enumerate(pairs)]
    states = dk_in.shape[0]
    wanted = [m_hbm.at[i * length : (i + 1) * length] for i in range(states // length)] + [h1_hbm, e2_hbm, h0_hbm]
    turns = [pltpu.make_async_copy(s, ring.at[i % 2], rsem.at[i % 2]) for i, s in enumerate(wanted)]
    loads[1].start()
    first[0].start()
    first[1].start()
    turns[0].start()
    loads[0].start()
    first[2].start()
    first[3].start()
    for load in loads[2:]:
        load.start()

    def turn(i):
        turns[i].wait()
        if i + 1 < len(turns):
            turns[i + 1].start()
        tr[...] = ring[i % 2].T

    heads_in, hs, hr = take(3)
    exchange = HeadExchange(p, dqc_ref, heads_in, (hs, hr), tile)
    share = CoreShare(p, e1, take(2), tile)
    last = TensorSum(p, take(9))
    ms0, ms1, mr0, mr1, myr, mss, mrs = take(7)
    if reduce:
        greet([p.x] + [p.z(k) for k in range(1, n // 2)] + late.tensor_peers + [
            (lax.rem(p.d + k, n), p.t) for k in range(1, n)
        ])
    else:
        greet([p.core, p.y, (p.d, p.tcy)])
    exchange.begin()

    def pair(k):
        return rows((p.t, p.ty)[k], tile)

    def put(mine, i, value):
        mine[:, :, i * width : (i + 1) * width] = value.astype(BF).reshape(mine.shape[0], -1, width)

    plots = mem_ref.shape[0]
    patches = states // plots
    blocks = patches // 4 // 256

    def mem_part(owner, b):
        at = pl.ds(pl.multiple_of(b // blocks * patches + owner * (patches // 4) + b % blocks * 256, 256), 256)
        return nt(dk_in[at, :], flat(gb)[:, 0:width]) + nt(dv_in[at, :], flat(gb)[:, width : 2 * width])

    total_blocks = plots * blocks
    mc0 = [rcopy(ms0.at[b], mr0.at[b], mss.at[0, b], mrs.at[0, b], p.core) for b in range(total_blocks)]
    mc1 = [rcopy(ms1.at[b], mr1.at[b], mss.at[1, b], mrs.at[1, b], p.core) for b in range(total_blocks)]
    mcy = [rcopy(ms0.at[b], myr.at[b], mss.at[2, b], mrs.at[2, b], p.y) for b in range(total_blocks)]
    loads[1].wait()
    first[0].wait()
    first[1].wait()
    for b in range(total_blocks):
        ms0[b] = mem_part(p.tcy, b).astype(BF)
        mc0[b].start()
    for b in range(total_blocks):
        ms1[b] = mem_part(p.tc, b).astype(BF)
        mc1[b].start()
    for b in range(total_blocks):
        mc0[b].wait_recv()
        mc0[b].wait_send()
        ms0[b] = (mem_part(p.ty, b) + mr0[b].astype(F32)).astype(BF)
        if b + 1 < total_blocks:
            mcy[b].start()

    for i in range(states // length):
        part = slice(i * length, (i + 1) * length)
        turn(i)
        if i == 0:
            dka[...] = nn(tr[...], dk_in[part, :])
            dva[...] = nn(tr[...], dv_in[part, :])
        else:
            dka[...] += nn(tr[...], dk_in[part, :])
            dva[...] += nn(tr[...], dv_in[part, :])
    put(mine_r, 0, dka[...])
    put(mine_r, 1, dva[...])
    if reduce:
        rest_r.begin()

    loads[0].wait()
    first[2].wait()
    first[3].wait()
    g1 = []
    dgain1 = None
    for k in (0, 1):
        exchange.arrive(k)
        dv1, dgain = norm_back(x1[k], gain_ref[1:2, :], exchange.project(k, wa3))
        dgain1 = dgain if k == 0 else dgain1
        g1.append(g2[k] + dv1)
        e1[pair(k), :] = g1[k].astype(BF)
        share.begin(k)
    turn(states // length)
    put(mine_b, 0, nn(tr[...], dqc_ref[...]))
    turn(states // length + 1)
    loads[2].wait()
    put(mine_b, 1, nn(tr[...], c[...]))
    if reduce:
        rest_b.begin()
        early.begin(jnp.concatenate([lanes(dgain1), lanes(dgain2_ref[...]), jnp.zeros((16 - width_d // 64, 128), F32)], axis=0))
        rest_r.step(1)
    for load in loads[3:]:
        load.wait()
    share.end()
    tr[...] = e1[...].T
    put(mine_o, 0, nn(tr[...], a[...]))
    if reduce:
        rest_o.begin()
        for k in range(2, n // 2):
            rest_r.step(k)

    start = segment_starts(seg_ref[...])
    wo = flat(ga)[:, 3 * width : 4 * width]
    for i in range(tiles):
        at = slice(i * tile, (i + 1) * tile)
        keys = (i + 1) * tile
        da = nn(e1[at, :], wo)
        dar = da.astype(BF)
        dat = da.T.astype(BF).astype(F32)
        qt = qkvt[0:width, at].astype(F32) * SCALE
        allowed = causal_mask(keys, tile, i, start[:, at])
        kk = qkv[0:keys, width : 2 * width]
        vv = qkv[0:keys, 2 * width : 3 * width]
        ps, ds, dq = [], [], []
        for h in range(heads):
            hs = slice(h * HEAD, (h + 1) * HEAD)
            inner = jnp.sum(dat[hs, :] * att[hs, at], axis=0, keepdims=True)
            prob = jnp.where(allowed, jnp.exp(nn(kk, head_rows(qt, h)) - lse[h : h + 1, at]), 0.0)
            grad = (prob * (nn(vv, head_rows(dat, h)) - inner)).astype(BF)
            ps.append(prob.astype(BF))
            ds.append(grad)
            dq.append(nn(qkvt[width + h * HEAD : width + (h + 1) * HEAD, 0:keys], grad))
        dqkv[at, 0:width] = (jnp.concatenate(dq, axis=0) * SCALE).T
        dk = nn(jnp.concatenate(ds, axis=1), head_block(qkv[at, 0:width].astype(F32) * SCALE, heads))
        dv = nn(jnp.concatenate(ps, axis=1), head_block(dar.astype(F32), heads))
        if i:
            dqkv[0 : keys - tile, width : 2 * width] += dk[0 : keys - tile]
            dqkv[0 : keys - tile, 2 * width : 3 * width] += dv[0 : keys - tile]
        dqkv[at, width : 2 * width] = dk[keys - tile :]
        dqkv[at, 2 * width : 3 * width] = dv[keys - tile :]
        if reduce and 0 < i < n // 2:
            rest_b.step(i)
    turn(states // length + 2)
    mine_a[...] = nn(tr[...], dqkv[...].astype(BF)).astype(BF).reshape(mine_a.shape)
    if reduce:
        rest_a.begin()
    last.begin(lambda j: nt(dqkv[rows(j, tile), :].astype(BF), flat(ga)[:, 0 : 3 * width]))
    if reduce:
        for k in range(tiles, n // 2):
            rest_b.step(k)
        for k in range(1, n // 2):
            rest_o.step(k)
        for k in range(1, n // 2):
            rest_a.step(k)
    dv0, dgain0 = norm_back(x0_ref[...].astype(F32), gain_ref[0:1, :], last.end())
    res_ref[...] = (g1[0] + dv0).astype(BF)
    tail = lanes(dgain0)
    if reduce:
        squares = squares_of(du_own[...])
        for r, out in zip(sums, own_outs):
            total = r.end()
            out[...] = total
            squares = squares + squares_of(total)
        late.begin(jnp.concatenate([tail, jnp.broadcast_to(squares, (8 - width_d // 128, 128))], axis=0))
    mcy[total_blocks - 1].start()
    if reduce:
        early.pass_on()
        late.pass_on()
    for b in range(total_blocks):
        mc1[b].wait_recv()
        mcy[b].wait_recv()
        own = mem_part(p.t, b) + mr1[b].astype(F32) + myr[b].astype(F32)
        mem_ref[b // blocks, (b % blocks) * 256 : (b % blocks + 1) * 256, :] = own.astype(BF)
    if reduce:
        stat_ref[0:8, :] = late.end()
        stat_ref[8:24, :] = early.end()
        for r in sums:
            r.sent()
    else:
        stat_ref[...] = jnp.concatenate(
            [tail, jnp.zeros((8 - width_d // 128, 128), F32), lanes(dgain1), lanes(dgain2_ref[...]),
             jnp.zeros((16 - width_d // 64, 128), F32)], axis=0)
    exchange.sent()
    for cpy in mc1 + mcy:
        cpy.wait_send()


def call_self_backward(n, reduce, plots, x0, x1, g2, gain, dgain2, seg, dqc, dk, dv, du,
                       e2, h1, h0, mem, ga, gb, c, a, qkv, qkvt, att, lse, wa3):
    _, tile, width_d = x1.shape
    length, width = dqc.shape
    states = mem.shape[0]
    patches = states // plots
    total_blocks = plots * (patches // 4 // 256)
    shard = width_d // n
    widths = (2 * width, 2 * width, width, 3 * width)
    out_shape = [
        sds((tile, width_d), BF),
        sds((plots, patches // 4, width_d), BF),
        sds((24, 128), F32),
    ]
    scratch = []
    if reduce:
        out_shape += [sds((shard, w), F32) for w in widths]
        scratch += [pltpu.VMEM((n, shard, w), BF) for w in widths]
        for w in widths:
            scratch += RowSum.scratch(n, shard, w)
        scratch += EveryoneSum.scratch(n, 16) + EveryoneSum.scratch(n, 8)
    else:
        out_shape += [sds((8, width_d // 8, w), BF) for w in widths]
    scratch += [pltpu.VMEM(v.shape, v.dtype) for v in (ga, gb, c, a, qkv, qkvt, att, lse, wa3, x1, g2, dk, dv, du)]
    scratch += [
        pltpu.VMEM((2, length, width_d), BF),
        pltpu.VMEM((length, width_d), BF),
        pltpu.VMEM((length, 3 * width), F32),
        pltpu.VMEM((width_d, width), F32),
        pltpu.VMEM((width_d, width), F32),
        pltpu.VMEM((width_d, length), BF),
        DMA((14,)),
        DMA((2,)),
    ]
    scratch += HeadExchange.scratch(tile, width) + CoreShare.scratch()
    scratch += TensorSum.scratch(tile, width_d)
    scratch += [pltpu.VMEM((total_blocks, 256, width_d), BF)] * 5 + [DMA((3, total_blocks))] * 2
    return pl.pallas_call(
        functools.partial(self_backward_kernel, n, reduce, width // HEAD),
        out_shape=out_shape,
        in_specs=[VM] * 5 + [ANY] * 18,
        out_specs=[VM] * len(out_shape),
        scratch_shapes=scratch,
        compiler_params=pltpu.CompilerParams(collective_id=3, has_side_effects=True, vmem_limit_bytes=VLIMIT),
        name="self_backward",
    )(x0, gain, dgain2, seg, dqc, x1, g2, dk, dv, du, e2, h1, h0, mem, ga, gb, c, a, qkv, qkvt, att, lse, wa3)


def adam_step(master, moment, second, gradient, step_rate, decay_rate):
    moment_new = BETA_ONE * moment + (1.0 - BETA_ONE) * gradient
    second_new = BETA_TWO * second + (1.0 - BETA_TWO) * gradient * gradient
    moment_hat = moment_new * (1.0 / (1.0 - BETA_ONE**STEP))
    second_hat = second_new * (1.0 / (1.0 - BETA_TWO**STEP))
    master_new = master - step_rate * (
        moment_hat / (jnp.sqrt(second_hat) + ADAM_EPS) + decay_rate * master
    )
    return (master_new, moment_new, second_new)


def update_kernel(width, hidden, *refs):
    stat_ref, u_ref, r_ref, b_ref, o_ref, a_ref = refs[0:6]
    inputs = refs[6:27]
    norm_ref = refs[27]
    outputs = refs[28:54]
    held = refs[54:75]
    copies = refs[75:80]
    lsem, osem = refs[80:82]
    loads = [pltpu.make_async_copy(s, d, lsem.at[i]) for i, (s, d) in enumerate(zip(inputs, held))]
    for load in loads:
        load.start()
    put = Puts(osem)
    count = inputs[15].shape[1] // 128
    gains = jnp.concatenate(
        [jnp.concatenate([stat_ref[at + i : at + i + 1, :] for i in range(count)], axis=1) for at in (0, 8, 8 + count)],
        axis=0,
    )
    grad_norm = jnp.sqrt(stat_ref[count : count + 1, 0:1] + squares_of(gains))
    norm_ref[...] = grad_norm
    factor = jnp.minimum(1.0, CLIP / (grad_norm + 1e-06))

    def columns(ref, i, size):
        return ref[:, i * size : (i + 1) * size]

    grads = (
        [columns(a_ref, 0, width), columns(a_ref, 1, width), columns(a_ref, 2, width), columns(b_ref, 0, width)],
        [columns(r_ref, 0, width), columns(r_ref, 1, width)],
        [o_ref[...].T, columns(b_ref, 1, width).T],
        [columns(u_ref, 0, hidden), columns(u_ref, 1, hidden)],
        [columns(u_ref, 2, hidden)],
        [gains],
    )
    rates = (RATE_INNER, RATE_INNER, RATE_OUTER, RATE_INNER, RATE_INNER, RATE_GAIN)
    for group, (parts, rate) in enumerate(zip(grads, rates)):
        mine = held[3 * group : 3 * group + 3]
        master, moment, second = mine
        for load in loads[3 * group : 3 * group + 3]:
            load.wait()
        for i, g in enumerate(parts):
            at = i if len(master.shape) == 3 else Ellipsis
            new = adam_step(master[at], moment[at], second[at], g * factor, rate, DECAY if group < 5 else 0.0)
            for ref, value in zip(mine, new):
                ref[at] = value
            if group < 5:
                copies[group][at] = new[0].astype(BF)
        for ref, out in zip(mine + copies[group : group + 1], outputs[4 * group : 4 * group + 4]):
            put(ref, out)
    for load, ref, out in zip(loads[18:21], held[18:21], outputs[23:26]):
        load.wait()
        put(ref, out)
    put.end()


def call_update(stat, own, weights, passed):
    flat_weights = [w for group in weights for w in group]
    late = []
    for group in weights[0:5]:
        late += [sds(group[0].shape, F32)] * 3 + [sds(group[0].shape, BF)]
    late += [sds(weights[5][0].shape, F32)] * 3
    late += [sds(v.shape, BF) for v in passed]
    inputs = list(flat_weights) + list(passed)
    return pl.pallas_call(
        functools.partial(update_kernel, weights[0][0].shape[2], weights[3][0].shape[2]),
        out_shape=[sds((1, 1), F32)] + late,
        in_specs=[VM] * 6 + [ANY] * 21,
        out_specs=[VM] + [ANY] * 26,
        scratch_shapes=[pltpu.VMEM(v.shape, v.dtype) for v in inputs]
        + [pltpu.VMEM(group[0].shape, BF) for group in weights[0:5]]
        + [DMA((21,)), DMA((26,))],
        compiler_params=pltpu.CompilerParams(vmem_limit_bytes=VLIMIT),
        name="update",
    )(stat, *own, *inputs)


def local(
    n,
    residual,
    cotangent,
    memory,
    segment_ids,
    plot_ids,
    attend_weight,
    attend_first,
    attend_second,
    recall_weight,
    recall_first,
    recall_second,
    outward_weight,
    outward_first,
    outward_second,
    expand_weight,
    expand_first,
    expand_second,
    narrow_weight,
    narrow_first,
    narrow_second,
    gain_weight,
    gain_first,
    gain_second,
):
    _, plots, patches, width_d = memory.shape
    shard = attend_weight.shape[1]
    aligned = shard % 16 == 0
    length = segment_ids.shape[1]

    def by_rows(w):
        return jnp.transpose(w, (1, 0, 2)).reshape(w.shape[1], -1)

    if aligned:
        shards = (attend_weight, recall_weight, outward_weight, expand_weight, narrow_weight.T)
    else:
        out_rows = jnp.transpose(outward_weight, (2, 0, 1))
        shards = (
            jnp.concatenate([by_rows(attend_weight[0:3]), out_rows[:, 0]], axis=1),
            by_rows(recall_weight),
            jnp.concatenate([attend_weight[3], out_rows[:, 1]], axis=1),
            by_rows(expand_weight),
            narrow_weight.T,
        )
        shards = tuple(
            lax.all_gather(s.astype(BF), "dp", axis=0, tiled=True).reshape(8, width_d // 8, s.shape[1]) for s in shards
        )
    mem = memory.reshape(plots * patches, width_d)
    x0 = residual[0]
    plot_row = plot_ids.reshape(-1)
    outs = call_first(
        n, aligned, plot_row, x0, cotangent[0], gain_weight, segment_ids, shards, mem
    )
    lse, qct, c, ct, lse_c, qkv, qkvt, a, att, x1, ga, gr, gb, gc, wn, h0, h1, e3, kk, vv, kt, wo1, wa3 = outs
    dgain2, f, g2, e2, du, x2 = call_ffn(n, c, x1, gain_weight, wo1, gc, wn, e3)
    outs = call_cross_backward(n, aligned, plot_row, segment_ids, e2, gb, qct, kk, vv, kt, ct, lse_c, f, x2, wn, du)
    dqc, dk, dv, block_out = outs[0:4]
    own_u = outs[4] if aligned else du[0 : width_d // n].astype(F32)
    outs = call_self_backward(
        n, aligned, plots, x0, x1, g2, gain_weight, dgain2, segment_ids, dqc, dk, dv, own_u,
        e2, h1, h0, mem, ga, gr, c, a, qkv, qkvt, att, lse, wa3
    )
    residual_grad, memory_grad, stat = outs[0:3]
    if aligned:
        own = (own_u,) + tuple(outs[3:7])
    else:
        own = tuple(
            lax.psum_scatter(g.reshape(width_d, -1).astype(F32), "dp", scatter_dimension=0, tiled=True)
            for g in (du,) + tuple(outs[3:7])
        )
        squares = sum(jnp.sum(g * g) for g in own)
        stat = lax.psum(stat.at[width_d // 128, :].set(squares), ("dp", "tensor"))
    weights = (
        (attend_weight, attend_first, attend_second),
        (recall_weight, recall_first, recall_second),
        (outward_weight, outward_first, outward_second),
        (expand_weight, expand_first, expand_second),
        (narrow_weight.T, narrow_first.T, narrow_second.T),
        (gain_weight, gain_first, gain_second),
    )
    new = call_update(stat, own, weights, (block_out, residual_grad, memory_grad))
    narrow_new = tuple(v.T for v in new[17:21])
    return (
        (new[24][None], new[25][None], new[26][None], new[0].reshape(())) + tuple(new[1:17]) + narrow_new + tuple(new[21:24])
    )


def solution(mesh):
    rows_in = P("dp", "tensor", None)
    inner = P(None, "dp", "tensor")
    outer = P(None, "tensor", "dp")
    narrow = P("tensor", "dp")
    in_specs = (
        (rows_in, rows_in, P("dp", None, None, None), P("dp", None), P("dp", None))
        + (inner,) * 3
        + (inner,) * 3
        + (outer,) * 3
        + (inner,) * 3
        + (narrow,) * 3
        + (P(),) * 3
    )
    out_specs = (
        (rows_in, rows_in, P("dp", None, "tensor", None), P())
        + (inner,) * 4
        + (inner,) * 4
        + (outer,) * 4
        + (inner,) * 4
        + (narrow,) * 4
        + (P(),) * 3
    )
    return jax.shard_map(
        functools.partial(local, mesh.shape["dp"]),
        mesh=mesh,
        in_specs=in_specs,
        out_specs=out_specs,
        check_vma=False,
    )
```
